128 devices in a mesh: fsdp: 16 (over z_hi, x, core), ctx: 8 (over y, z_lo).
Axes of the slice: x: 4, y: 4, z: 4 (z_hi: 2, z_lo: 2; z = z_hi * 2 + z_lo), core: 2. Of those that a mesh axis runs over, the one named last changes fastest.
Arguments:
- tokens: bfloat16 [16384, 2048], P(('fsdp', 'ctx')), may hold values from -6 to 6
- cotangent: bfloat16 [16384, 2048], P(('fsdp', 'ctx')), may hold values from -6 to 6
- tree_lengths: int32 [16, 13], P('fsdp'), may hold values from 1 to 512, as said below
- gain_attn: bfloat16 [2048], P('fsdp'), may hold values from 0.5 to 1.5
- w_qkv: bfloat16 [2048, 2560], P('fsdp'), may hold values from -0.125 to 0.125
- w_out: bfloat16 [2048, 2048], P('fsdp'), may hold values from -1.5 to 1.5
- gain_mlp: bfloat16 [2048], P('fsdp'), may hold values from 0.5 to 1.5
- w_gate: bfloat16 [2048, 5632], P('fsdp'), may hold values from -0.125 to 0.125
- w_up: bfloat16 [2048, 5632], P('fsdp'), may hold values from -0.125 to 0.125
- w_down: bfloat16 [5632, 2048], P('fsdp'), may hold values from -0.078125 to 0.078125
Outputs:
- mixed: bfloat16 [16384, 2048], P(('fsdp', 'ctx'))
- grad_tokens: float32 [16384, 2048], P(('fsdp', 'ctx'))
- grad_gain_attn: float32 [2048], P('fsdp')
- grad_qkv: float32 [2048, 2560], P('fsdp')
- grad_out: float32 [2048, 2048], P('fsdp')
- grad_gain_mlp: float32 [2048], P('fsdp')
- grad_gate: float32 [2048, 5632], P('fsdp')
- grad_up: float32 [2048, 5632], P('fsdp')
- grad_down: float32 [5632, 2048], P('fsdp')
The draws below stay inside these ranges and needn't reach their ends.
Inputs may be any that keep to these rules, and one draw needn't show every extreme that they name: `tree_lengths`: row f gives the token counts of tree f's 13 segments in the order trunk, then for each of 4 branches the branch followed by its 2 leaves; every count is positive and each row sums to 1024. Every trunk holds 256 tokens or more, and some tree's trunk holds exactly 512.
All inputs are finite; a program needn't handle non-finite values.
Results may differ from the reference program's by a relative error of at most 0.023.
Values may be sent and summed in bfloat16 or wider, within the bound.
A program may use at most 320 MiB of HBM per device.

```python
from functools import partial
import jax
import jax.numpy as jnp
import numpy as np
from jax import lax

D = 2048
FF = 5632
H = 32
KVH = 4
HD = 64
QKV = 2560
TREE = 1024
TREES = 16
TOKENS = 16384


def draw_tree_lengths(key, part):
    key = jax.random.fold_in(key, 7)
    trunk_key, weight_key, chosen_key = jax.random.split(key, 3)
    trunk_len = TREE // 4 + jax.random.randint(trunk_key, (TREES, 1), 0, TREE // 4 + 1)
    chosen_tree = jax.random.randint(chosen_key, (), 0, TREES)
    rows_index = jnp.arange(TREES, dtype=jnp.int32)[:, None]
    trunk_len = jnp.where(rows_index == chosen_tree, TREE // 2, trunk_len).astype(jnp.int32)
    shares_raw = jax.random.randint(weight_key, (TREES, 12), 1, 9)
    remaining = TREE - trunk_len
    spare_tokens = remaining - 12
    shares = 1 + shares_raw * spare_tokens // jnp.sum(shares_raw, axis=1, keepdims=True)
    shortfall = remaining - jnp.sum(shares, axis=1, keepdims=True)
    shares = jnp.concatenate([shares[:, :11], shares[:, 11:] + shortfall], axis=1)
    return jnp.concatenate([trunk_len, shares], axis=1).astype(jnp.int32)


def level_of(own_key, dims, cuts, smallest, high):
    level = 1.0
    for axis_at, shards_of in cuts:
        heights = jax.random.uniform(jax.random.fold_in(jax.random.fold_in(own_key, 6), axis_at), (shards_of,), jnp.float32, smallest / len(cuts), high / len(cuts))
        level = level * jnp.repeat(jnp.exp(heights), dims[axis_at] // shards_of).reshape((-1,) + (1,) * (len(dims) - 1 - axis_at))
    return level


def noise(rng, dims, scale, reach, shards=(), kind=jnp.bfloat16):
    drawn = jax.random.normal(rng, dims, jnp.float32) * scale
    if len(shards) > 0:
        drawn = level_of(rng, dims, shards, -0.22, 0.18) * drawn
    return jnp.clip(drawn, min=-reach, max=reach).astype(kind)


def setup_inputs(seed: int = 0) -> dict:
    seeds = jax.random.split(jax.random.key(seed), 11)
    return {
        "tokens": noise(seeds[0], (TOKENS, D), 1.0, 6.0, ((0, 128),)),
        "cotangent": noise(seeds[1], (TOKENS, D), 1.0, 6.0, ((0, 128),)),
        "tree_lengths": draw_tree_lengths(jax.random.fold_in(seeds[10], 71), 0),
        "gain_attn": jnp.clip(1.0 + 0.1 * jax.random.normal(seeds[3], (D,), jnp.float32), 0.5, 1.5).astype(jnp.bfloat16),
        "w_qkv": noise(seeds[4], (D, QKV), D ** -0.5, 0.125, ((0, 16),)),
        "w_out": noise(seeds[5], (H * HD, D), (max(16, D // 128)) ** -0.5, 1.5, ((0, 16),)),
        "gain_mlp": jnp.clip(1.0 + 0.1 * jax.random.normal(seeds[6], (D,), jnp.float32), 0.5, 1.5).astype(jnp.bfloat16),
        "w_gate": noise(seeds[7], (D, FF), D ** -0.5, 0.125, ((0, 16),)),
        "w_up": noise(seeds[8], (D, FF), D ** -0.5, 0.125, ((0, 16),)),
        "w_down": noise(seeds[9], (FF, D), FF ** -0.5, 0.078125, ((0, 16),)),
    }


epsilon = 1e-05
rope_base = 10000.0
masked_score = -1e+30
segment_total = 13
highest = lax.Precision.HIGHEST

@jax.custom_vjp
def low(v):
    return lax.optimization_barrier(v.astype(jnp.bfloat16)).astype(jnp.float32)

@jax.custom_vjp
def low_back(v):
    return v

def low_keep(v):
    return (low(v), None)

def low_pass(kept, grad):
    return (grad,)

def back_keep(v):
    return (v, None)

def back_low(kept, grad):
    return (low(grad),)
low.defvjp(low_keep, low_pass)
low_back.defvjp(back_keep, back_low)

def ancestry_table():
    ancestors = np.eye(segment_total, dtype=np.float32)
    ancestors[:, 0] = 1.0
    for branch in range(4):
        parent = 1 + 3 * branch
        ancestors[parent + 1, parent] = 1.0
        ancestors[parent + 2, parent] = 1.0
    return ancestors

def tree_layout(lengths, offsets):
    lengths = lengths.astype(jnp.int32)
    segment_ends = jnp.cumsum(lengths).astype(jnp.int32)
    starts = segment_ends - lengths
    strict = jnp.asarray(ancestry_table() - np.eye(segment_total, dtype=np.float32)).astype(jnp.int32)
    depth_start = lax.optimization_barrier(jnp.sum(strict * lengths[None, :], axis=1)).astype(jnp.int32)
    segment = lax.optimization_barrier(jnp.sum((offsets[:, None] >= segment_ends[None, :]).astype(jnp.int32), axis=1))
    onehot = segment[:, None] == jnp.arange(segment_total, dtype=jnp.int32)[None, :]
    begin_at = lax.optimization_barrier(jnp.sum(jnp.where(onehot, starts[None, :], 0), axis=1)).astype(jnp.int32)
    depth_of = lax.optimization_barrier(jnp.sum(jnp.where(onehot, depth_start[None, :], 0), axis=1)).astype(jnp.int32)
    return (onehot.astype(jnp.float32), (offsets - begin_at + depth_of).astype(jnp.int32))

def path_mask(onehot_rows, position_rows, onehot_keys, position_keys):
    reachable = jnp.dot(onehot_rows, jnp.asarray(ancestry_table()), precision=highest)
    shared = jnp.dot(reachable, onehot_keys.T, precision=highest)
    return (shared > 0.5) & (position_keys[None, :] <= position_rows[:, None])

def rotate_pairs(values, position, direction):
    half_dim = values.shape[-1] // 2
    frequency = rope_base ** (-2.0 * jnp.arange(half_dim, dtype=jnp.float32) / values.shape[-1])
    angles = position.astype(jnp.float32)[:, None] * frequency[None, :]
    cosine = jnp.cos(angles)[:, None, :]
    sine_part = direction * jnp.sin(angles)[:, None, :]
    former = values[..., :half_dim]
    latter = values[..., half_dim:]
    return jnp.concatenate([former * cosine - latter * sine_part, latter * cosine + former * sine_part], axis=-1)

def tree_attention(pieces):
    queries, key_rows, value_rows, onehot, position = pieces
    allowed = path_mask(onehot, position, onehot, position)
    length_rows = queries.shape[0]
    grouped_heads = queries.reshape(length_rows, KVH, H // KVH, HD)
    scores = low_back(jnp.einsum('qkgd,tkd->kgqt', grouped_heads, key_rows, precision=highest) * HD ** (-0.5))
    scores = jnp.where(allowed[None, None], scores, masked_score)
    attention_weights = low(jax.nn.softmax(scores, axis=-1))
    combined = jnp.einsum('kgqt,tkd->qkgd', attention_weights, value_rows, precision=highest)
    return combined.reshape(length_rows, H * HD)

def layer_forward(inputs, gain_one, qkv_weight, out_weight, gain_two, gate_weight, up_weight, down_weight, onehot=None, position=None):
    query_width = H * HD
    kv_width = KVH * HD
    normed = low(inputs * lax.rsqrt(lax.optimization_barrier(jnp.mean(inputs * inputs, axis=-1, keepdims=True)) + epsilon) * gain_one)
    projected = low_back(jnp.dot(normed, qkv_weight, precision=highest))
    queries = low(rotate_pairs(projected[:, :query_width].reshape(-1, H, HD), position, 1.0))
    key_rows = low(rotate_pairs(projected[:, query_width:query_width + kv_width].reshape(-1, KVH, HD), position, 1.0))
    value_rows = low(projected[:, query_width + kv_width:].reshape(-1, KVH, HD))
    stacked = (queries.reshape(TREES, TREE, H, HD), key_rows.reshape(TREES, TREE, KVH, HD), value_rows.reshape(TREES, TREE, KVH, HD), onehot.reshape(TREES, TREE, segment_total), position.reshape(TREES, TREE))
    attended = lax.map(jax.checkpoint(tree_attention), stacked).reshape(-1, query_width)
    attended = low(low_back(attended))
    hidden = inputs + low_back(jnp.dot(attended, out_weight, precision=highest))
    normed_two = low(hidden * lax.rsqrt(lax.optimization_barrier(jnp.mean(hidden * hidden, axis=-1, keepdims=True)) + epsilon) * gain_two)
    gate_value = low_back(jnp.dot(normed_two, gate_weight, precision=highest))
    up_value = low_back(jnp.dot(normed_two, up_weight, precision=highest))
    inner_act = low(jax.nn.silu(gate_value) * up_value)
    return hidden + low_back(jnp.dot(inner_act, down_weight, precision=highest))

def reference(tokens, cotangent, tree_lengths, gain_attn, w_qkv, w_out, gain_mlp, w_gate, w_up, w_down):
    offsets = jnp.arange(TREE, dtype=jnp.int32)
    onehot, position = jax.vmap(lambda lengths: tree_layout(lengths, offsets))(tree_lengths)
    onehot = onehot.reshape(TOKENS, segment_total)
    position = position.reshape(TOKENS).astype(jnp.int32)
    forward = partial(layer_forward, onehot=onehot, position=position)
    output, pullback = jax.vjp(forward, tokens.astype(jnp.float32), gain_attn.astype(jnp.float32), w_qkv.astype(jnp.float32), w_out.astype(jnp.float32), gain_mlp.astype(jnp.float32), w_gate.astype(jnp.float32), w_up.astype(jnp.float32), w_down.astype(jnp.float32))
    grads = pullback(cotangent.astype(jnp.float32))
    return (output.astype(jnp.bfloat16), grads[0], grads[1], grads[2], grads[3], grads[4], grads[5], grads[6], grads[7])
```

```python
import functools

import jax
import jax.numpy as jnp
import numpy as np
from jax import lax
from jax.experimental import pallas as pl
from jax.experimental.pallas import tpu as pltpu
from jax.sharding import PartitionSpec as P

D = 2048
FF = 5632
H = 32
KVH = 4
HD = 64
FJ = FF // 8
bf16 = jnp.bfloat16
f32 = jnp.float32
MESH = pl.DeviceIdType.MESH
epsilon = 1e-05
masked_score = -1e30
ANY = pl.BlockSpec(memory_space=pl.ANY)
VM = pl.BlockSpec(memory_space=pltpu.VMEM)


class Place:
    def __init__(self):
        fs = lax.axis_index("fsdp")
        ct = lax.axis_index("ctx")
        self.zh, self.x, self.k = fs // 8, (fs // 2) % 4, fs % 2
        self.y, self.zl = ct // 2, ct % 2
        self.z = 2 * self.zh + self.zl

    def device(self, z=None, x=None, k=None, y=None):
        z = self.z if z is None else z
        x = self.x if x is None else x
        k = self.k if k is None else k
        y = self.y if y is None else y
        return ((z // 2) * 8 + x * 2 + k, y * 2 + z % 2)

    def sibling(self):
        return self.device(k=1 - self.k)

    def along(self, axis, r):
        at = (getattr(self, axis) + r + 4) % 4
        return self.device(**{axis: at})

    def piece(self, z=None, x=None):
        z = self.z if z is None else z
        x = self.x if x is None else x
        return (z // 2) * 8 + x * 2 + z % 2

    def moved(self, axis, r):
        return (getattr(self, axis) + r + 4) % 4


def rcopy(src, dst, ssem, rsem, dev):
    return pltpu.make_async_remote_copy(
        src_ref=src, dst_ref=dst, send_sem=ssem, recv_sem=rsem, device_id=dev, device_id_type=MESH
    )


def greet(devices):
    bar = pltpu.get_barrier_semaphore()
    for dev in devices:
        pl.semaphore_signal(bar, inc=1, device_id=dev, device_id_type=MESH)


def await_greetings(count):
    pl.semaphore_wait(pltpu.get_barrier_semaphore(), count)


class RingGather:
    def __init__(self, at, buf, ssem, rsem):
        self.at, self.buf, self.ssem, self.rsem = at, buf, ssem, rsem

    def slot(self, r, k=None):
        k = self.at.k if k is None else k
        return self.buf.at[k * 4 + self.at.moved("y", r)]

    def out(self, r):
        return rcopy(self.slot(0), self.slot(0), self.ssem.at[r], self.rsem.at[r], self.at.along("y", r))

    def arrival(self, r):
        return rcopy(self.slot(-r), self.slot(-r), self.ssem.at[r], self.rsem.at[r], self.at.along("y", r))

    def relay(self, r):
        return rcopy(
            self.slot(-r), self.slot(-r), self.ssem.at[4 + r], self.rsem.at[4 + r], self.at.sibling()
        )

    def relayed(self, r):
        other = self.slot(-r, 1 - self.at.k)
        return rcopy(other, other, self.ssem.at[4 + r], self.rsem.at[4 + r], self.at.sibling())

    def start(self):
        for r in (2, 1, 3):
            self.out(r).start()
        self.relay(0).start()

    def pass_on(self, r):
        self.arrival(r).wait_recv()
        self.relay(r).start()

    def finish(self):
        for r in range(4):
            self.relayed(r).wait_recv()
            self.relay(r).wait_send()
        for r in (1, 2, 3):
            self.out(r).wait_send()


class PlaneGather:
    def __init__(self, at, view, first, second, ssem, rsem):
        self.at, self.view, self.first, self.second = at, view, first, second
        self.ssem, self.rsem = ssem, rsem

    def slot(self, a, b):
        return self.view(
            self.at.piece(**{self.first: self.at.moved(self.first, a), self.second: self.at.moved(self.second, b)})
        )

    def out1(self, r):
        return rcopy(self.slot(0, 0), self.slot(0, 0), self.ssem.at[r], self.rsem.at[r], self.at.along(self.first, r))

    def in1(self, r):
        return rcopy(self.slot(-r, 0), self.slot(-r, 0), self.ssem.at[r], self.rsem.at[r], self.at.along(self.first, r))

    def out2(self, c, s):
        i = 4 + c * 4 + s
        return rcopy(self.slot(-c, 0), self.slot(-c, 0), self.ssem.at[i], self.rsem.at[i], self.at.along(self.second, s))

    def in2(self, c, s):
        i = 4 + c * 4 + s
        return rcopy(self.slot(-c, -s), self.slot(-c, -s), self.ssem.at[i], self.rsem.at[i], self.at.along(self.second, s))

    def start(self):
        for r in (2, 1, 3):
            self.out1(r).start()
        for s in (2, 1, 3):
            self.out2(0, s).start()

    def step(self, r):
        self.in1(r).wait_recv()
        for s in (2, 1, 3):
            self.out2(r, s).start()

    def finish(self):
        for r in (1, 2, 3):
            self.out1(r).wait_send()
        for c in range(4):
            for s in (1, 2, 3):
                self.in2(c, s).wait_recv()
                self.out2(c, s).wait_send()


def weights_kernel(
    hat, cot, wq, wg, wu, wo, wd, hat_all, cot_all, gq, gg, gu, go, gd, ysem_s, ysem_r, psem_s, psem_r, lsem, csem_s, csem_r,
    rsem_s, rsem_r,
):
    at = Place()
    own8 = at.zh * 4 + at.x
    is_src = own8 // 2 == at.y
    kd = at.x % 2
    both = jnp.where(is_src & (kd == at.k), 1, 0)
    src_n = jnp.where(is_src, 1, 0)
    j = 2 * at.y + at.k
    jz, jx = (j // 4) * 2 + at.zl, j % 4

    partners = [at.sibling()] + [at.along(a, r) for a in ("x", "z", "y") for r in (1, 2, 3)]
    greet(partners)
    for s in range(2):
        mine = (jz == at.z) & (jx == at.x) & (at.k == s)

        @pl.when(jnp.logical_not(mine))
        def _():
            greet([at.device(z=jz, x=jx, k=s)])

    def row_dest(t):
        q = (own8 + t) % 8
        z = (q // 4) * 2 + at.zl
        return at.device(z=z, x=q % 4, k=kd), at.piece(z=z, x=q % 4)

    @pl.when(is_src)
    def _():
        for t in range(8):
            dev, _ = row_dest(t)
            if t == 0:

                @pl.when(kd != at.k)
                def _():
                    greet([dev])
            else:
                greet([dev])

    await_greetings(10 + (2 - both) + src_n * 8 - both * src_n)

    ring_h = RingGather(at, hat_all, ysem_s.at[0], ysem_r.at[0])
    ring_c = RingGather(at, cot_all, ysem_s.at[1], ysem_r.at[1])
    own = at.k * 4 + at.y
    piece = at.piece()
    h_in = pltpu.make_async_copy(hat, hat_all.at[own], lsem.at[0])
    c_in = pltpu.make_async_copy(cot, cot_all.at[own], lsem.at[1])
    h_in.start()
    c_in.start()
    cols = ((wq, gq), (wg, gg), (wu, gu))
    rows = ((wo, go, 128), (wd, gd, 352))

    def col_send(i):
        src, dst = cols[i]
        return rcopy(src.at[1 - at.k], dst.at[piece], csem_s.at[i], csem_r.at[i], at.sibling())

    def col_keep(i):
        src, dst = cols[i]
        return pltpu.make_async_copy(src.at[at.k], dst.at[piece], csem_r.at[i])

    def row_send(i, t):
        src, dst, n = rows[i]
        dev, p = row_dest(t)
        lanes = pl.ds(pl.multiple_of(p * 128, 128), 128)
        return rcopy(
            src.at[:, lanes],
            dst.at[pl.ds(pl.multiple_of(at.k * n, 16), n), lanes],
            rsem_s.at[i, t],
            rsem_r.at[i, at.k],
            dev,
        )

    def row_keep(i):
        src, dst, n = rows[i]
        lanes = pl.ds(pl.multiple_of(piece * 128, 128), 128)
        return pltpu.make_async_copy(
            src.at[:, lanes], dst.at[pl.ds(pl.multiple_of(at.k * n, 16), n), lanes], rsem_r.at[i, at.k]
        )

    def row_in(i, s):
        src, dst, n = rows[i]
        lanes = pl.ds(pl.multiple_of(piece * 128, 128), 128)
        there = dst.at[pl.ds(s * n, n), lanes]
        return rcopy(there, there, rsem_s.at[i, s], rsem_r.at[i, s], at.device(z=jz, x=jx, k=s))

    @pl.when(at.k == at.zl)
    def _():
        for i in range(3):
            col_send(i).start()
            col_keep(i).start()

    @pl.when(is_src)
    def _():
        for i in range(2):
            for t in range(1, 8):
                row_send(i, t).start()

            @pl.when(kd == at.k)
            def _():
                row_keep(i).start()

            @pl.when(kd != at.k)
            def _():
                row_send(i, 0).start()

    h_in.wait()
    ring_h.start()
    orders = (("x", "z"), ("x", "z"), ("z", "x"), ("z", "x"), ("z", "x"))

    def col_view(ref):
        return lambda p: ref.at[p]

    def row_view(ref):
        return lambda p: ref.at[:, pl.ds(pl.multiple_of(p * 128, 128), 128)]

    views = [col_view(gq), col_view(gg), col_view(gu), row_view(go), row_view(gd)]
    planes = [
        PlaneGather(at, views[i], *orders[i], psem_s.at[i], psem_r.at[i]) for i in range(5)
    ]

    def ready(i):
        if i < 3:
            col_keep(i).wait()
        else:
            for s in range(2):
                row_in(i - 3, s).wait_recv()

    c_in.wait()
    order = (0, 3, 1, 2, 4)
    ready(0)
    planes[0].start()
    ready(3)
    planes[3].start()
    for r in (1, 3, 2):
        ring_h.pass_on(r)
    ring_c.start()
    for i in (1, 2, 4):
        ready(i)
        planes[i].start()
    for i in order:
        for r in (1, 3, 2):
            planes[i].step(r)
    for r in (1, 3, 2):
        ring_c.pass_on(r)
    ring_h.finish()
    ring_c.finish()
    for i in order:
        planes[i].finish()

    @pl.when(at.k == at.zl)
    def _():
        for i in range(3):
            col_send(i).wait_send()

    @pl.when(is_src)
    def _():
        for i in range(2):
            for t in range(1, 8):
                row_send(i, t).wait_send()

            @pl.when(kd != at.k)
            def _():
                row_send(i, 0).wait_send()


def gather_weights(hat, cot, wq, wg, wu, wo, wd):
    shape = jax.ShapeDtypeStruct
    dma = pltpu.SemaphoreType.DMA
    return pl.pallas_call(
        weights_kernel,
        name="gather_weights",
        out_shape=(
            shape((8, 128, D), bf16),
            shape((8, 128, D), bf16),
            shape((16, 128, 384), bf16),
            shape((16, 128, FJ), bf16),
            shape((16, 128, FJ), bf16),
            shape((256, D), bf16),
            shape((FJ, D), bf16),
        ),
        in_specs=[ANY] * 7,
        out_specs=[ANY] * 7,
        scratch_shapes=[
            dma((2, 8)), dma((2, 8)), dma((5, 20)), dma((5, 20)), dma((2,)), dma((3,)), dma((3,)), dma((2, 8)), dma((2, 2)),
        ],
        compiler_params=pltpu.CompilerParams(collective_id=0, has_side_effects=True),
    )(hat, cot, wq, wg, wu, wo, wd)


def ring_gather_kernel(src, out, ssem, rsem, lsem):
    at = Place()
    greet([at.sibling()] + [at.along("y", r) for r in (1, 2, 3)])
    cp = pltpu.make_async_copy(src, out.at[at.k * 4 + at.y], lsem)
    cp.start()
    await_greetings(4)
    cp.wait()
    ring = RingGather(at, out, ssem, rsem)
    ring.start()
    for r in (1, 3, 2):
        ring.pass_on(r)
    ring.finish()


def ring_gather(src):
    dma = pltpu.SemaphoreType.DMA
    return pl.pallas_call(
        ring_gather_kernel,
        name="ring_gather",
        out_shape=jax.ShapeDtypeStruct((8, 128, D), bf16),
        in_specs=[VM],
        out_specs=VM,
        scratch_shapes=[dma((8,)), dma((8,)), dma],
        compiler_params=pltpu.CompilerParams(
            collective_id=1, has_side_effects=True, vmem_limit_bytes=32 * 2**20
        ),
    )(src).reshape(1024, D)


class RingReduce:
    def __init__(self, at, part, sib, ring, send, ssem, rsem):
        self.at, self.part, self.sib, self.ring, self.send = at, part, sib, ring, send
        self.ssem, self.rsem = ssem, rsem

    def cross(self, r):
        y = self.at.moved("y", r)
        return rcopy(
            self.part.at[(1 - self.at.k) * 4 + y], self.sib.at[r], self.ssem.at[r], self.rsem.at[r], self.at.sibling()
        )

    def out(self, r):
        return rcopy(
            self.send.at[r], self.ring.at[r], self.ssem.at[4 + r], self.rsem.at[4 + r], self.at.along("y", r)
        )

    def mine(self, r, rows):
        y = self.at.moved("y", r)
        return self.part[self.at.k * 4 + y, rows, :].astype(f32) + self.sib[r, rows, :].astype(f32)

    def cross_all(self):
        for r in (2, 1, 3, 0):
            self.cross(r).start()

    def forward(self):
        for r in (2, 1, 3):
            self.cross(r).wait_recv()

            @pl.loop(0, 8)
            def _(i):
                rows = pl.ds(pl.multiple_of(i * 16, 16), 16)
                self.send[r, rows, :] = self.mine(r, rows).astype(bf16)

            self.out(r).start()

    def collect(self, emit):
        self.cross(0).wait_recv()
        for r in (1, 3, 2):
            self.out(r).wait_recv()

        @pl.loop(0, 8)
        def _(i):
            rows = pl.ds(pl.multiple_of(i * 16, 16), 16)
            total = self.mine(0, rows)
            for r in (1, 2, 3):
                total += self.ring[r, rows, :].astype(f32)
            emit(rows, total)

        for r in range(4):
            self.cross(r).wait_send()
        for r in (1, 2, 3):
            self.out(r).wait_send()


def ring_reduce_kernel(part, out, sib, ring, send, ssem, rsem):
    at = Place()
    greet([at.sibling()] + [at.along("y", r) for r in (1, 2, 3)])
    await_greetings(4)
    red = RingReduce(at, part, sib, ring, send, ssem, rsem)
    red.cross_all()
    red.forward()

    def emit(rows, total):
        out[rows, :] = total

    red.collect(emit)


def ring_reduce(part):
    dma = pltpu.SemaphoreType.DMA
    buf = pltpu.VMEM((4, 128, D), bf16)
    return pl.pallas_call(
        ring_reduce_kernel,
        name="ring_reduce",
        out_shape=jax.ShapeDtypeStruct((128, D), f32),
        in_specs=[VM],
        out_specs=VM,
        scratch_shapes=[buf, buf, buf, dma((8,)), dma((8,))],
        compiler_params=pltpu.CompilerParams(
            collective_id=2, has_side_effects=True, vmem_limit_bytes=32 * 2**20
        ),
    )(part.reshape(8, 128, D))


class PlaneReduce:
    def __init__(self, at, part, buf1, send, buf2, first, second, ssem, rsem):
        self.at, self.part, self.buf1, self.send, self.buf2 = at, part, buf1, send, buf2
        self.first, self.second, self.ssem, self.rsem = first, second, ssem, rsem

    def piece(self, a, b):
        return self.at.piece(**{self.first: self.at.moved(self.first, a), self.second: self.at.moved(self.second, b)})

    def out1(self, s, c):
        i = s * 4 + c
        return rcopy(
            self.part.at[self.piece(s, c)], self.buf1.at[s - 1, c], self.ssem.at[i], self.rsem.at[i], self.at.along(self.first, s)
        )

    def out2(self, c):
        return rcopy(self.send.at[c], self.buf2.at[c - 1], self.ssem.at[c], self.rsem.at[c], self.at.along(self.second, c))

    def start(self):
        for c in (2, 1, 3, 0):
            for s in (2, 1, 3):
                self.out1(s, c).start()

    def rows_loop(self, body):
        n = self.part.shape[1]

        @pl.loop(0, n // 32)
        def _(i):
            body(pl.ds(pl.multiple_of(i * 32, 32), 32))

    def forward(self, c):
        for s in (1, 2, 3):
            self.out1(s, c).wait_recv()
        p = self.piece(0, c)

        def body(rows):
            t = self.part[p, rows, :].astype(f32)
            for s in range(3):
                t += self.buf1[s, c, rows, :].astype(f32)
            self.send[c, rows, :] = t.astype(bf16)

        self.rows_loop(body)
        if c:
            self.out2(c).start()

    def collect(self):
        for c in (1, 2, 3):
            self.out2(c).wait_recv()

        def body(rows):
            t = self.send[0, rows, :].astype(f32)
            for c in range(3):
                t += self.buf2[c, rows, :].astype(f32)
            self.send[0, rows, :] = t.astype(bf16)

        self.rows_loop(body)

    def finish(self):
        for c in range(4):
            for s in (1, 2, 3):
                self.out1(s, c).wait_send()
        for c in (1, 2, 3):
            self.out2(c).wait_send()


def plane_reduce_kernel(first, second, part, out, buf1, send, buf2, ssem, rsem, lsem):
    at = Place()
    greet([at.along(a, r) for a in ("x", "z") for r in (1, 2, 3)])
    await_greetings(6)
    red = PlaneReduce(at, part, buf1, send, buf2, first, second, ssem, rsem)
    red.start()
    for c in (2, 1, 3, 0):
        red.forward(c)
    red.collect()
    cp = pltpu.make_async_copy(send.at[0], out, lsem)
    cp.start()
    cp.wait()
    red.finish()


def plane_reduce(part, first, second, cid):
    dma = pltpu.SemaphoreType.DMA
    n, r, c = part.shape
    return pl.pallas_call(
        functools.partial(plane_reduce_kernel, first, second),
        name="plane_reduce",
        out_shape=jax.ShapeDtypeStruct((r, c), bf16),
        in_specs=[VM],
        out_specs=ANY,
        scratch_shapes=[
            pltpu.VMEM((3, 4, r, c), bf16), pltpu.VMEM((4, r, c), bf16), pltpu.VMEM((3, r, c), bf16),
            dma((16,)), dma((16,)), dma,
        ],
        compiler_params=pltpu.CompilerParams(
            collective_id=cid, has_side_effects=True, vmem_limit_bytes=56 * 2**20
        ),
    )(part)


def spread_kernel(gq, gg, gu, go, gd, oq, og, ou, oo, od, csem_s, csem_r, rsem_s, rsem_r):
    at = Place()
    cols = ((gq, oq), (gg, og), (gu, ou))
    rows = ((go, oo, 128), (gd, od, 352))
    j = 2 * at.y + at.k
    jzh, jx = j // 4, j % 4
    piece = at.piece()
    keep_col = at.k == at.zl

    def col_dev(dy, dz):
        zl = (at.zl + dz) % 2
        return at.device(z=2 * at.zh + zl, y=at.moved("y", dy), k=at.zl)

    def col_copy(i, dy, dz):
        n = (dy * 2 + dz) * 3 + i
        src, dst = cols[i]
        return rcopy(src, dst.at[j], csem_s.at[n], csem_r.at[i, j], col_dev(dy, dz))

    def row_dev(dy, dz, cc):
        zl = (at.zl + dz) % 2
        return at.device(z=2 * jzh + zl, x=jx, y=at.moved("y", dy), k=cc)

    self_row = (jzh == at.zh) & (jx == at.x)

    def row_copy(i, dy, dz, cc):
        n = ((dy * 2 + dz) * 2 + cc) * 2 + i
        src, dst, m = rows[i]
        lanes = pl.ds(pl.multiple_of(piece * 128, 128), 128)
        return rcopy(
            src.at[pl.ds(cc * m, m)], dst.at[:, lanes], rsem_s.at[n], rsem_r.at[i, piece], row_dev(dy, dz, cc)
        )

    def row_local(i, cc):
        src, dst, m = rows[i]
        lanes = pl.ds(pl.multiple_of(piece * 128, 128), 128)
        return pltpu.make_async_copy(src.at[pl.ds(cc * m, m)], dst.at[:, lanes], rsem_r.at[i, piece])

    def each_col(f, g):
        for dy in (2, 1, 3, 0):
            for dz in (1, 0):
                if dy == 0 and dz == 0:
                    pl.when(keep_col)(g)
                    pl.when(jnp.logical_not(keep_col))(functools.partial(f, dy, dz))
                else:
                    f(dy, dz)

    def each_row(f, g):
        for dy in (2, 1, 3, 0):
            for dz in (1, 0):
                for cc in range(2):
                    if dy == 0 and dz == 0:
                        mine = self_row & (at.k == cc)
                        pl.when(mine)(functools.partial(g, cc))
                        pl.when(jnp.logical_not(mine))(functools.partial(f, dy, dz, cc))
                    else:
                        f(dy, dz, cc)

    src_y = (at.zh * 4 + at.x) // 2
    src_k = at.x % 2

    def nothing(*_):
        pass

    each_col(lambda dy, dz: greet([col_dev(dy, dz)]), nothing)
    each_row(lambda dy, dz, cc: greet([row_dev(dy, dz, cc)]), nothing)
    col_count = jnp.where(keep_col, 7, 8)
    for y in range(4):
        for k in range(2):
            mine = (at.y == y) & (at.k == k) & (at.zl == at.k)

            @pl.when(jnp.logical_not(mine))
            def _():
                greet([at.device(z=2 * at.zh + at.k, y=y, k=k)])

    for p in range(16):
        z, x = (p // 8) * 2 + p % 2, (p // 2) % 4
        mine = (at.z == z) & (at.x == x) & (at.y == src_y) & (at.k == src_k)

        @pl.when(jnp.logical_not(mine))
        def _():
            greet([at.device(z=z, x=x, y=src_y, k=src_k)])

    own_row = jnp.where(self_row, 1, 0)
    await_greetings(2 * col_count + 2 * (16 - own_row))

    def col_start(dy, dz):
        for i in range(3):
            col_copy(i, dy, dz).start()

    def col_local():
        for i in range(3):
            src, dst = cols[i]
            pltpu.make_async_copy(src, dst.at[j], csem_r.at[i, j]).start()

    def row_start(dy, dz, cc):
        for i in range(2):
            row_copy(i, dy, dz, cc).start()

    def row_local_start(cc):
        for i in range(2):
            row_local(i, cc).start()

    each_row(row_start, row_local_start)
    each_col(col_start, col_local)
    for i in range(3):
        src, dst = cols[i]
        for q in range(8):
            pltpu.make_async_copy(src, dst.at[q], csem_r.at[i, q]).wait()
    for i in range(2):
        src, dst, m = rows[i]
        for p in range(16):
            pltpu.make_async_copy(
                src.at[pl.ds(0, m)], dst.at[:, pl.ds(p * 128, 128)], rsem_r.at[i, p]
            ).wait()

    def col_done(dy, dz):
        for i in range(3):
            col_copy(i, dy, dz).wait_send()

    def row_done(dy, dz, cc):
        for i in range(2):
            row_copy(i, dy, dz, cc).wait_send()

    each_row(row_done, nothing)
    each_col(col_done, nothing)


def spread(gq, gg, gu, go, gd):
    dma = pltpu.SemaphoreType.DMA
    shape = jax.ShapeDtypeStruct
    return pl.pallas_call(
        spread_kernel,
        name="spread",
        out_shape=(
            shape((8, 128, 384), bf16),
            shape((8, 128, FJ), bf16),
            shape((8, 128, FJ), bf16),
            shape((128, D), bf16),
            shape((352, D), bf16),
        ),
        in_specs=[ANY] * 5,
        out_specs=[ANY] * 5,
        scratch_shapes=[dma((24,)), dma((3, 8)), dma((32,)), dma((2, 16))],
        compiler_params=pltpu.CompilerParams(collective_id=9, has_side_effects=True),
    )(gq, gg, gu, go, gd)


def low_half(shape):
    return lax.broadcasted_iota(jnp.int32, shape, len(shape) - 1) % 128 < 64


def dot_nt(a, b):
    return lax.dot_general(a, b, (((1,), (1,)), ((), ())), preferred_element_type=f32)


def dot_nn(a, b):
    return lax.dot_general(a, b, (((1,), (0,)), ((), ())), preferred_element_type=f32)


def dot_tn(a, b):
    return lax.dot_general(a, b, (((0,), (0,)), ((), ())), preferred_element_type=f32)


def spread_heads(q):
    low = low_half((128, 128))
    zero = jnp.zeros((128, 128), q.dtype)
    parts = []
    for pair in range(2):
        both = q[:, pair * 128 : pair * 128 + 128]
        parts += [jnp.where(low, both, zero), jnp.where(low, zero, both)]
    return jnp.concatenate(parts, axis=0)


def join_heads(o):
    low = low_half((128, 128))
    return jnp.concatenate(
        [jnp.where(low, o[256 * p : 256 * p + 128], o[256 * p + 128 : 256 * p + 256]) for p in range(2)], axis=1
    )


def doubled(kv):
    other = pltpu.roll(kv.astype(f32), 64, 1).astype(bf16)
    low = low_half(kv.shape)
    return jnp.where(low, kv, other), jnp.where(low, other, kv)


def allowed_rows(bounds, n):
    col = lax.broadcasted_iota(jnp.int32, (128, n), 1)
    own, trunk, start, b0, b1 = [bounds[:, i : i + 1] for i in range(5)]
    past = col <= own
    return past & ((col < trunk) | (col >= start) | ((col >= b0) & (col < b1)))


def attend_fwd_kernel(q_ref, kv_ref, bounds_ref, out_ref, lse_ref):
    for y in range(4):

        @pl.when(pl.program_id(1) == y)
        def _():
            n = 256 * (y + 1)
            kd, vd = doubled(kv_ref[0, :n, :])
            qs = spread_heads(q_ref[...])
            bias = jnp.where(allowed_rows(bounds_ref[...], n), 0.0, masked_score)
            s = dot_nt(qs, kd) * (HD**-0.5) + jnp.concatenate([bias] * 4, axis=0)
            peak = jnp.max(s, axis=1, keepdims=True)
            e = jnp.exp(s - peak)
            total = jnp.sum(e, axis=1, keepdims=True)
            o = dot_nn(e.astype(bf16), vd) / total
            out_ref[...] = join_heads(o).astype(bf16)
            lse_ref[...] = jnp.broadcast_to(peak + jnp.log(total), (512, 128))


def attend_fwd(q, kv, bounds):
    return pl.pallas_call(
        attend_fwd_kernel,
        name="attend_fwd",
        grid=(2, 4),
        out_shape=(jax.ShapeDtypeStruct((1024, 256), bf16), jax.ShapeDtypeStruct((4096, 128), f32)),
        in_specs=[
            pl.BlockSpec((128, 256), lambda t, y: (t * 4 + y, 0)),
            pl.BlockSpec((1, 1024, 128), lambda t, y: (t, 0, 0)),
            pl.BlockSpec((128, 128), lambda t, y: (t * 4 + y, 0)),
        ],
        out_specs=(
            pl.BlockSpec((128, 256), lambda t, y: (t * 4 + y, 0)),
            pl.BlockSpec((512, 128), lambda t, y: (t * 4 + y, 0)),
        ),
        compiler_params=pltpu.CompilerParams(vmem_limit_bytes=48 * 2**20),
    )(q, kv, bounds)


def attend_bwd_kernel(q_ref, do_ref, kv_ref, bounds_ref, lse_ref, dq_ref, dkv_ref):
    low = low_half((1024, 128))

    @pl.when(pl.program_id(1) == 0)
    def _():
        dkv_ref[...] = jnp.zeros_like(dkv_ref)

    for y in range(4):

        @pl.when(pl.program_id(1) == y)
        def _():
            n = 256 * (y + 1)
            kd, vd = doubled(kv_ref[0, :n, :])
            qs = spread_heads(q_ref[...])
            dos = spread_heads(do_ref[...])
            bias = jnp.where(allowed_rows(bounds_ref[...], n), 0.0, masked_score)
            s = dot_nt(qs, kd) * (HD**-0.5) + jnp.concatenate([bias] * 4, axis=0)
            prob = jnp.exp(s - lse_ref[:, :1])
            dprob = dot_nt(dos, vd)
            inner = jnp.sum(prob * dprob, axis=1, keepdims=True)
            ds = (prob * (dprob - inner)).astype(bf16)
            dq_ref[...] = join_heads(dot_nn(ds, kd)) * (HD**-0.5)
            dk = dot_tn(ds, qs)
            dv = dot_tn(prob.astype(bf16), dos)
            dk = (dk + pltpu.roll(dk, 64, 1)) * (HD**-0.5)
            dv = dv + pltpu.roll(dv, 64, 1)
            dkv_ref[0, :n, :] += jnp.where(low[:n], dk, dv)


def attend_bwd(q, do, kv, bounds, lse):
    return pl.pallas_call(
        attend_bwd_kernel,
        name="attend_bwd",
        grid=(2, 4),
        out_shape=(jax.ShapeDtypeStruct((1024, 256), f32), jax.ShapeDtypeStruct((2, 1024, 128), f32)),
        in_specs=[
            pl.BlockSpec((128, 256), lambda t, y: (t * 4 + y, 0)),
            pl.BlockSpec((128, 256), lambda t, y: (t * 4 + y, 0)),
            pl.BlockSpec((1, 1024, 128), lambda t, y: (t, 0, 0)),
            pl.BlockSpec((128, 128), lambda t, y: (t * 4 + y, 0)),
            pl.BlockSpec((512, 128), lambda t, y: (t * 4 + y, 0)),
        ],
        out_specs=(
            pl.BlockSpec((128, 256), lambda t, y: (t * 4 + y, 0)),
            pl.BlockSpec((1, 1024, 128), lambda t, y: (t, 0, 0)),
        ),
        compiler_params=pltpu.CompilerParams(vmem_limit_bytes=48 * 2**20),
    )(q, do, kv, bounds, lse)


def segment_bounds(lengths, offsets):
    ends = jnp.cumsum(lengths)
    starts = ends - lengths
    segment = jnp.sum((offsets[:, None] >= ends[None, :]).astype(jnp.int32), axis=1)
    seg_ids = np.arange(13)
    branch_of = jnp.asarray(np.where(seg_ids > 0, 1 + 3 * ((seg_ids - 1) // 3), 0), jnp.int32)
    onehot = segment[:, None] == jnp.asarray(seg_ids, jnp.int32)[None, :]

    def pick(values):
        return jnp.sum(jnp.where(onehot, values[None, :], 0), axis=1)

    table = np.zeros((13, 13), np.int32)
    for s in range(13):
        if s:
            table[s, 1 + 3 * ((s - 1) // 3)] = 1
        else:
            table[s, 0] = 1
    table = jnp.asarray(table)
    b0 = jnp.sum(table * starts[None, :], axis=1)
    b1 = jnp.sum(table * ends[None, :], axis=1)
    is_leaf = jnp.asarray((seg_ids > 0) & ((seg_ids - 1) % 3 > 0), jnp.int32)
    depth = jnp.where(jnp.asarray(seg_ids > 0), lengths[0], 0) + is_leaf * (b1 - b0)
    position = offsets - pick(starts) + pick(depth)
    trunk = jnp.broadcast_to(lengths[0], offsets.shape)
    return jnp.stack([offsets, trunk, pick(starts), pick(b0), pick(b1)], axis=1), position


def rope(u, cosine, sine):
    rows, width = u.shape
    halves = u.reshape(rows, width // 64, 2, 32)
    other = jnp.flip(halves, axis=2).reshape(rows, width)
    m = width // 64
    return u * jnp.tile(cosine, (1, m)) + other * jnp.tile(sine, (1, m))


def shards(tokens, cotangent, tree_lengths, gain_attn, w_qkv, w_out, gain_mlp, w_gate, w_up, w_down):
    at = Place()
    swapped = lax.ppermute(tree_lengths, "fsdp", [(f, f ^ 1) for f in range(16)])
    lengths = jnp.where(at.k == 0, jnp.stack([tree_lengths[0], swapped[0]]), jnp.stack([swapped[0], tree_lengths[0]]))
    offsets = (
        (2 * jnp.arange(4, dtype=jnp.int32)[:, None] + at.zl) * 128 + jnp.arange(128, dtype=jnp.int32)[None, :]
    ).reshape(512)
    b_a, p_a = segment_bounds(lengths[0], offsets)
    b_b, p_b = segment_bounds(lengths[1], offsets)
    bounds = jnp.pad(jnp.concatenate([b_a, b_b], axis=0), ((0, 0), (0, 123)))
    position = jnp.concatenate([p_a, p_b], axis=0).astype(f32)
    frequency = 10000.0 ** (-2.0 * jnp.arange(32, dtype=f32) / 64)
    angles = position[:, None] * frequency[None, :]
    cosine = jnp.concatenate([jnp.cos(angles)] * 2, axis=1)
    sine = jnp.concatenate([-jnp.sin(angles), jnp.sin(angles)], axis=1)

    gain1 = gain_attn.astype(f32)[:, None]
    gain2 = gain_mlp.astype(f32)[:, None]
    q_cols = lax.dynamic_slice_in_dim(w_qkv, at.y * 512, 512, axis=1).astype(f32) * gain1
    k_cols = lax.dynamic_slice_in_dim(w_qkv, 2048 + at.y * 64, 64, axis=1).astype(f32) * gain1
    v_cols = lax.dynamic_slice_in_dim(w_qkv, 2304 + at.y * 64, 64, axis=1).astype(f32) * gain1
    wq = jnp.stack([jnp.concatenate([q_cols[:, 256 * i : 256 * i + 256], k_cols, v_cols], axis=1) for i in range(2)])
    g_cols = lax.dynamic_slice_in_dim(w_gate, at.y * 2 * FJ, 2 * FJ, axis=1).astype(f32) * gain2
    u_cols = lax.dynamic_slice_in_dim(w_up, at.y * 2 * FJ, 2 * FJ, axis=1).astype(f32) * gain2
    wg = jnp.stack([g_cols[:, :FJ], g_cols[:, FJ:]])
    wu = jnp.stack([u_cols[:, :FJ], u_cols[:, FJ:]])

    inputs = tokens.astype(f32)
    inv1 = lax.rsqrt(jnp.mean(inputs * inputs, axis=-1, keepdims=True) + epsilon)
    hat1 = inputs * inv1
    hat_all, cot_all, gq, gg, gu, go, gd = gather_weights(
        hat1.astype(bf16), cotangent, wq.astype(bf16), wg.astype(bf16), wu.astype(bf16), w_out, w_down
    )
    hat_all = hat_all.reshape(1024, D)
    cot_all = cot_all.reshape(1024, D)
    gq, gg, gu = gq.reshape(D, 384), gg.reshape(D, FJ), gu.reshape(D, FJ)

    proj = jnp.dot(hat_all, gq, preferred_element_type=f32)
    q = rope(proj[:, :256], cosine, sine).astype(bf16)
    kv = jnp.concatenate([rope(proj[:, 256:320], cosine, sine), proj[:, 320:]], axis=1).astype(bf16)
    kv_far = lax.ppermute(kv, "ctx", [(c, c ^ 1) for c in range(8)])

    def weave(mine, far):
        lo = jnp.where(at.zl == 0, mine, far).reshape(2, 4, 1, 128, 128)
        hi = jnp.where(at.zl == 0, far, mine).reshape(2, 4, 1, 128, 128)
        return jnp.concatenate([lo, hi], axis=2).reshape(2, 1024, 128)

    kv_tree = weave(kv, kv_far)
    attended, lse = attend_fwd(q, kv_tree, bounds)
    hidden = inputs + ring_reduce(jnp.dot(attended, go, preferred_element_type=f32).astype(bf16))
    inv2 = lax.rsqrt(jnp.mean(hidden * hidden, axis=-1, keepdims=True) + epsilon)
    hat2 = hidden * inv2
    hat2_all = ring_gather(hat2.astype(bf16))
    gate = jnp.dot(hat2_all, gg, preferred_element_type=f32)
    up = jnp.dot(hat2_all, gu, preferred_element_type=f32)
    sig = jax.nn.sigmoid(gate)
    silu = gate * sig
    inner = (silu * up).astype(bf16)
    grad_inner = dot_nt(cot_all, gd)
    dgate = (grad_inner * up * sig * (1.0 + gate * (1.0 - sig))).astype(bf16)
    dup = (grad_inner * silu).astype(bf16)
    scaled2 = ring_reduce((dot_nt(dgate, gg) + dot_nt(dup, gu)).astype(bf16))
    mixed = (hidden + ring_reduce(jnp.dot(inner, gd, preferred_element_type=f32).astype(bf16))).astype(bf16)
    ghidden = cotangent.astype(f32) + inv2 * (scaled2 - hat2 * jnp.mean(scaled2 * hat2, axis=-1, keepdims=True))
    gb_all = ring_gather(ghidden.astype(bf16))
    dattended = dot_nt(gb_all, go).astype(bf16)
    dq, dkv = attend_bwd(q, dattended, kv_tree, bounds, lse)
    dkv = dkv.reshape(2, 4, 2, 128, 128)
    dkv_mine = jnp.where(at.zl == 0, dkv[:, :, 0], dkv[:, :, 1]).reshape(1024, 128)
    dkv_far = jnp.where(at.zl == 0, dkv[:, :, 1], dkv[:, :, 0]).reshape(1024, 128).astype(bf16)
    dkv_sum = dkv_mine + lax.ppermute(dkv_far, "ctx", [(c, c ^ 1) for c in range(8)]).astype(f32)
    dproj = jnp.concatenate(
        [rope(dq, cosine, -sine), rope(dkv_sum[:, :64], cosine, -sine), dkv_sum[:, 64:]], axis=1
    ).astype(bf16)
    scaled1 = ring_reduce(dot_nt(dproj, gq).astype(bf16))
    grad_tokens = ghidden + inv1 * (scaled1 - hat1 * jnp.mean(scaled1 * hat1, axis=-1, keepdims=True))

    def blocks(left, right):
        n = left.shape[1]
        return dot_tn(left, right).astype(bf16).reshape(n, 16, 128).transpose(1, 0, 2)

    part_q = dot_tn(hat_all, dproj).astype(bf16).reshape(16, 128, 384)
    part_g = dot_tn(hat2_all, dgate).astype(bf16).reshape(16, 128, FJ)
    part_u = dot_tn(hat2_all, dup).astype(bf16).reshape(16, 128, FJ)
    part_o = blocks(attended, gb_all)
    part_d = blocks(inner, cot_all)
    sums = (
        plane_reduce(part_q, "x", "z", 3),
        plane_reduce(part_g, "x", "z", 4),
        plane_reduce(part_u, "z", "x", 5),
        plane_reduce(part_o, "z", "x", 6),
        plane_reduce(part_d, "z", "x", 7),
    )
    oq, og, ou, oo, od = spread(*sums)
    oq, og, ou = oq.astype(f32), og.astype(f32), ou.astype(f32)
    q_part = oq[:, :, :256].transpose(1, 0, 2).reshape(128, 2048)
    kv_part = oq[:, :, 256:].reshape(4, 2, 128, 2, 64).sum(axis=1)
    k_part = kv_part[:, :, 0].transpose(1, 0, 2).reshape(128, 256)
    v_part = kv_part[:, :, 1].transpose(1, 0, 2).reshape(128, 256)
    raw_qkv = jnp.concatenate([q_part, k_part, v_part], axis=1)
    raw_gate = og.transpose(1, 0, 2).reshape(128, FF)
    raw_up = ou.transpose(1, 0, 2).reshape(128, FF)
    grad_gain1 = jnp.sum(raw_qkv * w_qkv.astype(f32), axis=1)
    grad_gain2 = jnp.sum(raw_gate * w_gate.astype(f32) + raw_up * w_up.astype(f32), axis=1)
    return (
        mixed,
        grad_tokens,
        grad_gain1,
        raw_qkv * gain1,
        oo.astype(f32),
        grad_gain2,
        raw_gate * gain2,
        raw_up * gain2,
        od.astype(f32),
    )


def solution(mesh):
    row = P("fsdp", None)
    tok = P(("fsdp", "ctx"), None)
    vec = P("fsdp")
    return jax.shard_map(
        shards,
        mesh=mesh,
        in_specs=(tok, tok, row, vec, row, row, vec, row, row, row),
        out_specs=(tok, tok, vec, row, row, vec, row, row, row),
        check_vma=False,
    )
```

```python
import functools

import jax
import jax.numpy as jnp
import numpy as np
from jax import lax
from jax.experimental import pallas as pl
from jax.experimental.pallas import tpu as pltpu
from jax.sharding import PartitionSpec as P

D = 2048
FF = 5632
H = 32
KVH = 4
HD = 64
FJ = FF // 8
bf16 = jnp.bfloat16
f32 = jnp.float32
MESH = pl.DeviceIdType.MESH
epsilon = 1e-05
masked_score = -1e30
ANY = pl.BlockSpec(memory_space=pl.ANY)
VM = pl.BlockSpec(memory_space=pltpu.VMEM)


class Place:
    def __init__(self):
        fs = lax.axis_index("fsdp")
        ct = lax.axis_index("ctx")
        self.zh, self.x, self.k = fs // 8, (fs // 2) % 4, fs % 2
        self.y, self.zl = ct // 2, ct % 2
        self.z = 2 * self.zh + self.zl

    def device(self, z=None, x=None, k=None, y=None):
        z = self.z if z is None else z
        x = self.x if x is None else x
        k = self.k if k is None else k
        y = self.y if y is None else y
        return ((z // 2) * 8 + x * 2 + k, y * 2 + z % 2)

    def sibling(self):
        return self.device(k=1 - self.k)

    def along(self, axis, r):
        at = (getattr(self, axis) + r + 4) % 4
        return self.device(**{axis: at})

    def piece(self, z=None, x=None):
        z = self.z if z is None else z
        x = self.x if x is None else x
        return (z // 2) * 8 + x * 2 + z % 2

    def moved(self, axis, r):
        return (getattr(self, axis) + r + 4) % 4


def rcopy(src, dst, ssem, rsem, dev):
    return pltpu.make_async_remote_copy(
        src_ref=src, dst_ref=dst, send_sem=ssem, recv_sem=rsem, device_id=dev, device_id_type=MESH
    )


def greet(devices):
    bar = pltpu.get_barrier_semaphore()
    for dev in devices:
        pl.semaphore_signal(bar, inc=1, device_id=dev, device_id_type=MESH)


def await_greetings(count):
    pl.semaphore_wait(pltpu.get_barrier_semaphore(), count)


class RingGather:
    messages = 12

    def __init__(self, at, buf, ssem, rsem):
        self.at, self.buf, self.ssem, self.rsem = at, buf, ssem, rsem

    def half(self, r, h, k=None):
        k = self.at.k if k is None else k
        return self.buf.at[k * 4 + self.at.moved("y", r), pl.ds(64 * h, 64)]

    def copy(self, d, m, incoming):
        step = 1 - 2 * d
        h = d if m in (0, 2) else 1 - d
        back = (-step if m == 2 else 0) - (step if incoming else 0)
        ref = self.half(back, h)
        i = d * 3 + m
        return rcopy(ref, ref, self.ssem.at[i], self.rsem.at[i], self.at.along("y", step))

    def relay(self, i, incoming):
        k = 1 - self.at.k if incoming else self.at.k
        if i < 6:
            d, m = i // 3, i % 3
            step = 1 - 2 * d
            h = d if m in (0, 2) else 1 - d
            ref = self.half((-2 if m == 2 else -1) * step, h, k)
        else:
            ref = self.half(0, i - 6, k)
        return rcopy(ref, ref, self.ssem.at[6 + i], self.rsem.at[6 + i], self.at.sibling())

    def start(self):
        for m in (0, 1):
            for d in (0, 1):
                self.copy(d, m, False).start()
        for i in (6, 7):
            self.relay(i, False).start()

    def step(self, m):
        for d in (0, 1):
            self.copy(d, m, True).wait_recv()
            if m == 0:
                self.copy(d, 2, False).start()
            self.relay(d * 3 + m, False).start()

    def finish(self):
        for i in range(8):
            self.relay(i, True).wait_recv()
            self.relay(i, False).wait_send()
        for d in (0, 1):
            for m in range(3):
                self.copy(d, m, False).wait_send()


RING_SEMS = 14


class RingReduce:
    def __init__(self, at, part, sib, recv, ssem, rsem):
        self.at, self.part, self.sib, self.recv = at, part, sib, recv
        self.ssem, self.rsem = ssem, rsem

    def cross(self, r):
        y = self.at.moved("y", r)
        return rcopy(
            self.part.at[(1 - self.at.k) * 4 + y], self.sib.at[r], self.ssem.at[6 + r], self.rsem.at[6 + r], self.at.sibling()
        )

    def copy(self, d, m):
        step = 1 - 2 * d
        h = d if m in (0, 2) else 1 - d
        y = self.at.moved("y", 2 if m == 0 else step)
        i = d * 3 + m
        return rcopy(
            self.part.at[self.at.k * 4 + y, pl.ds(64 * h, 64)], self.recv.at[i], self.ssem.at[i], self.rsem.at[i], self.at.along("y", step)
        )

    def cross_all(self):
        for r in (2, 1, 3, 0):
            self.cross(r).start()

    def add(self, r, h, others):
        y = self.at.moved("y", r)

        @pl.loop(0, 4)
        def _(i):
            rows = pl.ds(pl.multiple_of(64 * h + i * 16, 16), 16)
            total = self.part[self.at.k * 4 + y, rows, :].astype(f32) + self.sib[r, rows, :].astype(f32)
            for o in others:
                total += self.recv[o, pl.ds(pl.multiple_of(i * 16, 16), 16), :].astype(f32)
            self.part[self.at.k * 4 + y, rows, :] = total.astype(bf16)

    def first(self):
        self.cross(2).wait_recv()
        for d in (0, 1):
            self.add(2, d, ())
            self.copy(d, 0).start()
        for d in (0, 1):
            r = 1 if d == 0 else 3
            self.cross(r).wait_recv()
            self.add(r, 1 - d, ())
            self.copy(d, 1).start()

    def second(self):
        for d in (0, 1):
            self.copy(d, 0).wait_recv()
            self.add(1 if d == 0 else 3, d, (d * 3,))
            self.copy(d, 2).start()

    def collect(self, emit):
        self.cross(0).wait_recv()
        for d in (0, 1):
            for m in (1, 2):
                self.copy(d, m).wait_recv()
        for h in range(2):
            left, right = (2, 4) if h == 0 else (1, 5)

            @pl.loop(0, 4)
            def _(i):
                rows = pl.ds(pl.multiple_of(64 * h + i * 16, 16), 16)
                here = pl.ds(pl.multiple_of(i * 16, 16), 16)
                total = self.part[self.at.k * 4 + self.at.y, rows, :].astype(f32) + self.sib[0, rows, :].astype(f32)
                total += self.recv[left, here, :].astype(f32) + self.recv[right, here, :].astype(f32)
                emit(rows, total)

    def finish(self):
        for r in range(4):
            self.cross(r).wait_send()
        for d in (0, 1):
            for m in range(3):
                self.copy(d, m).wait_send()


REDUCE_SEMS = 10


class PlaneReduce:
    def __init__(self, at, part, recv, first, second, ssem, rsem):
        self.at, self.part, self.recv = at, part, recv
        self.first, self.second, self.ssem, self.rsem = first, second, ssem, rsem
        self.rows = part.shape[1] // 2

    def piece(self, a, c):
        return self.at.piece(**{self.first: self.at.moved(self.first, a), self.second: self.at.moved(self.second, c)})

    def half(self, h):
        return pl.ds(h * self.rows, self.rows)

    def copy(self, c, d, m):
        step = 1 - 2 * d
        h = d if m in (0, 2) else 1 - d
        r = 2 if m == 0 else step
        p = self.piece(r, c) if c < 4 else self.piece(0, r)
        i = c * 6 + d * 3 + m
        return rcopy(
            self.part.at[p, self.half(h)], self.recv.at[i], self.ssem.at[i], self.rsem.at[i],
            self.at.along(self.first if c < 4 else self.second, step),
        )

    def add(self, p, h, others):
        @pl.loop(0, self.rows // 32)
        def _(i):
            rows = pl.ds(pl.multiple_of(h * self.rows + i * 32, 32), 32)
            here = pl.ds(pl.multiple_of(i * 32, 32), 32)
            total = self.part[p, rows, :].astype(f32)
            for o in others:
                total += self.recv[o, here, :].astype(f32)
            self.part[p, rows, :] = total.astype(bf16)

    def start(self, c):
        for m in (0, 1):
            for d in (0, 1):
                self.copy(c, d, m).start()

    def middle(self, c):
        for d in (0, 1):
            self.copy(c, d, 0).wait_recv()
            r = 1 - 2 * d
            p = self.piece(r, c) if c < 4 else self.piece(0, r)
            self.add(p, d, (c * 6 + d * 3,))
            self.copy(c, d, 2).start()

    def end(self, c):
        for d in (0, 1):
            for m in (1, 2):
                self.copy(c, d, m).wait_recv()
        p = self.piece(0, c) if c < 4 else self.piece(0, 0)
        self.add(p, 0, (c * 6 + 2, c * 6 + 4))
        self.add(p, 1, (c * 6 + 1, c * 6 + 5))

    def start_all(self):
        for c in (2, 1, 3, 0):
            self.start(c)

    def middle_all(self):
        for c in (2, 1, 3, 0):
            self.middle(c)

    def end_all(self):
        for c in (2, 1, 3, 0):
            self.end(c)
        self.start(4)

    def last(self):
        self.middle(4)
        self.end(4)

    def finish(self):
        for c in range(5):
            for d in (0, 1):
                for m in range(3):
                    self.copy(c, d, m).wait_send()


PLANE_SEMS = 30


class PlaneGather:
    def __init__(self, at, view, first, second, ssem, rsem):
        self.at, self.view, self.first, self.second = at, view, first, second
        self.ssem, self.rsem = ssem, rsem

    def copy(self, c, d, m, incoming):
        step = 1 - 2 * d
        h = d if m in (0, 2) else 1 - d
        back = (-step if m == 2 else 0) - (step if incoming else 0)
        a, b = (back, 0) if c == 4 else (c, back)
        p = self.at.piece(**{self.first: self.at.moved(self.first, a), self.second: self.at.moved(self.second, b)})
        ref = self.view(p, h)
        i = c * 6 + d * 3 + m
        axis = self.first if c == 4 else self.second
        return rcopy(ref, ref, self.ssem.at[i], self.rsem.at[i], self.at.along(axis, step))

    def start(self, c):
        for m in (0, 1):
            for d in (0, 1):
                self.copy(c, d, m, False).start()

    def middle(self, c):
        for d in (0, 1):
            self.copy(c, d, 0, True).wait_recv()
            self.copy(c, d, 2, False).start()

    def arrive(self, c, m):
        for d in (0, 1):
            self.copy(c, d, m, True).wait_recv()

    def step0(self):
        self.start(4)
        self.start(0)

    def step1(self):
        self.middle(4)
        self.arrive(4, 1)
        self.start(3)
        self.start(1)

    def step2(self):
        self.middle(0)
        self.arrive(4, 2)
        self.start(2)

    def step3(self):
        for c in (3, 1, 2):
            self.middle(c)

    def step4(self):
        for c in range(4):
            self.arrive(c, 1)
            self.arrive(c, 2)
        for c in range(5):
            for d in (0, 1):
                for m in range(3):
                    self.copy(c, d, m, False).wait_send()


def dot_nt(a, b):
    return lax.dot_general(a, b, (((1,), (1,)), ((), ())), preferred_element_type=f32)


def dot_nn(a, b):
    return lax.dot_general(a, b, (((1,), (0,)), ((), ())), preferred_element_type=f32)


def dot_tn(a, b):
    return lax.dot_general(a, b, (((0,), (0,)), ((), ())), preferred_element_type=f32)


Q0, O0, G0, U0, D0, ROWS = 0, 384, 640, 1344, 2048, 2752
SCALE = HD**-0.5


def rotate(u, cosine, sine, sign):
    a, b = u[:32], u[32:]
    s = sine * sign
    return jnp.concatenate([a * cosine - b * s, b * cosine + a * s], axis=0)


def mask_bias(bounds, n):
    key = lax.broadcasted_iota(jnp.int32, (n, 128), 0)
    own, trunk, start, b0, b1 = [bounds[i : i + 1, :] for i in range(5)]
    keep = (key <= own) & ((key < trunk) | (key >= start) | ((key >= b0) & (key < b1)))
    return jnp.where(keep, 0.0, masked_score)


def heads_side_by_side(ref, t, y):
    return jnp.concatenate([ref[t, 64 * h : 64 * h + 64, 128 * y : 128 * y + 128] for h in range(4)], axis=1)


def tree_keys(kvb, kvt, kvn, t):
    for y in range(4):
        for z in range(2):
            b = 2 * y + z
            blk = kvb[t, y, z]
            kvt[:, 128 * b : 128 * b + 128] = blk
            kvn[128 * b : 128 * b + 128, :] = blk.astype(f32).T.astype(bf16)


def forward_kernel(
    hat, x, cot, wcol, wo, wd, cosine, sine, bounds,
    hat_out, cot_all, w_all, q_out, kvb, att, lse, hidden, hat2_all,
    hat_all, wqo, part, sib, recv, kvt, kvn, own2,
    hsem_s, hsem_r, csem_s, csem_r, gsem_s, gsem_r, psem_s, psem_r, rsem_s, rsem_r,
    colsem_s, colsem_r, rowsem_s, rowsem_r, kvsem_s, kvsem_r, lsem,
):
    at = Place()
    k, y, zl = at.k, at.y, at.zl
    own8 = at.zh * 4 + at.x
    is_src = own8 // 2 == y
    kd = at.x % 2
    both = jnp.where(is_src & (kd == k), 1, 0)
    src_n = jnp.where(is_src, 1, 0)
    j = 2 * y + k
    jz, jx = (j // 4) * 2 + zl, j % 4
    zd = at.z + 1 - 2 * zl
    zpeer = at.device(z=zd)

    own = k * 4 + y
    piece = at.piece()
    lanes = pl.ds(pl.multiple_of(piece * 128, 128), 128)
    h_in = pltpu.make_async_copy(hat, hat_all.at[own], lsem.at[0])
    c_in = pltpu.make_async_copy(cot, cot_all.at[own], lsem.at[1])
    h_in.start()
    c_in.start()

    greet([at.sibling()] + [at.along(a, r) for a in ("x", "z", "y") for r in (1, -1)])
    for s in range(2):
        mine = (jz == at.z) & (jx == at.x) & (k == s)

        @pl.when(jnp.logical_not(mine))
        def _():
            greet([at.device(z=jz, x=jx, k=s)])

    def row_dest(t):
        q = (own8 + t) % 8
        z = (q // 4) * 2 + zl
        return at.device(z=z, x=q % 4, k=kd), at.piece(z=z, x=q % 4)

    @pl.when(is_src)
    def _():
        for t in range(8):
            dev, _ = row_dest(t)
            if t == 0:

                @pl.when(kd != k)
                def _():
                    greet([dev])
            else:
                greet([dev])

    await_greetings(7 + (2 - both) + src_n * 8 - both * src_n)

    ring_h = RingGather(at, hat_all, hsem_s, hsem_r)
    ring_c = RingGather(at, cot_all, csem_s, csem_r)
    ring_2 = RingGather(at, hat2_all, gsem_s, gsem_r)
    red = RingReduce(at, part, sib, recv, rsem_s, rsem_r)

    cols = ((0, 384, wqo, Q0), (384, 1408, w_all, G0))
    rows = ((wo, wqo, O0, 128), (wd, w_all, D0, 352))

    def col_send(i):
        s0, n, dst, d0 = cols[i]
        return rcopy(
            wcol.at[1 - k, pl.ds(s0, n)], dst.at[pl.ds(d0, n), lanes], colsem_s.at[i], colsem_r.at[i], at.sibling()
        )

    def col_keep(i):
        s0, n, dst, d0 = cols[i]
        return pltpu.make_async_copy(wcol.at[k, pl.ds(s0, n)], dst.at[pl.ds(d0, n), lanes], colsem_r.at[i])

    def row_send(i, t):
        src, dst, d0, n = rows[i]
        dev, p = row_dest(t)
        there = pl.ds(pl.multiple_of(p * 128, 128), 128)
        return rcopy(
            src.at[:, there], dst.at[pl.ds(pl.multiple_of(d0 + k * n, 16), n), there],
            rowsem_s.at[i, t], rowsem_r.at[i, k], dev,
        )

    def row_keep(i):
        src, dst, d0, n = rows[i]
        return pltpu.make_async_copy(
            src.at[:, lanes], dst.at[pl.ds(pl.multiple_of(d0 + k * n, 16), n), lanes], rowsem_r.at[i, k]
        )

    def row_in(i, s):
        src, dst, d0, n = rows[i]
        there = dst.at[pl.ds(d0 + s * n, n), lanes]
        return rcopy(there, there, rowsem_s.at[i, s], rowsem_r.at[i, s], at.device(z=jz, x=jx, k=s))

    @pl.when(k == zl)
    def _():
        for i in range(2):
            col_send(i).start()
            col_keep(i).start()

    h_in.wait()
    ring_h.start()

    @pl.when(is_src)
    def _():
        for i in range(2):
            for t in range(1, 8):
                row_send(i, t).start()

            @pl.when(kd == k)
            def _():
                row_keep(i).start()

            @pl.when(kd != k)
            def _():
                row_send(i, 0).start()

    def view(ref, r0, n):
        return lambda p, h: ref.at[pl.ds(r0 + h * (n // 2), n // 2), pl.ds(pl.multiple_of(p * 128, 128), 128)]

    planes = [
        PlaneGather(at, view(ref, r0, n), *order, psem_s.at[i], psem_r.at[i])
        for i, (ref, r0, n, order) in enumerate(
            (
                (wqo, Q0, 384, ("x", "z")),
                (wqo, O0, 256, ("z", "x")),
                (w_all, G0, 704, ("x", "z")),
                (w_all, U0, 704, ("z", "x")),
                (w_all, D0, 352, ("x", "z")),
                (w_all, D0 + 352, 352, ("z", "x")),
            )
        )
    ]
    pq, po = planes[:2]
    bulk = planes[2:]
    col_keep(0).wait()
    pq.step0()
    for s in range(2):
        row_in(0, s).wait_recv()
    po.step0()
    ring_h.step(0)
    pq.step1()
    po.step1()
    ring_h.step(1)
    pq.step2()
    po.step2()
    col_keep(1).wait()
    for p in bulk[:2]:
        p.step0()
    for s in range(2):
        row_in(1, s).wait_recv()
    for p in bulk[2:]:
        p.step0()
    pq.step3()
    po.step3()
    ring_h.step(2)
    ring_h.finish()
    c_in.wait()
    ring_c.start()
    pq.step4()

    @pl.loop(0, 4)
    def _(i):
        t, c = i // 2, i % 2
        h = hat_all[pl.ds(2 * i, 2)].reshape(256, D)
        proj = dot_nt(wqo[Q0 : Q0 + 384, :], h)
        col = pl.ds(pl.multiple_of(256 * c, 256), 256)
        co, si = cosine[t, :, col], sine[t, :, col]
        for head in range(4):
            u = rotate(proj[64 * head : 64 * head + 64], co, si, 1.0)
            q_out[t, 64 * head : 64 * head + 64, col] = (u * SCALE).astype(bf16)
        kv = jnp.concatenate([rotate(proj[256:320], co, si, 1.0), proj[320:]], axis=0).astype(bf16)
        for b in range(2):
            kvb[t, 2 * c + b, zl] = kv[:, 128 * b : 128 * b + 128]

    def kv_send():
        ref = kvb.at[k, :, zl]
        return rcopy(ref, ref, kvsem_s.at[0], kvsem_r.at[0], zpeer)

    def kv_in():
        ref = kvb.at[k, :, 1 - zl]
        return rcopy(ref, ref, kvsem_s.at[0], kvsem_r.at[0], zpeer)

    def kv_relay(kk):
        ref = kvb.at[kk, :, 1 - zl]
        return rcopy(ref, ref, kvsem_s.at[1], kvsem_r.at[1], at.sibling())

    kv_send().start()
    h_out = pltpu.make_async_copy(hat_all, hat_out, lsem.at[0])
    h_out.start()
    for p in bulk:
        p.step1()
    kv_in().wait_recv()
    kv_relay(k).start()
    po.step4()
    w_out_copy = pltpu.make_async_copy(wqo, w_all.at[pl.ds(0, G0)], lsem.at[2])
    w_out_copy.start()
    kv_relay(1 - k).wait_recv()

    def attend(t):
        tree_keys(kvb, kvt, kvn, t)
        for b in range(4):
            n = 256 * (b + 1)
            col = slice(128 * b, 128 * b + 128)
            qs = heads_side_by_side(q_out, t, b)
            qs = jnp.concatenate([qs, jnp.zeros_like(qs)], axis=0)
            bias = mask_bias(bounds[t, :, col], n)
            s = dot_nn(kvn[:n, :], qs) + jnp.concatenate([bias] * 4, axis=1)
            peak = jnp.max(s, axis=0, keepdims=True)
            e = jnp.exp(s - peak)
            total = jnp.sum(e, axis=0, keepdims=True)
            o = dot_nn(kvt[64:128, :n], e.astype(bf16)) / total
            log_total = peak + jnp.log(total)
            for head in range(4):
                c = slice(128 * head, 128 * head + 128)
                att[t, 64 * head : 64 * head + 64, col] = o[:, c].astype(bf16)
                lse[t, head : head + 1, col] = log_total[:, c]

        @pl.loop(0, 2)
        def _(i):
            a = att[t, :, pl.ds(pl.multiple_of(256 * i, 256), 256)]
            r = dot_tn(a, wqo[O0 : O0 + 256, :]).astype(bf16)
            part[pl.ds(4 * t + 2 * i, 2)] = r.reshape(2, 128, D)

    attend(1 - k)
    red.cross_all()
    ring_c.step(0)
    for p in bulk:
        p.step2()
    attend(k)
    red.first()
    ring_c.step(1)
    for p in bulk[:2]:
        p.step3()
    red.second()
    ring_c.step(2)
    for p in bulk[2:]:
        p.step3()

    def emit(rows, total):
        h = x[rows, :].astype(f32) + total
        hidden[rows, :] = h
        inv = lax.rsqrt(jnp.mean(h * h, axis=1, keepdims=True) + epsilon)
        own2[rows, :] = (h * inv).astype(bf16)

    red.collect(emit)
    two_in = pltpu.make_async_copy(own2, hat2_all.at[own], lsem.at[3])
    two_in.start()
    two_in.wait()
    ring_2.start()
    ring_c.finish()
    ring_2.step(0)
    ring_2.step(1)
    for p in bulk[:2]:
        p.step4()
    ring_2.step(2)
    for p in bulk[2:]:
        p.step4()
    ring_2.finish()
    red.finish()
    h_out.wait()
    w_out_copy.wait()
    kv_send().wait_send()
    kv_relay(k).wait_send()

    @pl.when(k == zl)
    def _():
        for i in range(2):
            col_send(i).wait_send()

    @pl.when(is_src)
    def _():
        for i in range(2):
            for t in range(1, 8):
                row_send(i, t).wait_send()

            @pl.when(kd != k)
            def _():
                row_send(i, 0).wait_send()


def forward_pass(hat, x, cot, wcol, wo, wd, cosine, sine, bounds):
    shape = jax.ShapeDtypeStruct
    dma = pltpu.SemaphoreType.DMA
    return pl.pallas_call(
        forward_kernel,
        name="forward_pass",
        out_shape=(
            shape((8, 128, D), bf16),
            shape((8, 128, D), bf16),
            shape((ROWS, D), bf16),
            shape((2, 256, 512), bf16),
            shape((2, 4, 2, 128, 128), bf16),
            shape((2, 256, 512), bf16),
            shape((2, 8, 512), f32),
            shape((128, D), f32),
            shape((8, 128, D), bf16),
        ),
        in_specs=[VM, VM, ANY, ANY, ANY, ANY, VM, VM, VM],
        out_specs=[ANY, ANY, ANY, VM, VM, VM, VM, VM, ANY],
        scratch_shapes=[
            pltpu.VMEM((8, 128, D), bf16),
            pltpu.VMEM((G0, D), bf16),
            pltpu.VMEM((8, 128, D), bf16),
            pltpu.VMEM((4, 128, D), bf16),
            pltpu.VMEM((6, 64, D), bf16),
            pltpu.VMEM((128, 1024), bf16),
            pltpu.VMEM((1024, 128), bf16),
            pltpu.VMEM((128, D), bf16),
        ]
        + [dma((RING_SEMS,))] * 6
        + [dma((6, PLANE_SEMS))] * 2
        + [dma((REDUCE_SEMS,))] * 2
        + [dma((2,)), dma((2,)), dma((2, 8)), dma((2, 2)), dma((2,)), dma((2,)), dma((4,))],
        compiler_params=pltpu.CompilerParams(
            collective_id=0, has_side_effects=True, vmem_limit_bytes=56 * 2**20
        ),
    )(hat, x, cot, wcol, wo, wd, cosine, sine, bounds)


def mlp_kernel(
    hat2_hbm, cot_hbm, w_hbm, hidden, cot,
    ghidden, gb_all, mixed_part, up_part, sum_g, sum_d,
    hat2, cotv, wg, wu, wdn, part, sib, recv, innert, dgt, dut, pd, pg, precv_d, precv_g, tile, own_gb,
    rsem_s, rsem_r, gsem_s, gsem_r, psem_s, psem_r, lsem, tsem,
):
    at = Place()
    k, y = at.k, at.y
    loads = [
        pltpu.make_async_copy(src, dst, lsem.at[i])
        for i, (src, dst) in enumerate(
            (
                (w_hbm.at[pl.ds(G0, 704)], wg),
                (hat2_hbm, hat2),
                (w_hbm.at[pl.ds(U0, 704)], wu),
                (w_hbm.at[pl.ds(D0, 704)], wdn),
                (cot_hbm, cotv),
            )
        )
    ]
    for c in loads:
        c.start()
    greet([at.sibling()] + [at.along(a, r) for a in ("x", "z", "y") for r in (1, -1)])
    await_greetings(7)
    red = RingReduce(at, part, sib, recv, rsem_s, rsem_r)
    ring = RingGather(at, gb_all, gsem_s, gsem_r)
    pr_d = PlaneReduce(at, pd, precv_d, "x", "z", psem_s.at[0], psem_r.at[0])
    pr_g = PlaneReduce(at, pg, precv_g, "z", "x", psem_s.at[1], psem_r.at[1])
    for c in loads:
        c.wait()

    def mlp_half(t):
        @pl.loop(0, 2)
        def _(i):
            slot = 4 * t + 2 * i
            cols = pl.ds(pl.multiple_of(slot * 128, 256), 256)
            h = hat2[pl.ds(slot, 2)].reshape(256, D)
            c = cotv[pl.ds(slot, 2)].reshape(256, D)
            gate = dot_nt(wg[...], h)
            up = dot_nt(wu[...], h)
            sig = jax.nn.sigmoid(gate)
            silu = gate * sig
            innert[:, cols] = (silu * up).astype(bf16)
            gi = dot_nt(wdn[...], c)
            dg = (gi * up * sig * (1.0 + gate * (1.0 - sig))).astype(bf16)
            du = (gi * silu).astype(bf16)
            dgt[:, cols] = dg
            dut[:, cols] = du
            r = (dot_tn(dg, wg[...]) + dot_tn(du, wu[...])).astype(bf16)
            part[pl.ds(slot, 2)] = r.reshape(2, 128, D)

    def weight_grad(left, right, store):
        @pl.loop(0, 8)
        def _(i):
            cols = pl.ds(pl.multiple_of(256 * i, 256), 256)
            g = dot_nn(left[...], right[:, :, cols].reshape(1024, 256)).astype(bf16)
            store(i, g)

    def into(ref):
        def store(i, g):
            ref[2 * i] = g[:, :128]
            ref[2 * i + 1] = g[:, 128:]

        return store

    mlp_half(1 - k)
    red.cross_all()
    mlp_half(k)
    red.first()
    weight_grad(innert, cotv, into(pd))
    pr_d.start_all()
    red.second()
    weight_grad(dgt, hat2, into(pg))
    pr_g.start_all()
    pr_d.middle_all()

    def emit(rows, total):
        h = hidden[rows, :]
        inv = lax.rsqrt(jnp.mean(h * h, axis=1, keepdims=True) + epsilon)
        hat = h * inv
        g = cot[rows, :].astype(f32) + inv * (total - hat * jnp.mean(total * hat, axis=1, keepdims=True))
        ghidden[rows, :] = g
        own_gb[rows, :] = g.astype(bf16)

    red.collect(emit)
    gb_in = pltpu.make_async_copy(own_gb, gb_all.at[k * 4 + y], lsem.at[0])
    gb_in.start()
    gb_in.wait()
    ring.start()
    pr_g.middle_all()

    def store_tile(dst_of):
        def store(i, g):
            tile[0] = g[:, :128]
            tile[1] = g[:, 128:]
            cp = pltpu.make_async_copy(tile, dst_of(i), tsem)
            cp.start()
            cp.wait()

        return store

    ring.step(0)
    weight_grad(dut, hat2, store_tile(lambda i: up_part.at[pl.ds(2 * i, 2)]))
    ring.step(1)
    pr_d.end_all()
    pr_g.end_all()
    red.finish()
    ring.step(2)

    @pl.loop(0, 4)
    def _(i):
        cols = pl.ds(pl.multiple_of(256 * i, 256), 256)
        r = dot_tn(innert[:, cols], wdn[...]).astype(bf16)
        part[pl.ds(2 * i, 2)] = r.reshape(2, 128, D)

    m_out = pltpu.make_async_copy(part, mixed_part, lsem.at[1])
    m_out.start()
    pr_d.last()
    d_out = pltpu.make_async_copy(pd.at[at.piece()], sum_d, lsem.at[2])
    d_out.start()
    pr_g.last()
    g_out = pltpu.make_async_copy(pg.at[at.piece()], sum_g, lsem.at[3])
    g_out.start()
    ring.finish()
    pr_d.finish()
    pr_g.finish()
    m_out.wait()
    d_out.wait()
    g_out.wait()


def mlp_pass(hat2_all, cot_all, w_all, hidden, cot):
    shape = jax.ShapeDtypeStruct
    dma = pltpu.SemaphoreType.DMA
    block = pltpu.VMEM((8, 128, D), bf16)
    return pl.pallas_call(
        mlp_kernel,
        name="mlp_pass",
        out_shape=(
            shape((128, D), f32),
            shape((8, 128, D), bf16),
            shape((8, 128, D), bf16),
            shape((16, FJ, 128), bf16),
            shape((FJ, 128), bf16),
            shape((FJ, 128), bf16),
        ),
        in_specs=[ANY, ANY, ANY, VM, VM],
        out_specs=[VM, ANY, ANY, ANY, ANY, ANY],
        scratch_shapes=[
            block, block,
            pltpu.VMEM((FJ, D), bf16), pltpu.VMEM((FJ, D), bf16), pltpu.VMEM((FJ, D), bf16),
            block,
            pltpu.VMEM((4, 128, D), bf16),
            pltpu.VMEM((6, 64, D), bf16),
            pltpu.VMEM((FJ, 1024), bf16), pltpu.VMEM((FJ, 1024), bf16), pltpu.VMEM((FJ, 1024), bf16),
            pltpu.VMEM((16, FJ, 128), bf16), pltpu.VMEM((16, FJ, 128), bf16),
            pltpu.VMEM((30, FJ // 2, 128), bf16), pltpu.VMEM((30, FJ // 2, 128), bf16),
            pltpu.VMEM((2, FJ, 128), bf16),
            pltpu.VMEM((128, D), bf16),
            dma((REDUCE_SEMS,)), dma((REDUCE_SEMS,)), dma((RING_SEMS,)), dma((RING_SEMS,)),
            dma((2, PLANE_SEMS)), dma((2, PLANE_SEMS)), dma((5,)), dma,
        ],
        compiler_params=pltpu.CompilerParams(
            collective_id=1, has_side_effects=True, vmem_limit_bytes=62 * 2**20
        ),
    )(hat2_all, cot_all, w_all, hidden, cot)


class Spread:
    def __init__(self, at, csem_s, csem_r, rsem_s, rsem_r):
        self.at = at
        self.csem_s, self.csem_r, self.rsem_s, self.rsem_r = csem_s, csem_r, rsem_s, rsem_r
        self.j = 2 * at.y + at.k
        self.jzh, self.jx = self.j // 4, self.j % 4
        self.keep_col = at.k == at.zl
        self.self_row = (self.jzh == at.zh) & (self.jx == at.x)

    def col_dev(self, dy, dz):
        at = self.at
        return at.device(z=2 * at.zh + (at.zl + dz) % 2, y=at.moved("y", dy), k=at.zl)

    def row_dev(self, dy, dz, cc):
        at = self.at
        return at.device(z=2 * self.jzh + (at.zl + dz) % 2, x=self.jx, y=at.moved("y", dy), k=cc)

    def each_col(self, f, g):
        for dy in (2, 1, 3, 0):
            for dz in (1, 0):
                if dy == 0 and dz == 0:
                    pl.when(self.keep_col)(g)
                    pl.when(jnp.logical_not(self.keep_col))(functools.partial(f, dy, dz))
                else:
                    f(dy, dz)

    def each_row(self, f, g):
        for dy in (2, 1, 3, 0):
            for dz in (1, 0):
                for cc in range(2):
                    if dy == 0 and dz == 0:
                        mine = self.self_row & (self.at.k == cc)
                        pl.when(mine)(functools.partial(g, cc))
                        pl.when(jnp.logical_not(mine))(functools.partial(f, dy, dz, cc))
                    else:
                        f(dy, dz, cc)

    def greet(self):
        at = self.at
        src_y, src_k = (at.zh * 4 + at.x) // 2, at.x % 2

        def nothing(*_):
            pass

        self.each_col(lambda dy, dz: greet([self.col_dev(dy, dz)]), nothing)
        self.each_row(lambda dy, dz, cc: greet([self.row_dev(dy, dz, cc)]), nothing)
        for y in range(4):
            for k in range(2):
                mine = (at.y == y) & (at.k == k) & (at.zl == at.k)

                @pl.when(jnp.logical_not(mine))
                def _():
                    greet([at.device(z=2 * at.zh + at.k, y=y, k=k)])

        for p in range(16):
            z, x = (p // 8) * 2 + p % 2, (p // 2) % 4
            mine = (at.z == z) & (at.x == x) & (at.y == src_y) & (at.k == src_k)

            @pl.when(jnp.logical_not(mine))
            def _():
                greet([at.device(z=z, x=x, y=src_y, k=src_k)])

        return 2 * jnp.where(self.keep_col, 7, 8) + 2 * (16 - jnp.where(self.self_row, 1, 0))

    def col_copy(self, i, src, dst, dy, dz):
        n = dy * 2 + dz
        return rcopy(src, dst.at[self.j], self.csem_s.at[i, n], self.csem_r.at[i, self.j], self.col_dev(dy, dz))

    def col_start(self, i, src, dst):
        def local():
            pltpu.make_async_copy(src, dst.at[self.j], self.csem_r.at[i, self.j]).start()

        self.each_col(lambda dy, dz: self.col_copy(i, src, dst, dy, dz).start(), local)

    def col_finish(self, i, src, dst):
        for q in range(8):
            pltpu.make_async_copy(src, dst.at[q], self.csem_r.at[i, q]).wait()
        self.each_col(lambda dy, dz: self.col_copy(i, src, dst, dy, dz).wait_send(), lambda: None)

    def lanes(self):
        return pl.ds(pl.multiple_of(self.at.piece() * 128, 128), 128)

    def row_copy(self, i, src, dst, m, dy, dz, cc):
        n = (dy * 2 + dz) * 2 + cc
        return rcopy(
            src.at[pl.ds(cc * m, m)], dst.at[:, self.lanes()], self.rsem_s.at[i, n],
            self.rsem_r.at[i, self.at.piece()], self.row_dev(dy, dz, cc),
        )

    def row_start(self, i, src, dst, m):
        def local(cc):
            pltpu.make_async_copy(
                src.at[pl.ds(cc * m, m)], dst.at[:, self.lanes()], self.rsem_r.at[i, self.at.piece()]
            ).start()

        self.each_row(lambda dy, dz, cc: self.row_copy(i, src, dst, m, dy, dz, cc).start(), local)

    def row_finish(self, i, src, dst, m):
        for p in range(16):
            pltpu.make_async_copy(
                src.at[pl.ds(0, m)], dst.at[:, pl.ds(p * 128, 128)], self.rsem_r.at[i, p]
            ).wait()
        self.each_row(lambda dy, dz, cc: self.row_copy(i, src, dst, m, dy, dz, cc).wait_send(), lambda cc: None)


def backward_kernel(
    gb_hbm, hat_hbm, w_hbm, q, kvb, att, lse, cosine, sine, bounds, x, hidden, ghidden, mixed_part, up_part, sum_g, sum_d,
    mixed, grad_tokens, out_q, out_g, out_u, out_o, out_d,
    gb, hat, wqo, pu, pq, po, precv_u, precv_q, precv_o, part, sib, recv, mpart, msib, mrecv,
    datt, dproj, dkv, dkv_far, dkv_got, kvt, kvn,
    rsem_s, rsem_r, msem_s, msem_r, psem_s, psem_r, xsem_s, xsem_r, csem_s, csem_r, wsem_s, wsem_r, lsem,
):
    at = Place()
    k, y, zl = at.k, at.y, at.zl
    zpeer = at.device(z=at.z + 1 - 2 * zl)
    loads = [
        pltpu.make_async_copy(src, dst, lsem.at[i])
        for i, (src, dst) in enumerate(
            (
                (w_hbm.at[pl.ds(0, G0)], wqo),
                (gb_hbm, gb),
                (up_part, pu),
                (mixed_part, mpart),
                (hat_hbm, hat),
            )
        )
    ]
    for c in loads:
        c.start()
    spread = Spread(at, csem_s, csem_r, wsem_s, wsem_r)
    greet([at.sibling()] + [at.along(a, r) for a in ("x", "z", "y") for r in (1, -1)])
    await_greetings(7 + spread.greet())

    red = RingReduce(at, part, sib, recv, rsem_s, rsem_r)
    redm = RingReduce(at, mpart, msib, mrecv, msem_s, msem_r)
    pr_u = PlaneReduce(at, pu, precv_u, "x", "z", psem_s.at[0], psem_r.at[0])
    pr_q = PlaneReduce(at, pq, precv_q, "z", "x", psem_s.at[1], psem_r.at[1])
    pr_o = PlaneReduce(at, po, precv_o, "z", "x", psem_s.at[2], psem_r.at[2])
    loads[2].wait()
    pr_u.start_all()
    loads[3].wait()
    redm.cross_all()
    loads[0].wait()
    loads[1].wait()

    @pl.loop(0, 4)
    def _(i):
        g = gb[pl.ds(2 * i, 2)].reshape(256, D)
        r = dot_nt(wqo[O0 : O0 + 256, :], g)
        datt[i // 2, :, pl.ds(pl.multiple_of(256 * (i % 2), 256), 256)] = r.astype(bf16)

    redm.first()

    def weight_grad(left, right, ref):
        @pl.loop(0, 8)
        def _(i):
            cols = pl.ds(pl.multiple_of(256 * i, 256), 256)
            g = dot_nn(left[0], right[0:4, :, cols].reshape(512, 256))
            g += dot_nn(left[1], right[4:8, :, cols].reshape(512, 256))
            g = g.astype(bf16)
            ref[2 * i] = g[:, :128]
            ref[2 * i + 1] = g[:, 128:]

    weight_grad(att, gb, po)
    pr_o.start_all()
    spread.col_start(1, sum_g, out_g)
    spread.row_start(1, sum_d, out_d, 352)

    def attend(t):
        tree_keys(kvb, kvt, kvn, t)
        for b in (3, 2, 1, 0):
            n = 256 * (b + 1)
            col = slice(128 * b, 128 * b + 128)
            qs = heads_side_by_side(q, t, b)
            dos = heads_side_by_side(datt, t, b)
            zero = jnp.zeros_like(qs)
            bias = mask_bias(bounds[t, :, col], n)
            log_total = jnp.concatenate([lse[t, h : h + 1, col] for h in range(4)], axis=1)
            s = dot_nn(kvn[:n, :], jnp.concatenate([qs, zero], axis=0)) + jnp.concatenate([bias] * 4, axis=1)
            prob = jnp.exp(s - log_total)
            dprob = dot_nn(kvn[:n, :], jnp.concatenate([zero, dos], axis=0))
            inner = jnp.sum(prob * dprob, axis=0, keepdims=True)
            ds = (prob * (dprob - inner)).astype(bf16)
            dq = dot_nn(kvt[0:64, :n], ds) * SCALE
            co, si = cosine[t, :, col], sine[t, :, col]
            for h in range(4):
                u = rotate(dq[:, 128 * h : 128 * h + 128], co, si, -1.0)
                dproj[t, 64 * h : 64 * h + 64, col] = u.astype(bf16)
            dk = dot_nt(qs, ds)
            dv = dot_nt(dos, prob.astype(bf16))
            for c in range(2 * (b + 1)):
                blk = slice(128 * c, 128 * c + 128)
                if b == 3:
                    dkv[t, c // 2, c % 2, :64, :] = dk[:, blk]
                    dkv[t, c // 2, c % 2, 64:, :] = dv[:, blk]
                else:
                    dkv[t, c // 2, c % 2, :64, :] += dk[:, blk]
                    dkv[t, c // 2, c % 2, 64:, :] += dv[:, blk]
        for b in range(4):
            dkv_far[t, b] = dkv[t, b, 1 - zl].astype(bf16)

    def far_copy(t, s):
        return rcopy(dkv_far.at[t], dkv_got.at[t], xsem_s.at[s], xsem_r.at[s], zpeer)

    def project(t, s):
        far_copy(t, s).wait_recv()
        for b in range(4):
            col = slice(128 * b, 128 * b + 128)
            total = dkv[t, b, zl] + dkv_got[t, b].astype(f32)
            dk = rotate(total[:64], cosine[t, :, col], sine[t, :, col], -1.0)
            dproj[t, 256:320, col] = dk.astype(bf16)
            dproj[t, 320:384, col] = total[64:].astype(bf16)

        @pl.loop(0, 2)
        def _(i):
            a = dproj[t, :, pl.ds(pl.multiple_of(256 * i, 256), 256)]
            r = dot_tn(a, wqo[Q0 : Q0 + 384, :]).astype(bf16)
            part[pl.ds(4 * t + 2 * i, 2)] = r.reshape(2, 128, D)

    attend(1 - k)
    far_copy(1 - k, 0).start()
    redm.second()
    pr_u.middle_all()
    attend(k)
    far_copy(k, 1).start()
    pr_o.middle_all()
    project(1 - k, 0)
    red.cross_all()
    project(k, 1)
    red.first()
    loads[4].wait()
    weight_grad(dproj, hat, pq)
    pr_q.start_all()

    def emit_mixed(rows, total):
        mixed[rows, :] = (hidden[rows, :] + total).astype(bf16)

    pr_u.end_all()
    redm.collect(emit_mixed)
    red.second()
    pr_o.end_all()
    pr_q.middle_all()
    pr_u.last()
    spread.col_start(2, pu.at[at.piece()], out_u)
    pr_o.last()
    spread.row_start(0, po.at[at.piece()], out_o, 128)

    def emit(rows, total):
        h = x[rows, :].astype(f32)
        inv = lax.rsqrt(jnp.mean(h * h, axis=1, keepdims=True) + epsilon)
        hat1 = h * inv
        g = ghidden[rows, :] + inv * (total - hat1 * jnp.mean(total * hat1, axis=1, keepdims=True))
        grad_tokens[rows, :] = g

    pr_q.end_all()
    red.collect(emit)
    pr_q.last()
    spread.col_start(0, pq.at[at.piece()], out_q)
    spread.col_finish(1, sum_g, out_g)
    spread.row_finish(1, sum_d, out_d, 352)
    spread.col_finish(2, pu.at[at.piece()], out_u)
    spread.row_finish(0, po.at[at.piece()], out_o, 128)
    spread.col_finish(0, pq.at[at.piece()], out_q)
    for s, t in ((0, 1 - k), (1, k)):
        far_copy(t, s).wait_send()
    red.finish()
    redm.finish()
    pr_u.finish()
    pr_o.finish()
    pr_q.finish()


def backward_pass(*args):
    shape = jax.ShapeDtypeStruct
    dma = pltpu.SemaphoreType.DMA
    block = pltpu.VMEM((8, 128, D), bf16)
    return pl.pallas_call(
        backward_kernel,
        name="backward_pass",
        out_shape=(
            shape((128, D), bf16),
            shape((128, D), f32),
            shape((8, 384, 128), bf16),
            shape((8, FJ, 128), bf16),
            shape((8, FJ, 128), bf16),
            shape((128, D), bf16),
            shape((352, D), bf16),
        ),
        in_specs=[ANY, ANY, ANY, VM, VM, VM, VM, VM, VM, VM, VM, VM, VM, ANY, ANY, ANY, ANY],
        out_specs=[VM, VM, ANY, ANY, ANY, ANY, ANY],
        scratch_shapes=[
            block, block, pltpu.VMEM((G0, D), bf16),
            pltpu.VMEM((16, FJ, 128), bf16), pltpu.VMEM((16, 384, 128), bf16), pltpu.VMEM((16, 256, 128), bf16),
            pltpu.VMEM((30, FJ // 2, 128), bf16), pltpu.VMEM((30, 192, 128), bf16), pltpu.VMEM((30, 128, 128), bf16),
            block, pltpu.VMEM((4, 128, D), bf16), pltpu.VMEM((6, 64, D), bf16),
            block, pltpu.VMEM((4, 128, D), bf16), pltpu.VMEM((6, 64, D), bf16),
            pltpu.VMEM((2, 256, 512), bf16),
            pltpu.VMEM((2, 384, 512), bf16),
            pltpu.VMEM((2, 4, 2, 128, 128), f32),
            pltpu.VMEM((2, 4, 128, 128), bf16),
            pltpu.VMEM((2, 4, 128, 128), bf16),
            pltpu.VMEM((128, 1024), bf16),
            pltpu.VMEM((1024, 128), bf16),
            dma((REDUCE_SEMS,)), dma((REDUCE_SEMS,)), dma((REDUCE_SEMS,)), dma((REDUCE_SEMS,)),
            dma((3, PLANE_SEMS)), dma((3, PLANE_SEMS)), dma((2,)), dma((2,)),
            dma((3, 8)), dma((3, 8)), dma((2, 16)), dma((2, 16)), dma((5,)),
        ],
        compiler_params=pltpu.CompilerParams(
            collective_id=2, has_side_effects=True, vmem_limit_bytes=62 * 2**20
        ),
    )(*args)


def segment_bounds(lengths, offsets):
    ends = jnp.cumsum(lengths)
    starts = ends - lengths
    segment = jnp.sum((offsets[:, None] >= ends[None, :]).astype(jnp.int32), axis=1)
    seg_ids = np.arange(13)
    branch_of = jnp.asarray(np.where(seg_ids > 0, 1 + 3 * ((seg_ids - 1) // 3), 0), jnp.int32)
    onehot = segment[:, None] == jnp.asarray(seg_ids, jnp.int32)[None, :]

    def pick(values):
        return jnp.sum(jnp.where(onehot, values[None, :], 0), axis=1)

    table = np.zeros((13, 13), np.int32)
    for s in range(13):
        if s:
            table[s, 1 + 3 * ((s - 1) // 3)] = 1
        else:
            table[s, 0] = 1
    table = jnp.asarray(table)
    b0 = jnp.sum(table * starts[None, :], axis=1)
    b1 = jnp.sum(table * ends[None, :], axis=1)
    is_leaf = jnp.asarray((seg_ids > 0) & ((seg_ids - 1) % 3 > 0), jnp.int32)
    depth = jnp.where(jnp.asarray(seg_ids > 0), lengths[0], 0) + is_leaf * (b1 - b0)
    position = offsets - pick(starts) + pick(depth)
    trunk = jnp.broadcast_to(lengths[0], offsets.shape)
    return jnp.stack([offsets, trunk, pick(starts), pick(b0), pick(b1)], axis=1), position


def shards(tokens, cotangent, tree_lengths, gain_attn, w_qkv, w_out, gain_mlp, w_gate, w_up, w_down):
    at = Place()
    swapped = lax.ppermute(tree_lengths, "fsdp", [(f, f ^ 1) for f in range(16)])
    lengths = jnp.where(at.k == 0, jnp.stack([tree_lengths[0], swapped[0]]), jnp.stack([swapped[0], tree_lengths[0]]))
    offsets = (
        (2 * jnp.arange(4, dtype=jnp.int32)[:, None] + at.zl) * 128 + jnp.arange(128, dtype=jnp.int32)[None, :]
    ).reshape(512)
    b_a, p_a = segment_bounds(lengths[0], offsets)
    b_b, p_b = segment_bounds(lengths[1], offsets)
    bounds = jnp.pad(jnp.stack([b_a.T, b_b.T]), ((0, 0), (0, 3), (0, 0)))
    position = jnp.stack([p_a, p_b]).astype(f32)
    frequency = 10000.0 ** (-2.0 * jnp.arange(32, dtype=f32) / 64)
    angles = position[:, None, :] * frequency[None, :, None]
    cosine, sine = jnp.cos(angles), jnp.sin(angles)

    gain1 = gain_attn.astype(f32)[:, None]
    gain2 = gain_mlp.astype(f32)[:, None]

    def columns(w, start, n, gain):
        return (lax.dynamic_slice_in_dim(w, start, n, axis=1).astype(f32) * gain).astype(bf16).T

    q_cols = columns(w_qkv, at.y * 512, 512, gain1)
    k_cols = columns(w_qkv, 2048 + at.y * 64, 64, gain1)
    v_cols = columns(w_qkv, 2304 + at.y * 64, 64, gain1)
    g_cols = columns(w_gate, at.y * 2 * FJ, 2 * FJ, gain2)
    u_cols = columns(w_up, at.y * 2 * FJ, 2 * FJ, gain2)
    wcol = jnp.stack(
        [
            jnp.concatenate(
                [q_cols[256 * i : 256 * i + 256], k_cols, v_cols, g_cols[FJ * i : FJ * i + FJ], u_cols[FJ * i : FJ * i + FJ]]
            )
            for i in range(2)
        ]
    )

    inputs = tokens.astype(f32)
    inv1 = lax.rsqrt(jnp.mean(inputs * inputs, axis=-1, keepdims=True) + epsilon)
    hat1 = (inputs * inv1).astype(bf16)
    hat_all, cot_all, w_all, q, kvb, att, lse, hidden, hat2_all = forward_pass(
        hat1, tokens, cotangent, wcol, w_out, w_down, cosine, sine, bounds
    )
    ghidden, gb_all, mixed_part, up_part, sum_g, sum_d = mlp_pass(hat2_all, cot_all, w_all, hidden, cotangent)
    mixed, grad_tokens, oq, og, ou, oo, od = backward_pass(
        gb_all, hat_all, w_all, q, kvb, att, lse, cosine, sine, bounds, tokens, hidden, ghidden, mixed_part, up_part, sum_g, sum_d
    )
    kv_rows = oq[:, 256:].astype(f32).reshape(4, 2, 2, 64, 128).sum(axis=1)
    raw_qkv = jnp.concatenate(
        [oq[:, :256].astype(f32).reshape(2048, 128), kv_rows[:, 0].reshape(256, 128), kv_rows[:, 1].reshape(256, 128)]
    ).T
    raw_gate = og.reshape(FF, 128).T.astype(f32)
    raw_up = ou.reshape(FF, 128).T.astype(f32)
    grad_gain1 = jnp.sum(raw_qkv * w_qkv.astype(f32), axis=1)
    grad_gain2 = jnp.sum(raw_gate * w_gate.astype(f32) + raw_up * w_up.astype(f32), axis=1)
    return (
        mixed,
        grad_tokens,
        grad_gain1,
        raw_qkv * gain1,
        oo.astype(f32),
        grad_gain2,
        raw_gate * gain2,
        raw_up * gain2,
        od.astype(f32),
    )


def solution(mesh):
    row = P("fsdp", None)
    tok = P(("fsdp", "ctx"), None)
    vec = P("fsdp")
    return jax.shard_map(
        shards,
        mesh=mesh,
        in_specs=(tok, tok, row, vec, row, row, vec, row, row, row),
        out_specs=(tok, tok, vec, row, row, vec, row, row, row),
        check_vma=False,
    )
```

```python
import functools

import jax
import jax.numpy as jnp
import numpy as np
from jax import lax
from jax.experimental import pallas as pl
from jax.experimental.pallas import tpu as pltpu
from jax.sharding import PartitionSpec as P

D = 2048
FF = 5632
H = 32
KVH = 4
HD = 64
FJ = FF // 8
bf16 = jnp.bfloat16
f32 = jnp.float32
MESH = pl.DeviceIdType.MESH
epsilon = 1e-05
masked_score = -1e30
ANY = pl.BlockSpec(memory_space=pl.ANY)
VM = pl.BlockSpec(memory_space=pltpu.VMEM)


class Place:
    def __init__(self):
        fs = lax.axis_index("fsdp")
        ct = lax.axis_index("ctx")
        self.zh, self.x, self.k = fs // 8, (fs // 2) % 4, fs % 2
        self.y, self.zl = ct // 2, ct % 2
        self.z = 2 * self.zh + self.zl
        self.at = {a: [getattr(self, a)] + [(getattr(self, a) + r) % 4 for r in (1, 2, 3)] for a in ("x", "y", "z")}
        self.next = {(a, r): self.device(**{a: self.at[a][r % 4]}) for a in ("x", "y", "z") for r in (1, -1)}
        self.other = self.device(k=1 - self.k)
        self.pieces = [[self.piece_of(z, x) for x in self.at["x"]] for z in self.at["z"]]

    def device(self, z=None, x=None, k=None, y=None):
        z = self.z if z is None else z
        x = self.x if x is None else x
        k = self.k if k is None else k
        y = self.y if y is None else y
        return ((z // 2) * 8 + x * 2 + k, y * 2 + z % 2)

    def sibling(self):
        return self.other

    def along(self, axis, r):
        return self.next[axis, r]

    def piece_of(self, z, x):
        return (z // 2) * 8 + x * 2 + z % 2

    def piece(self, **r):
        return self.pieces[r.get("z", 0) % 4][r.get("x", 0) % 4]

    def moved(self, axis, r):
        return self.at[axis][r % 4]


def rcopy(src, dst, ssem, rsem, dev):
    return pltpu.make_async_remote_copy(
        src_ref=src, dst_ref=dst, send_sem=ssem, recv_sem=rsem, device_id=dev, device_id_type=MESH
    )


def greet(devices):
    bar = pltpu.get_barrier_semaphore()
    for dev in devices:
        pl.semaphore_signal(bar, inc=1, device_id=dev, device_id_type=MESH)


def await_greetings(count):
    pl.semaphore_wait(pltpu.get_barrier_semaphore(), count)


class RingGather:
    messages = 12

    def __init__(self, at, buf, ssem, rsem):
        self.at, self.buf, self.ssem, self.rsem = at, buf, ssem, rsem

    def half(self, r, h, k=None):
        k = self.at.k if k is None else k
        return self.buf.at[k * 4 + self.at.moved("y", r), pl.ds(64 * h, 64)]

    def copy(self, d, m, incoming):
        step = 1 - 2 * d
        h = d if m in (0, 2) else 1 - d
        back = (-step if m == 2 else 0) - (step if incoming else 0)
        ref = self.half(back, h)
        i = d * 3 + m
        return rcopy(ref, ref, self.ssem.at[i], self.rsem.at[i], self.at.along("y", step))

    def relay(self, i, incoming):
        k = 1 - self.at.k if incoming else self.at.k
        if i < 6:
            d, m = i // 3, i % 3
            step = 1 - 2 * d
            h = d if m in (0, 2) else 1 - d
            ref = self.half((-2 if m == 2 else -1) * step, h, k)
        else:
            ref = self.half(0, i - 6, k)
        return rcopy(ref, ref, self.ssem.at[6 + i], self.rsem.at[6 + i], self.at.sibling())

    def start(self):
        for m in (0, 1):
            for d in (0, 1):
                self.copy(d, m, False).start()
        for i in (6, 7):
            self.relay(i, False).start()

    def step(self, m):
        for d in (0, 1):
            self.copy(d, m, True).wait_recv()
            if m == 0:
                self.copy(d, 2, False).start()
            self.relay(d * 3 + m, False).start()

    def finish(self):
        for i in range(8):
            self.relay(i, True).wait_recv()
            self.relay(i, False).wait_send()
        for d in (0, 1):
            for m in range(3):
                self.copy(d, m, False).wait_send()


RING_SEMS = 14


class RingReduce:
    def __init__(self, at, part, sib, recv, ssem, rsem):
        self.at, self.part, self.sib, self.recv = at, part, sib, recv
        self.ssem, self.rsem = ssem, rsem

    def cross(self, r):
        y = self.at.moved("y", r)
        return rcopy(
            self.part.at[(1 - self.at.k) * 4 + y], self.sib.at[r], self.ssem.at[6 + r], self.rsem.at[6 + r], self.at.sibling()
        )

    def copy(self, d, m):
        step = 1 - 2 * d
        h = d if m in (0, 2) else 1 - d
        y = self.at.moved("y", 2 if m == 0 else step)
        i = d * 3 + m
        return rcopy(
            self.part.at[self.at.k * 4 + y, pl.ds(64 * h, 64)], self.recv.at[i], self.ssem.at[i], self.rsem.at[i], self.at.along("y", step)
        )

    def cross_all(self):
        for r in (2, 1, 3, 0):
            self.cross(r).start()

    def add(self, r, h, others):
        y = self.at.moved("y", r)

        @pl.loop(0, 4)
        def _(i):
            rows = pl.ds(pl.multiple_of(64 * h + i * 16, 16), 16)
            total = self.part[self.at.k * 4 + y, rows, :].astype(f32) + self.sib[r, rows, :].astype(f32)
            for o in others:
                total += self.recv[o, pl.ds(pl.multiple_of(i * 16, 16), 16), :].astype(f32)
            self.part[self.at.k * 4 + y, rows, :] = total.astype(bf16)

    def first(self):
        self.cross(2).wait_recv()
        for d in (0, 1):
            self.add(2, d, ())
            self.copy(d, 0).start()
        for d in (0, 1):
            r = 1 if d == 0 else 3
            self.cross(r).wait_recv()
            self.add(r, 1 - d, ())
            self.copy(d, 1).start()

    def second(self):
        for d in (0, 1):
            self.copy(d, 0).wait_recv()
            self.add(1 if d == 0 else 3, d, (d * 3,))
            self.copy(d, 2).start()

    def collect(self, emit):
        self.cross(0).wait_recv()
        for d in (0, 1):
            for m in (1, 2):
                self.copy(d, m).wait_recv()
        for h in range(2):
            left, right = (2, 4) if h == 0 else (1, 5)

            @pl.loop(0, 4)
            def _(i):
                rows = pl.ds(pl.multiple_of(64 * h + i * 16, 16), 16)
                here = pl.ds(pl.multiple_of(i * 16, 16), 16)
                total = self.part[self.at.k * 4 + self.at.y, rows, :].astype(f32) + self.sib[0, rows, :].astype(f32)
                total += self.recv[left, here, :].astype(f32) + self.recv[right, here, :].astype(f32)
                emit(rows, total)

    def finish(self):
        for r in range(4):
            self.cross(r).wait_send()
        for d in (0, 1):
            for m in range(3):
                self.copy(d, m).wait_send()


REDUCE_SEMS = 10


class PlaneReduce:
    def __init__(self, at, part, recv, first, second, ssem, rsem):
        self.at, self.part, self.recv = at, part, recv
        self.first, self.second, self.ssem, self.rsem = first, second, ssem, rsem
        self.rows = part.shape[1] // 2

    def piece(self, a, c):
        return self.at.piece(**{self.first: a, self.second: c})

    def half(self, h):
        return pl.ds(h * self.rows, self.rows)

    def copy(self, c, d, m):
        step = 1 - 2 * d
        h = d if m in (0, 2) else 1 - d
        r = 2 if m == 0 else step
        p = self.piece(r, c) if c < 4 else self.piece(0, r)
        i = c * 6 + d * 3 + m
        return rcopy(
            self.part.at[p, self.half(h)], self.recv.at[i], self.ssem.at[i], self.rsem.at[i],
            self.at.along(self.first if c < 4 else self.second, step),
        )

    def add(self, p, h, others):
        @pl.loop(0, self.rows // 32)
        def _(i):
            rows = pl.ds(pl.multiple_of(h * self.rows + i * 32, 32), 32)
            here = pl.ds(pl.multiple_of(i * 32, 32), 32)
            total = self.part[p, rows, :].astype(f32)
            for o in others:
                total += self.recv[o, here, :].astype(f32)
            self.part[p, rows, :] = total.astype(bf16)

    def start(self, c):
        for m in (0, 1):
            for d in (0, 1):
                self.copy(c, d, m).start()

    def middle(self, c):
        for d in (0, 1):
            self.copy(c, d, 0).wait_recv()
            r = 1 - 2 * d
            p = self.piece(r, c) if c < 4 else self.piece(0, r)
            self.add(p, d, (c * 6 + d * 3,))
            self.copy(c, d, 2).start()

    def end(self, c):
        for d in (0, 1):
            for m in (1, 2):
                self.copy(c, d, m).wait_recv()
        p = self.piece(0, c) if c < 4 else self.piece(0, 0)
        self.add(p, 0, (c * 6 + 2, c * 6 + 4))
        self.add(p, 1, (c * 6 + 1, c * 6 + 5))

    def start_all(self):
        for c in (2, 1, 3, 0):
            self.start(c)

    def middle_all(self):
        for c in (2, 1, 3, 0):
            self.middle(c)

    def end_all(self):
        for c in (2, 1, 3, 0):
            self.end(c)
        self.start(4)

    def last(self):
        self.middle(4)
        self.end(4)

    def finish(self):
        for c in range(5):
            for d in (0, 1):
                for m in range(3):
                    self.copy(c, d, m).wait_send()


PLANE_SEMS = 30


class PlaneGather:
    def __init__(self, at, view, first, second, ssem, rsem):
        self.at, self.view, self.first, self.second = at, view, first, second
        self.ssem, self.rsem = ssem, rsem

    def copy(self, c, d, m, incoming):
        step = 1 - 2 * d
        h = d if m in (0, 2) else 1 - d
        back = (-step if m == 2 else 0) - (step if incoming else 0)
        a, b = (back, 0) if c == 4 else (c, back)
        p = self.at.piece(**{self.first: a, self.second: b})
        ref = self.view(p, h)
        i = c * 6 + d * 3 + m
        axis = self.first if c == 4 else self.second
        return rcopy(ref, ref, self.ssem.at[i], self.rsem.at[i], self.at.along(axis, step))

    def start(self, c):
        for m in (0, 1):
            for d in (0, 1):
                self.copy(c, d, m, False).start()

    def middle(self, c):
        for d in (0, 1):
            self.copy(c, d, 0, True).wait_recv()
            self.copy(c, d, 2, False).start()

    def arrive(self, c, m):
        for d in (0, 1):
            self.copy(c, d, m, True).wait_recv()

    def step0(self):
        self.start(4)
        self.start(0)

    def step1(self):
        self.middle(4)
        self.arrive(4, 1)
        self.start(3)
        self.start(1)

    def step2(self):
        self.middle(0)
        self.arrive(4, 2)
        self.start(2)

    def step3(self):
        for c in (3, 1, 2):
            self.middle(c)

    def step4(self):
        for c in range(4):
            self.arrive(c, 1)
            self.arrive(c, 2)
        for c in range(5):
            for d in (0, 1):
                for m in range(3):
                    self.copy(c, d, m, False).wait_send()


def dot_nt(a, b):
    return lax.dot_general(a, b, (((1,), (1,)), ((), ())), preferred_element_type=f32)


def dot_nn(a, b):
    return lax.dot_general(a, b, (((1,), (0,)), ((), ())), preferred_element_type=f32)


def dot_tn(a, b):
    return lax.dot_general(a, b, (((0,), (0,)), ((), ())), preferred_element_type=f32)


Q0, O0, G0, U0, D0, ROWS = 0, 384, 640, 1344, 2048, 2752
SCALE = HD**-0.5


def rotate(u, cosine, sine, sign):
    a, b = u[:32], u[32:]
    s = sine * sign
    return jnp.concatenate([a * cosine - b * s, b * cosine + a * s], axis=0)


def mask_bias(bounds, n):
    key = lax.broadcasted_iota(jnp.int32, (n, 128), 0)
    own, trunk, start, b0, b1 = [bounds[i : i + 1, :] for i in range(5)]
    keep = (key <= own) & ((key < trunk) | (key >= start) | ((key >= b0) & (key < b1)))
    return jnp.where(keep, 0.0, masked_score)


def heads_side_by_side(ref, t, y):
    return jnp.concatenate([ref[t, 64 * h : 64 * h + 64, 128 * y : 128 * y + 128] for h in range(4)], axis=1)


def tree_keys(kvb, kvt, kvn, t):
    for y in range(4):
        for z in range(2):
            b = 2 * y + z
            blk = kvb[t, y, z]
            kvt[:, 128 * b : 128 * b + 128] = blk
            kvn[128 * b : 128 * b + 128, :] = blk.astype(f32).T.astype(bf16)


def forward_kernel(
    hat, x, cot, wcol, wo, wd, cosine, sine, bounds,
    hat_out, cot_all, w_all, q_out, kvb, att, lse, hidden, hat2_all,
    hat_all, wqo, part, sib, recv, kvt, kvn, own2,
    hsem_s, hsem_r, csem_s, csem_r, gsem_s, gsem_r, psem_s, psem_r, rsem_s, rsem_r,
    colsem_s, colsem_r, rowsem_s, rowsem_r, kvsem_s, kvsem_r, lsem,
):
    at = Place()
    k, y, zl = at.k, at.y, at.zl
    own8 = at.zh * 4 + at.x
    is_src = own8 // 2 == y
    kd = at.x % 2
    both = jnp.where(is_src & (kd == k), 1, 0)
    src_n = jnp.where(is_src, 1, 0)
    j = 2 * y + k
    jz, jx = (j // 4) * 2 + zl, j % 4
    zpeer = at.device(z=at.z + 1 - 2 * zl)

    own = k * 4 + y
    piece = at.piece()
    lanes = pl.ds(pl.multiple_of(piece * 128, 128), 128)
    h_in = pltpu.make_async_copy(hat, hat_all.at[own], lsem.at[0])
    c_in = pltpu.make_async_copy(cot, cot_all.at[own], lsem.at[1])
    h_in.start()
    c_in.start()

    greet([at.sibling()] + [at.along(a, r) for a in ("x", "z", "y") for r in (1, -1)])
    for s in range(2):
        mine = (jz == at.z) & (jx == at.x) & (k == s)

        @pl.when(jnp.logical_not(mine))
        def _():
            greet([at.device(z=jz, x=jx, k=s)])

    def row_dest(t):
        q = (own8 + t) % 8
        z = (q // 4) * 2 + zl
        return at.device(z=z, x=q % 4, k=kd), at.piece_of(z, q % 4)

    @pl.when(is_src)
    def _():
        for t in range(8):
            dev, _ = row_dest(t)
            if t == 0:

                @pl.when(kd != k)
                def _():
                    greet([dev])
            else:
                greet([dev])

    await_greetings(7 + (2 - both) + src_n * 8 - both * src_n)

    ring_h = RingGather(at, hat_all, hsem_s, hsem_r)
    ring_c = RingGather(at, cot_all, csem_s, csem_r)
    ring_2 = RingGather(at, hat2_all, gsem_s, gsem_r)
    red = RingReduce(at, part, sib, recv, rsem_s, rsem_r)

    cols = ((0, 384, wqo, Q0), (384, 1408, w_all, G0))
    rows = ((wo, wqo, O0, 128), (wd, w_all, D0, 352))

    def col_send(i):
        s0, n, dst, d0 = cols[i]
        return rcopy(
            wcol.at[1 - k, pl.ds(s0, n)], dst.at[pl.ds(d0, n), lanes], colsem_s.at[i], colsem_r.at[i], at.sibling()
        )

    def col_keep(i):
        s0, n, dst, d0 = cols[i]
        return pltpu.make_async_copy(wcol.at[k, pl.ds(s0, n)], dst.at[pl.ds(d0, n), lanes], colsem_r.at[i])

    def row_send(i, t):
        src, dst, d0, n = rows[i]
        dev, p = row_dest(t)
        there = pl.ds(pl.multiple_of(p * 128, 128), 128)
        return rcopy(
            src.at[:, there], dst.at[pl.ds(pl.multiple_of(d0 + k * n, 16), n), there],
            rowsem_s.at[i, t], rowsem_r.at[i, k], dev,
        )

    def row_keep(i):
        src, dst, d0, n = rows[i]
        return pltpu.make_async_copy(
            src.at[:, lanes], dst.at[pl.ds(pl.multiple_of(d0 + k * n, 16), n), lanes], rowsem_r.at[i, k]
        )

    def row_in(i, s):
        src, dst, d0, n = rows[i]
        there = dst.at[pl.ds(d0 + s * n, n), lanes]
        return rcopy(there, there, rowsem_s.at[i, s], rowsem_r.at[i, s], at.device(z=jz, x=jx, k=s))

    @pl.when(k == zl)
    def _():
        for i in range(2):
            col_send(i).start()
            col_keep(i).start()

    h_in.wait()
    ring_h.start()

    @pl.when(is_src)
    def _():
        for i in range(2):
            for t in range(1, 8):
                row_send(i, t).start()

            @pl.when(kd == k)
            def _():
                row_keep(i).start()

            @pl.when(kd != k)
            def _():
                row_send(i, 0).start()

    def view(ref, r0, n):
        return lambda p, h: ref.at[pl.ds(r0 + h * (n // 2), n // 2), pl.ds(pl.multiple_of(p * 128, 128), 128)]

    planes = [
        PlaneGather(at, view(ref, r0, n), *order, psem_s.at[i], psem_r.at[i])
        for i, (ref, r0, n, order) in enumerate(
            (
                (wqo, Q0, 384, ("x", "z")),
                (wqo, O0, 256, ("z", "x")),
                (w_all, G0, 704, ("x", "z")),
                (w_all, U0, 704, ("z", "x")),
                (w_all, D0, 352, ("x", "z")),
                (w_all, D0 + 352, 352, ("z", "x")),
            )
        )
    ]
    pq, po = planes[:2]
    bulk = planes[2:]
    col_keep(0).wait()
    pq.step0()
    for s in range(2):
        row_in(0, s).wait_recv()
    po.step0()
    ring_h.step(0)
    pq.step1()
    po.step1()
    ring_h.step(1)
    pq.step2()
    po.step2()
    col_keep(1).wait()
    for p in bulk[:2]:
        p.step0()
    for s in range(2):
        row_in(1, s).wait_recv()
    for p in bulk[2:]:
        p.step0()
    pq.step3()
    po.step3()
    ring_h.step(2)
    ring_h.finish()
    c_in.wait()
    ring_c.start()
    pq.step4()

    def project(t, c):
        h = hat_all[pl.ds(4 * t + 2 * c, 2)].reshape(256, D)
        proj = dot_nt(wqo[Q0 : Q0 + 384, :], h)
        col = pl.ds(pl.multiple_of(256 * c, 256), 256)
        co, si = cosine[t, :, col], sine[t, :, col]
        for head in range(4):
            u = rotate(proj[64 * head : 64 * head + 64], co, si, 1.0)
            q_out[t, 64 * head : 64 * head + 64, col] = (u * SCALE).astype(bf16)
        kv = jnp.concatenate([rotate(proj[256:320], co, si, 1.0), proj[320:]], axis=0).astype(bf16)
        for b in range(2):
            kvb[t, 2 * c + b, zl] = kv[:, 128 * b : 128 * b + 128]

    def kv_send():
        ref = kvb.at[k, :, zl]
        return rcopy(ref, ref, kvsem_s.at[0], kvsem_r.at[0], zpeer)

    def kv_in():
        ref = kvb.at[k, :, 1 - zl]
        return rcopy(ref, ref, kvsem_s.at[0], kvsem_r.at[0], zpeer)

    def kv_relay(kk):
        ref = kvb.at[kk, :, 1 - zl]
        return rcopy(ref, ref, kvsem_s.at[1], kvsem_r.at[1], at.sibling())

    pl.loop(0, 2)(functools.partial(project, k))
    kv_send().start()
    pl.loop(0, 2)(functools.partial(project, 1 - k))
    h_out = pltpu.make_async_copy(hat_all, hat_out, lsem.at[0])
    h_out.start()
    ring_c.step(0)
    kv_in().wait_recv()
    kv_relay(k).start()
    for p in bulk:
        p.step1()
    po.step4()
    w_out_copy = pltpu.make_async_copy(wqo, w_all.at[pl.ds(0, G0)], lsem.at[2])
    w_out_copy.start()
    kv_relay(1 - k).wait_recv()

    def attend(t):
        tree_keys(kvb, kvt, kvn, t)
        for b in range(4):
            n = 256 * (b + 1)
            col = slice(128 * b, 128 * b + 128)
            qs = heads_side_by_side(q_out, t, b)
            qs = jnp.concatenate([qs, jnp.zeros_like(qs)], axis=0)
            bias = mask_bias(bounds[t, :, col], n)
            s = dot_nn(kvn[:n, :], qs) + jnp.concatenate([bias] * 4, axis=1)
            peak = jnp.max(s, axis=0, keepdims=True)
            e = jnp.exp(s - peak)
            total = jnp.sum(e, axis=0, keepdims=True)
            o = dot_nn(kvt[64:128, :n], e.astype(bf16)) / total
            log_total = peak + jnp.log(total)
            for head in range(4):
                c = slice(128 * head, 128 * head + 128)
                att[t, 64 * head : 64 * head + 64, col] = o[:, c].astype(bf16)
                lse[t, head : head + 1, col] = log_total[:, c]

        @pl.loop(0, 2)
        def _(i):
            a = att[t, :, pl.ds(pl.multiple_of(256 * i, 256), 256)]
            r = dot_tn(a, wqo[O0 : O0 + 256, :]).astype(bf16)
            part[pl.ds(4 * t + 2 * i, 2)] = r.reshape(2, 128, D)

    attend(1 - k)
    red.cross_all()
    ring_c.step(1)
    attend(k)
    red.first()
    for p in bulk:
        p.step2()
    ring_c.step(2)
    red.second()
    for p in bulk:
        p.step3()

    def emit(rows, total):
        h = x[rows, :].astype(f32) + total
        hidden[rows, :] = h
        inv = lax.rsqrt(jnp.mean(h * h, axis=1, keepdims=True) + epsilon)
        own2[rows, :] = (h * inv).astype(bf16)

    red.collect(emit)
    two_in = pltpu.make_async_copy(own2, hat2_all.at[own], lsem.at[3])
    two_in.start()
    two_in.wait()
    ring_2.start()
    ring_c.finish()
    ring_2.step(0)
    ring_2.step(1)
    for p in bulk[:2]:
        p.step4()
    ring_2.step(2)
    for p in bulk[2:]:
        p.step4()
    ring_2.finish()
    red.finish()
    h_out.wait()
    w_out_copy.wait()
    kv_send().wait_send()
    kv_relay(k).wait_send()

    @pl.when(k == zl)
    def _():
        for i in range(2):
            col_send(i).wait_send()

    @pl.when(is_src)
    def _():
        for i in range(2):
            for t in range(1, 8):
                row_send(i, t).wait_send()

            @pl.when(kd != k)
            def _():
                row_send(i, 0).wait_send()


def forward_pass(hat, x, cot, wcol, wo, wd, cosine, sine, bounds):
    shape = jax.ShapeDtypeStruct
    dma = pltpu.SemaphoreType.DMA
    return pl.pallas_call(
        forward_kernel,
        name="forward_pass",
        out_shape=(
            shape((8, 128, D), bf16),
            shape((8, 128, D), bf16),
            shape((ROWS, D), bf16),
            shape((2, 256, 512), bf16),
            shape((2, 4, 2, 128, 128), bf16),
            shape((2, 256, 512), bf16),
            shape((2, 8, 512), f32),
            shape((128, D), f32),
            shape((8, 128, D), bf16),
        ),
        in_specs=[VM, VM, ANY, ANY, ANY, ANY, VM, VM, VM],
        out_specs=[ANY, ANY, ANY, VM, VM, VM, VM, VM, ANY],
        scratch_shapes=[
            pltpu.VMEM((8, 128, D), bf16),
            pltpu.VMEM((G0, D), bf16),
            pltpu.VMEM((8, 128, D), bf16),
            pltpu.VMEM((4, 128, D), bf16),
            pltpu.VMEM((6, 64, D), bf16),
            pltpu.VMEM((128, 1024), bf16),
            pltpu.VMEM((1024, 128), bf16),
            pltpu.VMEM((128, D), bf16),
        ]
        + [dma((RING_SEMS,))] * 6
        + [dma((6, PLANE_SEMS))] * 2
        + [dma((REDUCE_SEMS,))] * 2
        + [dma((2,)), dma((2,)), dma((2, 8)), dma((2, 2)), dma((2,)), dma((2,)), dma((4,))],
        compiler_params=pltpu.CompilerParams(
            collective_id=0, has_side_effects=True, vmem_limit_bytes=56 * 2**20
        ),
    )(hat, x, cot, wcol, wo, wd, cosine, sine, bounds)


def mlp_kernel(
    hat2_hbm, cot_hbm, w_hbm, hidden, cot,
    mixed, ghidden, gb_all, up_part, sum_g, sum_d,
    hat2, cotv, wgu, wdn, part, sib, recv, innert, dgu, pd, pg, pu, precv_d, precv_g, own_gb, mpart, msib, mrecv,
    rsem_s, rsem_r, msem_s, msem_r, gsem_s, gsem_r, psem_s, psem_r, lsem,
):
    at = Place()
    k, y = at.k, at.y
    loads = [
        pltpu.make_async_copy(src, dst, lsem.at[i])
        for i, (src, dst) in enumerate(
            (
                (w_hbm.at[pl.ds(G0, 1408)], wgu),
                (hat2_hbm, hat2),
                (w_hbm.at[pl.ds(D0, 704)], wdn),
                (cot_hbm, cotv),
            )
        )
    ]
    for c in loads:
        c.start()
    greet([at.sibling()] + [at.along(a, r) for a in ("x", "z", "y") for r in (1, -1)])
    await_greetings(7)
    red = RingReduce(at, part, sib, recv, rsem_s, rsem_r)
    redm = RingReduce(at, mpart, msib, mrecv, msem_s, msem_r)
    ring = RingGather(at, gb_all, gsem_s, gsem_r)
    pr_d = PlaneReduce(at, pd, precv_d, "x", "z", psem_s.at[0], psem_r.at[0])
    pr_g = PlaneReduce(at, pg, precv_g, "z", "x", psem_s.at[1], psem_r.at[1])
    def columns(t, i):
        slot = 4 * t + 2 * i
        return slot, pl.ds(pl.multiple_of(slot * 128, 256), 256)

    loads[0].wait()
    loads[1].wait()

    @pl.loop(0, 4)
    def _(i):
        slot, cols = columns(0, i)
        both = dot_nt(wgu[...], hat2[pl.ds(slot, 2)].reshape(256, D))
        gate, up = both[:FJ], both[FJ:]
        sig = jax.nn.sigmoid(gate)
        silu = gate * sig
        innert[:, cols] = (silu * up).astype(bf16)
        dgu[:FJ, cols] = (up * sig * (1.0 + gate * (1.0 - sig))).astype(bf16)
        dgu[FJ:, cols] = silu.astype(bf16)

    loads[2].wait()
    loads[3].wait()

    def mix(t):
        @pl.loop(0, 2)
        def _(i):
            slot, cols = columns(t, i)
            r = dot_tn(innert[:, cols], wdn[...]).astype(bf16)
            mpart[pl.ds(slot, 2)] = r.reshape(2, 128, D)

    def mlp_back(t):
        @pl.loop(0, 2)
        def _(i):
            slot, cols = columns(t, i)
            gi = dot_nt(wdn[...], cotv[pl.ds(slot, 2)].reshape(256, D))
            dgu[:FJ, cols] = (gi * dgu[:FJ, cols].astype(f32)).astype(bf16)
            dgu[FJ:, cols] = (gi * dgu[FJ:, cols].astype(f32)).astype(bf16)

        @pl.loop(0, 2)
        def _(i):
            slot, cols = columns(t, i)
            r = dot_tn(dgu[:, cols], wgu[...]).astype(bf16)
            part[pl.ds(slot, 2)] = r.reshape(2, 128, D)

    def weight_grad(left, right, out):
        @pl.loop(0, 4)
        def _(i):
            cols = pl.ds(pl.multiple_of(512 * i, 512), 512)
            g = dot_nn(left[...], right[:, :, cols].reshape(1024, 512)).astype(bf16)
            for q in range(4):
                out[4 * i + q] = g[:, 128 * q : 128 * q + 128]

    mix(1 - k)
    redm.cross_all()
    mix(k)
    redm.first()
    mlp_back(1 - k)
    red.cross_all()
    redm.second()
    mlp_back(k)
    red.first()
    weight_grad(innert, cotv, pd)
    pr_d.start_all()
    red.second()

    def emit_mixed(rows, total):
        mixed[rows, :] = (hidden[rows, :] + total).astype(bf16)

    redm.collect(emit_mixed)
    weight_grad(dgu.at[:FJ], hat2, pg)
    pr_g.start_all()
    pr_d.middle_all()

    def emit(rows, total):
        h = hidden[rows, :]
        inv = lax.rsqrt(jnp.mean(h * h, axis=1, keepdims=True) + epsilon)
        hat = h * inv
        g = cot[rows, :].astype(f32) + inv * (total - hat * jnp.mean(total * hat, axis=1, keepdims=True))
        ghidden[rows, :] = g
        own_gb[rows, :] = g.astype(bf16)

    red.collect(emit)
    gb_in = pltpu.make_async_copy(own_gb, gb_all.at[k * 4 + y], lsem.at[0])
    gb_in.start()
    gb_in.wait()
    ring.start()
    pr_g.middle_all()

    ring.step(0)
    weight_grad(dgu.at[FJ:], hat2, pu)
    u_out = pltpu.make_async_copy(pu, up_part, lsem.at[4])
    u_out.start()
    ring.step(1)
    pr_d.end_all()
    pr_g.end_all()
    red.finish()
    ring.step(2)

    pr_d.last()
    d_out = pltpu.make_async_copy(pd.at[at.piece()], sum_d, lsem.at[2])
    d_out.start()
    pr_g.last()
    g_out = pltpu.make_async_copy(pg.at[at.piece()], sum_g, lsem.at[3])
    g_out.start()
    ring.finish()
    pr_d.finish()
    pr_g.finish()
    redm.finish()
    u_out.wait()
    d_out.wait()
    g_out.wait()


def mlp_pass(hat2_all, cot_all, w_all, hidden, cot):
    shape = jax.ShapeDtypeStruct
    dma = pltpu.SemaphoreType.DMA
    block = pltpu.VMEM((8, 128, D), bf16)
    return pl.pallas_call(
        mlp_kernel,
        name="mlp_pass",
        out_shape=(
            shape((128, D), bf16),
            shape((128, D), f32),
            shape((8, 128, D), bf16),
            shape((16, FJ, 128), bf16),
            shape((FJ, 128), bf16),
            shape((FJ, 128), bf16),
        ),
        in_specs=[ANY, ANY, ANY, VM, VM],
        out_specs=[VM, VM, ANY, ANY, ANY, ANY],
        scratch_shapes=[
            block, block,
            pltpu.VMEM((2 * FJ, D), bf16), pltpu.VMEM((FJ, D), bf16),
            block,
            pltpu.VMEM((4, 128, D), bf16),
            pltpu.VMEM((6, 64, D), bf16),
            pltpu.VMEM((FJ, 1024), bf16), pltpu.VMEM((2 * FJ, 1024), bf16),
            pltpu.VMEM((16, FJ, 128), bf16), pltpu.VMEM((16, FJ, 128), bf16), pltpu.VMEM((16, FJ, 128), bf16),
            pltpu.VMEM((30, FJ // 2, 128), bf16), pltpu.VMEM((30, FJ // 2, 128), bf16),
            pltpu.VMEM((128, D), bf16),
            block, pltpu.VMEM((4, 128, D), bf16), pltpu.VMEM((6, 64, D), bf16),
            dma((REDUCE_SEMS,)), dma((REDUCE_SEMS,)), dma((REDUCE_SEMS,)), dma((REDUCE_SEMS,)), dma((RING_SEMS,)), dma((RING_SEMS,)),
            dma((2, PLANE_SEMS)), dma((2, PLANE_SEMS)), dma((5,)),
        ],
        compiler_params=pltpu.CompilerParams(
            collective_id=1, has_side_effects=True, vmem_limit_bytes=62 * 2**20
        ),
    )(hat2_all, cot_all, w_all, hidden, cot)


class ColSpread:
    def __init__(self, at, src, dst, ssem, rsem):
        self.at, self.src, self.dst, self.ssem, self.rsem = at, src, dst, ssem, rsem
        self.home = at.k == at.zl
        self.there = dst.at[2 * at.y + at.k]

    def near(self):
        return rcopy(self.src, self.there, self.ssem.at[6], self.rsem.at[6 + self.at.k], self.at.sibling())

    def far(self):
        at = self.at
        dev = at.device(z=at.z + 1 - 2 * at.zl, k=at.zl)
        return rcopy(self.src, self.there, self.ssem.at[7], self.rsem.at[6 + at.k], dev)

    def start(self):
        self.far().start()

        @pl.when(self.home)
        def _():
            pltpu.make_async_copy(self.src, self.there, self.rsem.at[6 + self.at.k]).start()

        @pl.when(jnp.logical_not(self.home))
        def _():
            self.near().start()

    def copy(self, d, m, incoming):
        step = 1 - 2 * d
        h = d if m in (0, 2) else 1 - d
        back = (-step if m == 2 else 0) - (step if incoming else 0)
        ref = self.dst.at[2 * self.at.moved("y", back) + h]
        i = d * 3 + m
        return rcopy(ref, ref, self.ssem.at[i], self.rsem.at[i], self.at.along("y", step))

    def ring(self):
        for h in range(2):
            pltpu.make_async_copy(self.src, self.dst.at[2 * self.at.y + h], self.rsem.at[6 + h]).wait()
        for m in (0, 1):
            for d in (0, 1):
                self.copy(d, m, False).start()

    def middle(self):
        for d in (0, 1):
            self.copy(d, 0, True).wait_recv()
            self.copy(d, 2, False).start()

    def finish(self):
        for d in (0, 1):
            for m in (1, 2):
                self.copy(d, m, True).wait_recv()
        for d in (0, 1):
            for m in range(3):
                self.copy(d, m, False).wait_send()
        self.far().wait_send()

        @pl.when(jnp.logical_not(self.home))
        def _():
            self.near().wait_send()


class RowSpread:
    def __init__(self, at, src, buf, dst, ssem, rsem):
        self.at, self.src, self.buf, self.dst, self.ssem, self.rsem = at, src, buf, dst, ssem, rsem
        self.m = dst.shape[0]
        self.lanes = pl.ds(pl.multiple_of(at.piece() * 128, 128), 128)

    def keep(self, h):
        return pltpu.make_async_copy(self.src.at[pl.ds(h * self.m, self.m)], self.buf.at[self.at.y, h], self.ssem.at[6 + h])

    def start(self):
        for h in range(2):
            self.keep(h).start()
        for m in (0, 1):
            for d in (0, 1):
                self.copy(d, m, False).start()

    def copy(self, d, m, incoming):
        step = 1 - 2 * d
        h = d if m in (0, 2) else 1 - d
        back = (-step if m == 2 else 0) - (step if incoming else 0)
        ref = self.buf.at[self.at.moved("y", back), h]
        i = d * 3 + m
        src = ref if incoming or m == 2 else self.src.at[pl.ds(h * self.m, self.m)]
        return rcopy(src, ref, self.ssem.at[i], self.rsem.at[i], self.at.along("y", step))

    def middle(self):
        for d in (0, 1):
            self.copy(d, 0, True).wait_recv()
            self.copy(d, 2, False).start()

    def each(self, f, g):
        at = self.at
        for y in range(4):
            for dz in (1, 0):
                for c in range(2):
                    if dz:
                        f(y, dz, c)
                    else:
                        mine = (at.zh == y // 2) & (at.x == 2 * (y % 2) + at.k) & (at.k == c)
                        pl.when(mine)(functools.partial(g, y, c))
                        pl.when(jnp.logical_not(mine))(functools.partial(f, y, dz, c))

    def device(self, y, dz, c):
        at = self.at
        return at.device(z=2 * (y // 2) + (at.zl + dz) % 2, x=2 * (y % 2) + at.k, k=c)

    def push_copy(self, y, dz, c):
        return rcopy(
            self.buf.at[y, c], self.dst.at[:, self.lanes], self.ssem.at[8 + (y * 2 + dz) * 2 + c],
            self.rsem.at[6 + self.at.piece()], self.device(y, dz, c),
        )

    def push(self):
        for h in range(2):
            self.keep(h).wait()
        for d in (0, 1):
            for m in (1, 2):
                self.copy(d, m, True).wait_recv()

        def local(y, c):
            pltpu.make_async_copy(
                self.buf.at[y, c], self.dst.at[:, self.lanes], self.rsem.at[6 + self.at.piece()]
            ).start()

        self.each(lambda y, dz, c: self.push_copy(y, dz, c).start(), local)

    def finish(self):
        for p in range(16):
            pltpu.make_async_copy(self.buf.at[0, 0], self.dst.at[:, pl.ds(p * 128, 128)], self.rsem.at[6 + p]).wait()
        for d in (0, 1):
            for m in range(3):
                self.copy(d, m, False).wait_send()
        self.each(lambda y, dz, c: self.push_copy(y, dz, c).wait_send(), lambda y, c: None)

    def greet(self):
        at = self.at
        self.each(lambda y, dz, c: greet([self.device(y, dz, c)]), lambda y, c: None)
        for p in range(16):
            z, x = (p // 8) * 2 + p % 2, (p // 2) % 4
            mine = (at.z == z) & (at.x == x) & (at.k == at.x % 2)

            @pl.when(jnp.logical_not(mine))
            def _():
                greet([at.device(z=z, x=x, k=at.x % 2)])

        return 2 * (16 - jnp.where(at.x % 2 == at.k, 1, 0))


def backward_kernel(
    gb_hbm, hat_hbm, w_hbm, q, kvb, att, lse, cosine, sine, bounds, x, ghidden, up_part, sum_g, sum_d,
    grad_tokens, out_q, out_g, out_u, out_o, out_d, buf_o, buf_d,
    gb, hat, wqo, pu, pq, po, precv_u, precv_q, precv_o, part, sib, recv,
    datt, dproj, dkv, dkv_far, dkv_got, kvt, kvn,
    rsem_s, rsem_r, psem_s, psem_r, xsem_s, xsem_r, csem_s, csem_r, wsem_s, wsem_r, lsem,
):
    at = Place()
    k, y, zl = at.k, at.y, at.zl
    zpeer = at.device(z=at.z + 1 - 2 * zl)
    loads = [
        pltpu.make_async_copy(src, dst, lsem.at[i])
        for i, (src, dst) in enumerate(
            (
                (w_hbm.at[pl.ds(0, G0)], wqo),
                (gb_hbm, gb),
                (up_part, pu),
                (hat_hbm, hat),
            )
        )
    ]
    for c in loads:
        c.start()
    cols_q = ColSpread(at, pq.at[at.piece()], out_q, csem_s.at[0], csem_r.at[0])
    cols_g = ColSpread(at, sum_g, out_g, csem_s.at[1], csem_r.at[1])
    cols_u = ColSpread(at, pu.at[at.piece()], out_u, csem_s.at[2], csem_r.at[2])
    rows_o = RowSpread(at, po.at[at.piece()], buf_o, out_o, wsem_s.at[0], wsem_r.at[0])
    rows_d = RowSpread(at, sum_d, buf_d, out_d, wsem_s.at[1], wsem_r.at[1])
    greet([at.sibling(), at.device(z=at.z + 1 - 2 * zl, k=1 - k)])
    greet([at.along(a, r) for a in ("x", "z", "y") for r in (1, -1)])
    await_greetings(8 + rows_o.greet())

    red = RingReduce(at, part, sib, recv, rsem_s, rsem_r)
    pr_u = PlaneReduce(at, pu, precv_u, "x", "z", psem_s.at[0], psem_r.at[0])
    pr_q = PlaneReduce(at, pq, precv_q, "z", "x", psem_s.at[1], psem_r.at[1])
    pr_o = PlaneReduce(at, po, precv_o, "z", "x", psem_s.at[2], psem_r.at[2])
    cols_g.start()
    rows_d.start()
    loads[2].wait()
    pr_u.start_all()
    loads[0].wait()
    loads[1].wait()

    @pl.loop(0, 4)
    def _(i):
        g = gb[pl.ds(2 * i, 2)].reshape(256, D)
        r = dot_nt(wqo[O0 : O0 + 256, :], g)
        datt[i // 2, :, pl.ds(pl.multiple_of(256 * (i % 2), 256), 256)] = r.astype(bf16)

    cols_g.ring()

    def weight_grad(left, right, ref):
        @pl.loop(0, 4)
        def _(i):
            cols = pl.ds(pl.multiple_of(512 * i, 512), 512)
            g = dot_nn(left[0], right[0:4, :, cols].reshape(512, 512))
            g += dot_nn(left[1], right[4:8, :, cols].reshape(512, 512))
            g = g.astype(bf16)
            for s in range(4):
                ref[4 * i + s] = g[:, 128 * s : 128 * s + 128]

    weight_grad(att, gb, po)
    pr_o.start_all()

    def attend(t):
        tree_keys(kvb, kvt, kvn, t)
        for b in (3, 2, 1, 0):
            n = 256 * (b + 1)
            col = slice(128 * b, 128 * b + 128)
            qs = heads_side_by_side(q, t, b)
            dos = heads_side_by_side(datt, t, b)
            zero = jnp.zeros_like(qs)
            bias = mask_bias(bounds[t, :, col], n)
            log_total = jnp.concatenate([lse[t, h : h + 1, col] for h in range(4)], axis=1)
            s = dot_nn(kvn[:n, :], jnp.concatenate([qs, zero], axis=0)) + jnp.concatenate([bias] * 4, axis=1)
            prob = jnp.exp(s - log_total)
            dprob = dot_nn(kvn[:n, :], jnp.concatenate([zero, dos], axis=0))
            inner = jnp.sum(prob * dprob, axis=0, keepdims=True)
            ds = (prob * (dprob - inner)).astype(bf16)
            dq = dot_nn(kvt[0:64, :n], ds) * SCALE
            co, si = cosine[t, :, col], sine[t, :, col]
            for h in range(4):
                u = rotate(dq[:, 128 * h : 128 * h + 128], co, si, -1.0)
                dproj[t, 64 * h : 64 * h + 64, col] = u.astype(bf16)
            dk = dot_nt(qs, ds)
            dv = dot_nt(dos, prob.astype(bf16))
            for c in range(2 * (b + 1)):
                blk = slice(128 * c, 128 * c + 128)
                if b == 3:
                    dkv[t, c // 2, c % 2, :64, :] = dk[:, blk]
                    dkv[t, c // 2, c % 2, 64:, :] = dv[:, blk]
                else:
                    dkv[t, c // 2, c % 2, :64, :] += dk[:, blk]
                    dkv[t, c // 2, c % 2, 64:, :] += dv[:, blk]
        for b in range(4):
            dkv_far[t, b] = dkv[t, b, 1 - zl].astype(bf16)

    def far_copy(t, s):
        return rcopy(dkv_far.at[t], dkv_got.at[t], xsem_s.at[s], xsem_r.at[s], zpeer)

    def project(t, s):
        far_copy(t, s).wait_recv()
        for b in range(4):
            col = slice(128 * b, 128 * b + 128)
            total = dkv[t, b, zl] + dkv_got[t, b].astype(f32)
            dk = rotate(total[:64], cosine[t, :, col], sine[t, :, col], -1.0)
            dproj[t, 256:320, col] = dk.astype(bf16)
            dproj[t, 320:384, col] = total[64:].astype(bf16)

        @pl.loop(0, 2)
        def _(i):
            a = dproj[t, :, pl.ds(pl.multiple_of(256 * i, 256), 256)]
            r = dot_tn(a, wqo[Q0 : Q0 + 384, :]).astype(bf16)
            part[pl.ds(4 * t + 2 * i, 2)] = r.reshape(2, 128, D)

    attend(1 - k)
    far_copy(1 - k, 0).start()
    rows_d.middle()
    pr_u.middle(2)
    pr_u.middle(1)
    attend(k)
    far_copy(k, 1).start()
    project(1 - k, 0)
    red.cross_all()
    pr_u.middle(3)
    pr_u.middle(0)
    project(k, 1)
    red.first()
    pr_o.middle_all()
    cols_g.middle()
    loads[3].wait()
    weight_grad(dproj, hat, pq)
    pr_q.start_all()
    red.second()
    pr_u.end_all()
    pr_o.end_all()
    rows_d.push()
    pr_q.middle_all()
    pr_u.last()
    cols_u.start()
    pr_o.last()
    rows_o.start()
    cols_u.ring()

    def emit(rows, total):
        h = x[rows, :].astype(f32)
        inv = lax.rsqrt(jnp.mean(h * h, axis=1, keepdims=True) + epsilon)
        hat1 = h * inv
        g = ghidden[rows, :] + inv * (total - hat1 * jnp.mean(total * hat1, axis=1, keepdims=True))
        grad_tokens[rows, :] = g

    pr_q.end_all()
    rows_o.middle()
    red.collect(emit)
    pr_q.last()
    cols_q.start()
    cols_u.middle()
    rows_o.push()
    cols_q.ring()
    cols_g.finish()
    rows_d.finish()
    cols_q.middle()
    cols_u.finish()
    rows_o.finish()
    cols_q.finish()
    for s, t in ((0, 1 - k), (1, k)):
        far_copy(t, s).wait_send()
    red.finish()
    pr_u.finish()
    pr_o.finish()
    pr_q.finish()


def backward_pass(*args):
    shape = jax.ShapeDtypeStruct
    dma = pltpu.SemaphoreType.DMA
    block = pltpu.VMEM((8, 128, D), bf16)
    return pl.pallas_call(
        backward_kernel,
        name="backward_pass",
        out_shape=(
            shape((128, D), f32),
            shape((8, 384, 128), bf16),
            shape((8, FJ, 128), bf16),
            shape((8, FJ, 128), bf16),
            shape((128, D), bf16),
            shape((352, D), bf16),
            shape((4, 2, 128, 128), bf16),
            shape((4, 2, 352, 128), bf16),
        ),
        in_specs=[ANY, ANY, ANY, VM, VM, VM, VM, VM, VM, VM, VM, VM, ANY, ANY, ANY],
        out_specs=[VM] + [ANY] * 7,
        scratch_shapes=[
            block, block, pltpu.VMEM((G0, D), bf16),
            pltpu.VMEM((16, FJ, 128), bf16), pltpu.VMEM((16, 384, 128), bf16), pltpu.VMEM((16, 256, 128), bf16),
            pltpu.VMEM((30, FJ // 2, 128), bf16), pltpu.VMEM((30, 192, 128), bf16), pltpu.VMEM((30, 128, 128), bf16),
            block, pltpu.VMEM((4, 128, D), bf16), pltpu.VMEM((6, 64, D), bf16),
            pltpu.VMEM((2, 256, 512), bf16),
            pltpu.VMEM((2, 384, 512), bf16),
            pltpu.VMEM((2, 4, 2, 128, 128), f32),
            pltpu.VMEM((2, 4, 128, 128), bf16),
            pltpu.VMEM((2, 4, 128, 128), bf16),
            pltpu.VMEM((128, 1024), bf16),
            pltpu.VMEM((1024, 128), bf16),
            dma((REDUCE_SEMS,)), dma((REDUCE_SEMS,)),
            dma((3, PLANE_SEMS)), dma((3, PLANE_SEMS)), dma((2,)), dma((2,)),
            dma((3, 8)), dma((3, 8)), dma((2, 24)), dma((2, 22)), dma((5,)),
        ],
        compiler_params=pltpu.CompilerParams(
            collective_id=2, has_side_effects=True, vmem_limit_bytes=62 * 2**20
        ),
    )(*args)


def finish_kernel(og, ou, rq, oo, od, wg, wu, wq, gain1, gain2, g_gate, g_up, g_qkv, g_out, g_down, s_one, s_two):
    i = pl.program_id(0)

    @pl.when(i == 0)
    def _():
        s_one[...] = jnp.zeros_like(s_one)
        s_two[...] = jnp.zeros_like(s_two)

    total = None
    for src, w, dst in ((og, wg, g_gate), (ou, wu, g_up)):
        raw = src[...].astype(f32).T
        dst[...] = raw * gain2[...]
        dot = jnp.sum(raw * w[...].astype(f32), axis=1, keepdims=True)
        total = dot if total is None else total + dot
    s_two[...] += total

    @pl.when(i < 5)
    def _():
        raw = rq[...].T
        g_qkv[...] = raw * gain1[...]
        s_one[...] += jnp.sum(raw * wq[...].astype(f32), axis=1, keepdims=True)

    g_out[...] = oo[...].astype(f32)
    g_down[...] = od[...].astype(f32)


def finish(og, ou, rq, oo, od, wg, wu, wq, gain1, gain2):
    shape = jax.ShapeDtypeStruct
    row = lambda i: (i, 0)
    col = lambda i: (0, i)
    whole = lambda i: (0, 0)
    q_col = lambda i: (0, jnp.minimum(i, 4))
    o_row = lambda i: (jnp.minimum(i, 7), 0)
    return pl.pallas_call(
        finish_kernel,
        name="finish",
        grid=(11,),
        out_shape=(
            shape((128, FF), f32), shape((128, FF), f32), shape((128, 2560), f32), shape((128, D), f32), shape((352, D), f32),
            shape((128, 1), f32), shape((128, 1), f32),
        ),
        in_specs=[
            pl.BlockSpec((512, 128), row),
            pl.BlockSpec((512, 128), row),
            pl.BlockSpec((512, 128), lambda i: (jnp.minimum(i, 4), 0)),
            pl.BlockSpec((16, D), o_row),
            pl.BlockSpec((32, D), row),
            pl.BlockSpec((128, 512), col),
            pl.BlockSpec((128, 512), col),
            pl.BlockSpec((128, 512), q_col),
            pl.BlockSpec((128, 1), whole),
            pl.BlockSpec((128, 1), whole),
        ],
        out_specs=(
            pl.BlockSpec((128, 512), col),
            pl.BlockSpec((128, 512), col),
            pl.BlockSpec((128, 512), q_col),
            pl.BlockSpec((16, D), o_row),
            pl.BlockSpec((32, D), row),
            pl.BlockSpec((128, 1), whole),
            pl.BlockSpec((128, 1), whole),
        ),
        compiler_params=pltpu.CompilerParams(vmem_limit_bytes=32 * 2**20),
    )(og, ou, rq, oo, od, wg, wu, wq, gain1, gain2)


def segment_bounds(lengths, offsets):
    ends = jnp.cumsum(lengths)
    starts = ends - lengths
    segment = jnp.sum((offsets[:, None] >= ends[None, :]).astype(jnp.int32), axis=1)
    seg_ids = np.arange(13)
    branch_of = jnp.asarray(np.where(seg_ids > 0, 1 + 3 * ((seg_ids - 1) // 3), 0), jnp.int32)
    onehot = segment[:, None] == jnp.asarray(seg_ids, jnp.int32)[None, :]

    def pick(values):
        return jnp.sum(jnp.where(onehot, values[None, :], 0), axis=1)

    table = np.zeros((13, 13), np.int32)
    for s in range(13):
        if s:
            table[s, 1 + 3 * ((s - 1) // 3)] = 1
        else:
            table[s, 0] = 1
    table = jnp.asarray(table)
    b0 = jnp.sum(table * starts[None, :], axis=1)
    b1 = jnp.sum(table * ends[None, :], axis=1)
    is_leaf = jnp.asarray((seg_ids > 0) & ((seg_ids - 1) % 3 > 0), jnp.int32)
    depth = jnp.where(jnp.asarray(seg_ids > 0), lengths[0], 0) + is_leaf * (b1 - b0)
    position = offsets - pick(starts) + pick(depth)
    trunk = jnp.broadcast_to(lengths[0], offsets.shape)
    return jnp.stack([offsets, trunk, pick(starts), pick(b0), pick(b1)], axis=1), position


def shards(tokens, cotangent, tree_lengths, gain_attn, w_qkv, w_out, gain_mlp, w_gate, w_up, w_down):
    at = Place()
    swapped = lax.ppermute(tree_lengths, "fsdp", [(f, f ^ 1) for f in range(16)])
    lengths = jnp.where(at.k == 0, jnp.stack([tree_lengths[0], swapped[0]]), jnp.stack([swapped[0], tree_lengths[0]]))
    offsets = (
        (2 * jnp.arange(4, dtype=jnp.int32)[:, None] + at.zl) * 128 + jnp.arange(128, dtype=jnp.int32)[None, :]
    ).reshape(512)
    b_a, p_a = segment_bounds(lengths[0], offsets)
    b_b, p_b = segment_bounds(lengths[1], offsets)
    bounds = jnp.pad(jnp.stack([b_a.T, b_b.T]), ((0, 0), (0, 3), (0, 0)))
    position = jnp.stack([p_a, p_b]).astype(f32)
    frequency = 10000.0 ** (-2.0 * jnp.arange(32, dtype=f32) / 64)
    angles = position[:, None, :] * frequency[None, :, None]
    cosine, sine = jnp.cos(angles), jnp.sin(angles)

    gain1 = gain_attn.astype(f32)[:, None]
    gain2 = gain_mlp.astype(f32)[:, None]

    def columns(w, start, n, gain):
        return (lax.dynamic_slice_in_dim(w, start, n, axis=1).astype(f32) * gain).astype(bf16).T

    q_cols = columns(w_qkv, at.y * 512, 512, gain1)
    k_cols = columns(w_qkv, 2048 + at.y * 64, 64, gain1)
    v_cols = columns(w_qkv, 2304 + at.y * 64, 64, gain1)
    g_cols = columns(w_gate, at.y * 2 * FJ, 2 * FJ, gain2)
    u_cols = columns(w_up, at.y * 2 * FJ, 2 * FJ, gain2)
    wcol = jnp.stack(
        [
            jnp.concatenate(
                [q_cols[256 * i : 256 * i + 256], k_cols, v_cols, g_cols[FJ * i : FJ * i + FJ], u_cols[FJ * i : FJ * i + FJ]]
            )
            for i in range(2)
        ]
    )

    inputs = tokens.astype(f32)
    inv1 = lax.rsqrt(jnp.mean(inputs * inputs, axis=-1, keepdims=True) + epsilon)
    hat1 = (inputs * inv1).astype(bf16)
    hat_all, cot_all, w_all, q, kvb, att, lse, hidden, hat2_all = forward_pass(
        hat1, tokens, cotangent, wcol, w_out, w_down, cosine, sine, bounds
    )
    mixed, ghidden, gb_all, up_part, sum_g, sum_d = mlp_pass(hat2_all, cot_all, w_all, hidden, cotangent)
    grad_tokens, oq, og, ou, oo, od, _, _ = backward_pass(
        gb_all, hat_all, w_all, q, kvb, att, lse, cosine, sine, bounds, tokens, ghidden, up_part, sum_g, sum_d
    )
    kv_rows = oq[:, 256:].astype(f32).reshape(4, 2, 2, 64, 128).sum(axis=1)
    raw_qkv = jnp.concatenate(
        [oq[:, :256].astype(f32).reshape(2048, 128), kv_rows[:, 0].reshape(256, 128), kv_rows[:, 1].reshape(256, 128)]
    )
    g_gate, g_up, g_qkv, g_out, g_down, grad_gain1, grad_gain2 = finish(
        og.reshape(FF, 128), ou.reshape(FF, 128), raw_qkv, oo, od, w_gate, w_up, w_qkv, gain1, gain2
    )
    return (mixed, grad_tokens, grad_gain1[:, 0], g_qkv, g_out, grad_gain2[:, 0], g_gate, g_up, g_down)


def solution(mesh):
    row = P("fsdp", None)
    tok = P(("fsdp", "ctx"), None)
    vec = P("fsdp")
    return jax.shard_map(
        shards,
        mesh=mesh,
        in_specs=(tok, tok, row, vec, row, row, vec, row, row, row),
        out_specs=(tok, tok, vec, row, row, vec, row, row, row),
        check_vma=False,
    )
```

```python
import functools

import jax
import jax.numpy as jnp
import numpy as np
from jax import lax
from jax.experimental import pallas as pl
from jax.experimental.pallas import tpu as pltpu
from jax.sharding import PartitionSpec as P

D = 2048
FF = 5632
H = 32
KVH = 4
HD = 64
FJ = FF // 8
bf16 = jnp.bfloat16
f32 = jnp.float32
MESH = pl.DeviceIdType.MESH
epsilon = 1e-05
masked_score = -1e30
ANY = pl.BlockSpec(memory_space=pl.ANY)
VM = pl.BlockSpec(memory_space=pltpu.VMEM)


class Place:
    def __init__(self):
        fs = lax.axis_index("fsdp")
        ct = lax.axis_index("ctx")
        self.zh, self.x, self.k = fs // 8, (fs // 2) % 4, fs % 2
        self.y, self.zl = ct // 2, ct % 2
        self.z = 2 * self.zh + self.zl
        self.at = {a: [getattr(self, a)] + [(getattr(self, a) + r) % 4 for r in (1, 2, 3)] for a in ("x", "y", "z")}
        self.next = {(a, r): self.device(**{a: self.at[a][r % 4]}) for a in ("x", "y", "z") for r in (1, -1)}
        self.other = self.device(k=1 - self.k)
        self.pieces = [[self.piece_of(z, x) for x in self.at["x"]] for z in self.at["z"]]

    def device(self, z=None, x=None, k=None, y=None):
        z = self.z if z is None else z
        x = self.x if x is None else x
        k = self.k if k is None else k
        y = self.y if y is None else y
        return ((z // 2) * 8 + x * 2 + k, y * 2 + z % 2)

    def sibling(self):
        return self.other

    def along(self, axis, r):
        return self.next[axis, r]

    def piece_of(self, z, x):
        return (z // 2) * 8 + x * 2 + z % 2

    def piece(self, **r):
        return self.pieces[r.get("z", 0) % 4][r.get("x", 0) % 4]

    def moved(self, axis, r):
        return self.at[axis][r % 4]


def rcopy(src, dst, ssem, rsem, dev):
    return pltpu.make_async_remote_copy(
        src_ref=src, dst_ref=dst, send_sem=ssem, recv_sem=rsem, device_id=dev, device_id_type=MESH
    )


def greet(devices):
    bar = pltpu.get_barrier_semaphore()
    for dev in devices:
        pl.semaphore_signal(bar, inc=1, device_id=dev, device_id_type=MESH)


def await_greetings(count):
    pl.semaphore_wait(pltpu.get_barrier_semaphore(), count)


class RingGather:
    messages = 12

    def __init__(self, at, own, buf, ssem, rsem, lsem):
        self.at, self.own, self.buf, self.ssem, self.rsem = at, own, buf, ssem, rsem
        self.keep = pltpu.make_async_copy(own, buf.at[at.k * 4 + at.y], lsem)

    def half(self, r, h, k=None):
        k = self.at.k if k is None else k
        return self.buf.at[k * 4 + self.at.moved("y", r), pl.ds(64 * h, 64)]

    def copy(self, d, m, incoming):
        step = 1 - 2 * d
        h = d if m in (0, 2) else 1 - d
        back = (-step if m == 2 else 0) - (step if incoming else 0)
        ref = self.half(back, h)
        i = d * 3 + m
        src = ref if incoming or m == 2 else self.own.at[pl.ds(64 * h, 64)]
        return rcopy(src, ref, self.ssem.at[i], self.rsem.at[i], self.at.along("y", step))

    def relay(self, i, incoming):
        k = 1 - self.at.k if incoming else self.at.k
        if i < 6:
            d, m = i // 3, i % 3
            step = 1 - 2 * d
            h = d if m in (0, 2) else 1 - d
            ref = self.half((-2 if m == 2 else -1) * step, h, k)
        else:
            ref = self.half(0, i - 6, k)
        src = ref if incoming or i < 6 else self.own.at[pl.ds(64 * (i - 6), 64)]
        return rcopy(src, ref, self.ssem.at[6 + i], self.rsem.at[6 + i], self.at.sibling())

    def start(self):
        for m in (0, 1):
            for d in (0, 1):
                self.copy(d, m, False).start()
        for i in (6, 7):
            self.relay(i, False).start()
        self.keep.start()

    def step(self, m):
        for d in (0, 1):
            self.copy(d, m, True).wait_recv()
            if m == 0:
                self.copy(d, 2, False).start()
            self.relay(d * 3 + m, False).start()

    def finish(self):
        self.keep.wait()
        for i in range(8):
            self.relay(i, True).wait_recv()
            self.relay(i, False).wait_send()
        for d in (0, 1):
            for m in range(3):
                self.copy(d, m, False).wait_send()


RING_SEMS = 14


class RingReduce:
    def __init__(self, at, part, sib, recv, ssem, rsem):
        self.at, self.part, self.sib, self.recv = at, part, sib, recv
        self.ssem, self.rsem = ssem, rsem

    def cross(self, r):
        y = self.at.moved("y", r)
        return rcopy(
            self.part.at[(1 - self.at.k) * 4 + y], self.sib.at[r], self.ssem.at[6 + r], self.rsem.at[6 + r], self.at.sibling()
        )

    def copy(self, d, m):
        step = 1 - 2 * d
        h = d if m in (0, 2) else 1 - d
        y = self.at.moved("y", 2 if m == 0 else step)
        i = d * 3 + m
        return rcopy(
            self.part.at[self.at.k * 4 + y, pl.ds(64 * h, 64)], self.recv.at[i], self.ssem.at[i], self.rsem.at[i], self.at.along("y", step)
        )

    def cross_all(self):
        for r in (2, 1, 3, 0):
            self.cross(r).start()

    def add(self, r, h, others):
        y = self.at.moved("y", r)

        @pl.loop(0, 4)
        def _(i):
            rows = pl.ds(pl.multiple_of(64 * h + i * 16, 16), 16)
            total = self.part[self.at.k * 4 + y, rows, :].astype(f32) + self.sib[r, rows, :].astype(f32)
            for o in others:
                total += self.recv[o, pl.ds(pl.multiple_of(i * 16, 16), 16), :].astype(f32)
            self.part[self.at.k * 4 + y, rows, :] = total.astype(bf16)

    def first(self):
        self.cross(2).wait_recv()
        for d in (0, 1):
            self.add(2, d, ())
            self.copy(d, 0).start()
        for d in (0, 1):
            r = 1 if d == 0 else 3
            self.cross(r).wait_recv()
            self.add(r, 1 - d, ())
            self.copy(d, 1).start()

    def second(self):
        for d in (0, 1):
            self.copy(d, 0).wait_recv()
            self.add(1 if d == 0 else 3, d, (d * 3,))
            self.copy(d, 2).start()

    def collect(self, emit):
        self.cross(0).wait_recv()
        for d in (0, 1):
            for m in (1, 2):
                self.copy(d, m).wait_recv()
        for h in range(2):
            left, right = (2, 4) if h == 0 else (1, 5)

            @pl.loop(0, 4)
            def _(i):
                rows = pl.ds(pl.multiple_of(64 * h + i * 16, 16), 16)
                here = pl.ds(pl.multiple_of(i * 16, 16), 16)
                total = self.part[self.at.k * 4 + self.at.y, rows, :].astype(f32) + self.sib[0, rows, :].astype(f32)
                total += self.recv[left, here, :].astype(f32) + self.recv[right, here, :].astype(f32)
                emit(rows, total)

    def finish(self):
        for r in range(4):
            self.cross(r).wait_send()
        for d in (0, 1):
            for m in range(3):
                self.copy(d, m).wait_send()


REDUCE_SEMS = 10


class PlaneReduce:
    def __init__(self, at, part, recv, first, second, ssem, rsem, base=0):
        self.at, self.part, self.recv, self.base = at, part, recv, base
        self.first, self.second, self.ssem, self.rsem = first, second, ssem, rsem
        self.rows = recv.shape[1]

    def piece(self, a, c):
        return self.at.piece(**{self.first: a, self.second: c})

    def half(self, h):
        return pl.ds(self.base + h * self.rows, self.rows)

    def copy(self, c, d, m):
        step = 1 - 2 * d
        h = d if m in (0, 2) else 1 - d
        r = 2 if m == 0 else step
        p = self.piece(r, c) if c < 4 else self.piece(0, r)
        i = c * 6 + d * 3 + m
        return rcopy(
            self.part.at[p, self.half(h)], self.recv.at[i], self.ssem.at[i], self.rsem.at[i],
            self.at.along(self.first if c < 4 else self.second, step),
        )

    def add(self, p, h, others):
        @pl.loop(0, self.rows // 32)
        def _(i):
            rows = pl.ds(pl.multiple_of(self.base + h * self.rows + i * 32, 32), 32)
            here = pl.ds(pl.multiple_of(i * 32, 32), 32)
            total = self.part[p, rows, :].astype(f32)
            for o in others:
                total += self.recv[o, here, :].astype(f32)
            self.part[p, rows, :] = total.astype(bf16)

    def start(self, c):
        for m in (0, 1):
            for d in (0, 1):
                self.copy(c, d, m).start()

    def middle(self, c):
        for d in (0, 1):
            self.copy(c, d, 0).wait_recv()
            r = 1 - 2 * d
            p = self.piece(r, c) if c < 4 else self.piece(0, r)
            self.add(p, d, (c * 6 + d * 3,))
            self.copy(c, d, 2).start()

    def end(self, c):
        for d in (0, 1):
            for m in (1, 2):
                self.copy(c, d, m).wait_recv()
        p = self.piece(0, c) if c < 4 else self.piece(0, 0)
        self.add(p, 0, (c * 6 + 2, c * 6 + 4))
        self.add(p, 1, (c * 6 + 1, c * 6 + 5))

    def start_all(self):
        for c in (2, 1, 3, 0):
            self.start(c)

    def middle_all(self):
        for c in (2, 1, 3, 0):
            self.middle(c)

    def end_all(self):
        for c in (2, 1, 3, 0):
            self.end(c)
        self.start(4)

    def last(self):
        self.middle(4)
        self.end(4)

    def finish(self):
        for c in range(5):
            for d in (0, 1):
                for m in range(3):
                    self.copy(c, d, m).wait_send()


PLANE_SEMS = 30


class PlaneGather:
    def __init__(self, at, view, first, second, ssem, rsem):
        self.at, self.view, self.first, self.second = at, view, first, second
        self.ssem, self.rsem = ssem, rsem

    def copy(self, c, d, m, incoming):
        step = 1 - 2 * d
        h = d if m in (0, 2) else 1 - d
        back = (-step if m == 2 else 0) - (step if incoming else 0)
        a, b = (back, 0) if c == 4 else (c, back)
        p = self.at.piece(**{self.first: a, self.second: b})
        ref = self.view(p, h)
        i = c * 6 + d * 3 + m
        axis = self.first if c == 4 else self.second
        return rcopy(ref, ref, self.ssem.at[i], self.rsem.at[i], self.at.along(axis, step))

    def start(self, c):
        for m in (0, 1):
            for d in (0, 1):
                self.copy(c, d, m, False).start()

    def middle(self, c):
        for d in (0, 1):
            self.copy(c, d, 0, True).wait_recv()
            self.copy(c, d, 2, False).start()

    def arrive(self, c, m):
        for d in (0, 1):
            self.copy(c, d, m, True).wait_recv()

    def step0(self):
        self.start(4)
        self.start(0)

    def step1(self):
        self.middle(4)
        self.arrive(4, 1)
        self.start(3)
        self.start(1)

    def step2(self):
        self.middle(0)
        self.arrive(4, 2)
        self.start(2)

    def step3(self):
        for c in (3, 1, 2):
            self.middle(c)

    def step4(self):
        for c in range(4):
            self.arrive(c, 1)
            self.arrive(c, 2)
        for c in range(5):
            for d in (0, 1):
                for m in range(3):
                    self.copy(c, d, m, False).wait_send()


def dot_nt(a, b):
    return lax.dot_general(a, b, (((1,), (1,)), ((), ())), preferred_element_type=f32)


def dot_nn(a, b):
    return lax.dot_general(a, b, (((1,), (0,)), ((), ())), preferred_element_type=f32)


def dot_tn(a, b):
    return lax.dot_general(a, b, (((0,), (0,)), ((), ())), preferred_element_type=f32)


Q0, O0, G0, U0, D0, ROWS = 0, 384, 640, 1344, 2048, 2752
SCALE = HD**-0.5


def rotate(u, cosine, sine, sign):
    a, b = u[:32], u[32:]
    s = sine * sign
    return jnp.concatenate([a * cosine - b * s, b * cosine + a * s], axis=0)


def mask_bias(bounds, n):
    key = lax.broadcasted_iota(jnp.int32, (n, 128), 0)
    own, trunk, start, b0, b1 = [bounds[i : i + 1, :] for i in range(5)]
    keep = (key <= own) & ((key < trunk) | (key >= start) | ((key >= b0) & (key < b1)))
    return jnp.where(keep, 0.0, masked_score)


def heads_side_by_side(ref, t, y):
    return jnp.concatenate([ref[t, 64 * h : 64 * h + 64, 128 * y : 128 * y + 128] for h in range(4)], axis=1)


def tree_keys(kvb, kvt, kvn, t):
    for y in range(4):
        for z in range(2):
            b = 2 * y + z
            blk = kvb[t, y, z]
            kvt[:, 128 * b : 128 * b + 128] = blk
            kvn[128 * b : 128 * b + 128, :] = blk.astype(f32).T.astype(bf16)


def forward_kernel(
    hat, x, cot, wcol, wo, wd, cosine, sine, bounds,
    hat_out, cot_all, w_all, q_out, kvb, att, lse, hidden, hat2_all,
    hat_all, wqo, part, sib, recv, kvt, kvn, own2,
    hsem_s, hsem_r, csem_s, csem_r, gsem_s, gsem_r, psem_s, psem_r, rsem_s, rsem_r,
    colsem_s, colsem_r, rowsem_s, rowsem_r, kvsem_s, kvsem_r, lsem,
):
    at = Place()
    k, y, zl = at.k, at.y, at.zl
    own8 = at.zh * 4 + at.x
    is_src = own8 // 2 == y
    kd = at.x % 2
    both = jnp.where(is_src & (kd == k), 1, 0)
    src_n = jnp.where(is_src, 1, 0)
    j = 2 * y + k
    jz, jx = (j // 4) * 2 + zl, j % 4
    zpeer = at.device(z=at.z + 1 - 2 * zl)

    piece = at.piece()
    lanes = pl.ds(pl.multiple_of(piece * 128, 128), 128)
    greet([at.sibling()] + [at.along(a, r) for a in ("x", "z", "y") for r in (1, -1)])
    for s in range(2):
        mine = (jz == at.z) & (jx == at.x) & (k == s)

        @pl.when(jnp.logical_not(mine))
        def _():
            greet([at.device(z=jz, x=jx, k=s)])

    def row_dest(t):
        q = (own8 + t) % 8
        z = (q // 4) * 2 + zl
        return at.device(z=z, x=q % 4, k=kd), at.piece_of(z, q % 4)

    @pl.when(is_src)
    def _():
        for t in range(8):
            dev, _ = row_dest(t)
            if t == 0:

                @pl.when(kd != k)
                def _():
                    greet([dev])
            else:
                greet([dev])

    await_greetings(7 + (2 - both) + src_n * 8 - both * src_n)

    ring_h = RingGather(at, hat, hat_all, hsem_s, hsem_r, lsem.at[0])
    ring_c = RingGather(at, cot, cot_all, csem_s, csem_r, lsem.at[1])
    ring_2 = RingGather(at, own2, hat2_all, gsem_s, gsem_r, lsem.at[3])
    red = RingReduce(at, part, sib, recv, rsem_s, rsem_r)

    cols = ((0, 384, wqo, Q0), (384, 1408, w_all, G0))
    rows = ((wo, wqo, O0, 128), (wd, w_all, D0, 352))

    def col_send(i):
        s0, n, dst, d0 = cols[i]
        return rcopy(
            wcol.at[1 - k, pl.ds(s0, n)], dst.at[pl.ds(d0, n), lanes], colsem_s.at[i], colsem_r.at[i], at.sibling()
        )

    def col_keep(i):
        s0, n, dst, d0 = cols[i]
        return pltpu.make_async_copy(wcol.at[k, pl.ds(s0, n)], dst.at[pl.ds(d0, n), lanes], colsem_r.at[i])

    def row_send(i, t):
        src, dst, d0, n = rows[i]
        dev, p = row_dest(t)
        there = pl.ds(pl.multiple_of(p * 128, 128), 128)
        return rcopy(
            src.at[:, there], dst.at[pl.ds(pl.multiple_of(d0 + k * n, 16), n), there],
            rowsem_s.at[i, t], rowsem_r.at[i, k], dev,
        )

    def row_keep(i):
        src, dst, d0, n = rows[i]
        return pltpu.make_async_copy(
            src.at[:, lanes], dst.at[pl.ds(pl.multiple_of(d0 + k * n, 16), n), lanes], rowsem_r.at[i, k]
        )

    def row_in(i, s):
        src, dst, d0, n = rows[i]
        there = dst.at[pl.ds(d0 + s * n, n), lanes]
        return rcopy(there, there, rowsem_s.at[i, s], rowsem_r.at[i, s], at.device(z=jz, x=jx, k=s))

    @pl.when(k == zl)
    def _():
        for i in range(2):
            col_send(i).start()
            col_keep(i).start()

    ring_h.start()

    @pl.when(is_src)
    def _():
        for i in range(2):
            for t in range(1, 8):
                row_send(i, t).start()

            @pl.when(kd == k)
            def _():
                row_keep(i).start()

            @pl.when(kd != k)
            def _():
                row_send(i, 0).start()

    def view(ref, r0, n):
        return lambda p, h: ref.at[pl.ds(r0 + h * (n // 2), n // 2), pl.ds(pl.multiple_of(p * 128, 128), 128)]

    planes = [
        PlaneGather(at, view(ref, r0, n), *order, psem_s.at[i], psem_r.at[i])
        for i, (ref, r0, n, order) in enumerate(
            (
                (wqo, Q0, 192, ("x", "z")),
                (wqo, Q0 + 192, 192, ("z", "x")),
                (wqo, O0, 256, ("z", "x")),
                (w_all, G0, 704, ("x", "z")),
                (w_all, U0, 704, ("z", "x")),
                (w_all, D0, 352, ("x", "z")),
                (w_all, D0 + 352, 352, ("z", "x")),
            )
        )
    ]
    pq, po, bulk = planes[:2], planes[2], planes[3:]
    col_keep(0).wait()
    for p in pq:
        p.step0()
    for s in range(2):
        row_in(0, s).wait_recv()
    po.step0()
    ring_h.step(0)
    for p in pq:
        p.step1()
    po.step1()
    ring_h.step(1)
    for p in pq:
        p.step2()
    po.step2()
    for p in pq:
        p.step3()
    po.step3()
    col_keep(1).wait()
    for p in bulk[:2]:
        p.step0()
    for s in range(2):
        row_in(1, s).wait_recv()
    for p in bulk[2:]:
        p.step0()
    ring_h.step(2)
    ring_h.finish()
    ring_c.start()
    for p in pq:
        p.step4()

    def project(t, c):
        h = hat_all[pl.ds(4 * t + 2 * c, 2)].reshape(256, D)
        proj = dot_nt(wqo[Q0 : Q0 + 384, :], h)
        col = pl.ds(pl.multiple_of(256 * c, 256), 256)
        co, si = cosine[t, :, col], sine[t, :, col]
        for head in range(4):
            u = rotate(proj[64 * head : 64 * head + 64], co, si, 1.0)
            q_out[t, 64 * head : 64 * head + 64, col] = (u * SCALE).astype(bf16)
        kv = jnp.concatenate([rotate(proj[256:320], co, si, 1.0), proj[320:]], axis=0).astype(bf16)
        for b in range(2):
            kvb[t, 2 * c + b, zl] = kv[:, 128 * b : 128 * b + 128]

    def kv_send():
        ref = kvb.at[k, :, zl]
        return rcopy(ref, ref, kvsem_s.at[0], kvsem_r.at[0], zpeer)

    def kv_in():
        ref = kvb.at[k, :, 1 - zl]
        return rcopy(ref, ref, kvsem_s.at[0], kvsem_r.at[0], zpeer)

    def kv_relay(kk):
        ref = kvb.at[kk, :, 1 - zl]
        return rcopy(ref, ref, kvsem_s.at[1], kvsem_r.at[1], at.sibling())

    pl.loop(0, 2)(functools.partial(project, k))
    kv_send().start()
    pl.loop(0, 2)(functools.partial(project, 1 - k))
    h_out = pltpu.make_async_copy(hat_all, hat_out, lsem.at[0])
    h_out.start()
    ring_c.step(0)
    kv_in().wait_recv()
    kv_relay(k).start()
    for p in bulk:
        p.step1()
    po.step4()
    w_out_copy = pltpu.make_async_copy(wqo, w_all.at[pl.ds(0, G0)], lsem.at[2])
    w_out_copy.start()
    kv_relay(1 - k).wait_recv()

    def attend(t):
        tree_keys(kvb, kvt, kvn, t)
        for b in range(4):
            n = 256 * (b + 1)
            col = slice(128 * b, 128 * b + 128)
            qs = heads_side_by_side(q_out, t, b)
            qs = jnp.concatenate([qs, jnp.zeros_like(qs)], axis=0)
            bias = mask_bias(bounds[t, :, col], n)
            s = dot_nn(kvn[:n, :], qs) + jnp.concatenate([bias] * 4, axis=1)
            peak = jnp.max(s, axis=0, keepdims=True)
            e = jnp.exp(s - peak)
            total = jnp.sum(e, axis=0, keepdims=True)
            o = dot_nn(kvt[64:128, :n], e.astype(bf16)) / total
            log_total = peak + jnp.log(total)
            for head in range(4):
                c = slice(128 * head, 128 * head + 128)
                att[t, 64 * head : 64 * head + 64, col] = o[:, c].astype(bf16)
                lse[t, head : head + 1, col] = log_total[:, c]

        @pl.loop(0, 2)
        def _(i):
            a = att[t, :, pl.ds(pl.multiple_of(256 * i, 256), 256)]
            r = dot_tn(a, wqo[O0 : O0 + 256, :]).astype(bf16)
            part[pl.ds(4 * t + 2 * i, 2)] = r.reshape(2, 128, D)

    attend(1 - k)
    red.cross_all()
    ring_c.step(1)
    attend(k)
    red.first()
    for p in bulk:
        p.step2()
    ring_c.step(2)
    red.second()
    for p in bulk:
        p.step3()

    def emit(rows, total):
        h = x[rows, :].astype(f32) + total
        hidden[rows, :] = h
        inv = lax.rsqrt(jnp.mean(h * h, axis=1, keepdims=True) + epsilon)
        own2[rows, :] = (h * inv).astype(bf16)

    red.collect(emit)
    ring_2.start()
    ring_c.finish()
    ring_2.step(0)
    ring_2.step(1)
    for p in bulk[:2]:
        p.step4()
    ring_2.step(2)
    for p in bulk[2:]:
        p.step4()
    ring_2.finish()
    red.finish()
    h_out.wait()
    w_out_copy.wait()
    kv_send().wait_send()
    kv_relay(k).wait_send()

    @pl.when(k == zl)
    def _():
        for i in range(2):
            col_send(i).wait_send()

    @pl.when(is_src)
    def _():
        for i in range(2):
            for t in range(1, 8):
                row_send(i, t).wait_send()

            @pl.when(kd != k)
            def _():
                row_send(i, 0).wait_send()


def forward_pass(hat, x, cot, wcol, wo, wd, cosine, sine, bounds):
    shape = jax.ShapeDtypeStruct
    dma = pltpu.SemaphoreType.DMA
    return pl.pallas_call(
        forward_kernel,
        name="forward_pass",
        out_shape=(
            shape((8, 128, D), bf16),
            shape((8, 128, D), bf16),
            shape((ROWS, D), bf16),
            shape((2, 256, 512), bf16),
            shape((2, 4, 2, 128, 128), bf16),
            shape((2, 256, 512), bf16),
            shape((2, 8, 512), f32),
            shape((128, D), f32),
            shape((8, 128, D), bf16),
        ),
        in_specs=[VM] * 9,
        out_specs=[ANY, ANY, ANY, VM, VM, VM, VM, VM, ANY],
        scratch_shapes=[
            pltpu.VMEM((8, 128, D), bf16),
            pltpu.VMEM((G0, D), bf16),
            pltpu.VMEM((8, 128, D), bf16),
            pltpu.VMEM((4, 128, D), bf16),
            pltpu.VMEM((6, 64, D), bf16),
            pltpu.VMEM((128, 1024), bf16),
            pltpu.VMEM((1024, 128), bf16),
            pltpu.VMEM((128, D), bf16),
        ]
        + [dma((RING_SEMS,))] * 6
        + [dma((7, PLANE_SEMS))] * 2
        + [dma((REDUCE_SEMS,))] * 2
        + [dma((2,)), dma((2,)), dma((2, 8)), dma((2, 2)), dma((2,)), dma((2,)), dma((4,))],
        compiler_params=pltpu.CompilerParams(
            collective_id=0, has_side_effects=True, vmem_limit_bytes=56 * 2**20
        ),
    )(hat, x, cot, wcol, wo, wd, cosine, sine, bounds)


def mlp_kernel(
    hat2_hbm, cot_hbm, w_hbm, hidden, cot,
    mixed, ghidden, gb_all, up_part, sum_g, sum_d,
    hat2, cotv, wgu, wdn, part, sib, recv, innert, dgu, pd, pg, pu, precv_d, precv_g, own_gb, mpart, msib, mrecv,
    rsem_s, rsem_r, msem_s, msem_r, gsem_s, gsem_r, psem_s, psem_r, lsem,
):
    at = Place()
    k, y = at.k, at.y
    loads = [
        pltpu.make_async_copy(src, dst, lsem.at[i])
        for i, (src, dst) in enumerate(
            (
                (w_hbm.at[pl.ds(G0, 1408)], wgu),
                (hat2_hbm, hat2),
                (w_hbm.at[pl.ds(D0, 704)], wdn),
                (cot_hbm, cotv),
            )
        )
    ]
    for c in loads:
        c.start()
    greet([at.sibling()] + [at.along(a, r) for a in ("x", "z", "y") for r in (1, -1)])
    await_greetings(7)
    red = RingReduce(at, part, sib, recv, rsem_s, rsem_r)
    redm = RingReduce(at, mpart, msib, mrecv, msem_s, msem_r)
    ring = RingGather(at, own_gb, gb_all, gsem_s, gsem_r, lsem.at[0])
    pr_d = PlaneReduce(at, pd, precv_d, "x", "z", psem_s.at[0], psem_r.at[0])
    pr_g = PlaneReduce(at, pg, precv_g, "z", "x", psem_s.at[1], psem_r.at[1])
    def columns(t, i):
        slot = 4 * t + 2 * i
        return slot, pl.ds(pl.multiple_of(slot * 128, 256), 256)

    loads[0].wait()
    loads[1].wait()

    @pl.loop(0, 4)
    def _(i):
        slot, cols = columns(0, i)
        both = dot_nt(wgu[...], hat2[pl.ds(slot, 2)].reshape(256, D))
        gate, up = both[:FJ], both[FJ:]
        sig = jax.nn.sigmoid(gate)
        silu = gate * sig
        innert[:, cols] = (silu * up).astype(bf16)
        dgu[:FJ, cols] = (up * sig * (1.0 + gate * (1.0 - sig))).astype(bf16)
        dgu[FJ:, cols] = silu.astype(bf16)

    loads[2].wait()

    def mix(t):
        @pl.loop(0, 2)
        def _(i):
            slot, cols = columns(t, i)
            r = dot_tn(innert[:, cols], wdn[...]).astype(bf16)
            mpart[pl.ds(slot, 2)] = r.reshape(2, 128, D)

    def mlp_back(t):
        @pl.loop(0, 2)
        def _(i):
            slot, cols = columns(t, i)
            gi = dot_nt(wdn[...], cotv[pl.ds(slot, 2)].reshape(256, D))
            dgu[:FJ, cols] = (gi * dgu[:FJ, cols].astype(f32)).astype(bf16)
            dgu[FJ:, cols] = (gi * dgu[FJ:, cols].astype(f32)).astype(bf16)

        @pl.loop(0, 2)
        def _(i):
            slot, cols = columns(t, i)
            r = dot_tn(dgu[:, cols], wgu[...]).astype(bf16)
            part[pl.ds(slot, 2)] = r.reshape(2, 128, D)

    def weight_grad(left, right, out):
        @pl.loop(0, 4)
        def _(i):
            cols = pl.ds(pl.multiple_of(512 * i, 512), 512)
            g = dot_nn(left[...], right[:, :, cols].reshape(1024, 512)).astype(bf16)
            for q in range(4):
                out[4 * i + q] = g[:, 128 * q : 128 * q + 128]

    loads[3].wait()
    mix(1 - k)
    redm.cross_all()
    mix(k)
    redm.first()
    mlp_back(1 - k)
    red.cross_all()
    redm.second()
    mlp_back(k)
    red.first()
    weight_grad(innert, cotv, pd)
    pr_d.start_all()
    red.second()

    def emit_mixed(rows, total):
        mixed[rows, :] = (hidden[rows, :] + total).astype(bf16)

    redm.collect(emit_mixed)
    weight_grad(dgu.at[:FJ], hat2, pg)
    pr_g.start_all()
    pr_d.middle_all()

    def emit(rows, total):
        h = hidden[rows, :]
        inv = lax.rsqrt(jnp.mean(h * h, axis=1, keepdims=True) + epsilon)
        hat = h * inv
        g = cot[rows, :].astype(f32) + inv * (total - hat * jnp.mean(total * hat, axis=1, keepdims=True))
        ghidden[rows, :] = g
        own_gb[rows, :] = g.astype(bf16)

    red.collect(emit)
    ring.start()
    pr_g.middle_all()

    ring.step(0)
    weight_grad(dgu.at[FJ:], hat2, pu)
    u_out = pltpu.make_async_copy(pu, up_part, lsem.at[4])
    u_out.start()
    ring.step(1)
    pr_d.end_all()
    pr_g.end_all()
    red.finish()
    ring.step(2)

    pr_d.last()
    d_out = pltpu.make_async_copy(pd.at[at.piece()], sum_d, lsem.at[2])
    d_out.start()
    pr_g.last()
    g_out = pltpu.make_async_copy(pg.at[at.piece()], sum_g, lsem.at[3])
    g_out.start()
    ring.finish()
    pr_d.finish()
    pr_g.finish()
    redm.finish()
    u_out.wait()
    d_out.wait()
    g_out.wait()


def mlp_pass(hat2_all, cot_all, w_all, hidden, cot):
    shape = jax.ShapeDtypeStruct
    dma = pltpu.SemaphoreType.DMA
    block = pltpu.VMEM((8, 128, D), bf16)
    return pl.pallas_call(
        mlp_kernel,
        name="mlp_pass",
        out_shape=(
            shape((128, D), bf16),
            shape((128, D), f32),
            shape((8, 128, D), bf16),
            shape((16, FJ, 128), bf16),
            shape((FJ, 128), bf16),
            shape((FJ, 128), bf16),
        ),
        in_specs=[ANY, ANY, ANY, VM, VM],
        out_specs=[VM, VM, ANY, ANY, ANY, ANY],
        scratch_shapes=[
            block, block,
            pltpu.VMEM((2 * FJ, D), bf16), pltpu.VMEM((FJ, D), bf16),
            block,
            pltpu.VMEM((4, 128, D), bf16),
            pltpu.VMEM((6, 64, D), bf16),
            pltpu.VMEM((FJ, 1024), bf16), pltpu.VMEM((2 * FJ, 1024), bf16),
            pltpu.VMEM((16, FJ, 128), bf16), pltpu.VMEM((16, FJ, 128), bf16), pltpu.VMEM((16, FJ, 128), bf16),
            pltpu.VMEM((30, FJ // 2, 128), bf16), pltpu.VMEM((30, FJ // 2, 128), bf16),
            pltpu.VMEM((128, D), bf16),
            block, pltpu.VMEM((4, 128, D), bf16), pltpu.VMEM((6, 64, D), bf16),
            dma((REDUCE_SEMS,)), dma((REDUCE_SEMS,)), dma((REDUCE_SEMS,)), dma((REDUCE_SEMS,)), dma((RING_SEMS,)), dma((RING_SEMS,)),
            dma((2, PLANE_SEMS)), dma((2, PLANE_SEMS)), dma((5,)),
        ],
        compiler_params=pltpu.CompilerParams(
            collective_id=1, has_side_effects=True, vmem_limit_bytes=62 * 2**20
        ),
    )(hat2_all, cot_all, w_all, hidden, cot)


class ColSpread:
    def __init__(self, at, src, dst, ssem, rsem):
        self.at, self.src, self.dst, self.ssem, self.rsem = at, src, dst, ssem, rsem
        self.home = at.k == at.zl
        self.there = dst.at[2 * at.y + at.k]

    def near(self):
        return rcopy(self.src, self.there, self.ssem.at[6], self.rsem.at[6 + self.at.k], self.at.sibling())

    def far(self):
        at = self.at
        dev = at.device(z=at.z + 1 - 2 * at.zl, k=at.zl)
        return rcopy(self.src, self.there, self.ssem.at[7], self.rsem.at[6 + at.k], dev)

    def start(self):
        self.far().start()

        @pl.when(self.home)
        def _():
            pltpu.make_async_copy(self.src, self.there, self.rsem.at[6 + self.at.k]).start()

        @pl.when(jnp.logical_not(self.home))
        def _():
            self.near().start()

    def copy(self, d, m, incoming):
        step = 1 - 2 * d
        h = d if m in (0, 2) else 1 - d
        back = (-step if m == 2 else 0) - (step if incoming else 0)
        ref = self.dst.at[2 * self.at.moved("y", back) + h]
        i = d * 3 + m
        return rcopy(ref, ref, self.ssem.at[i], self.rsem.at[i], self.at.along("y", step))

    def ring(self):
        for h in range(2):
            pltpu.make_async_copy(self.src, self.dst.at[2 * self.at.y + h], self.rsem.at[6 + h]).wait()
        for m in (0, 1):
            for d in (0, 1):
                self.copy(d, m, False).start()

    def middle(self):
        for d in (0, 1):
            self.copy(d, 0, True).wait_recv()
            self.copy(d, 2, False).start()

    def finish(self):
        for d in (0, 1):
            for m in (1, 2):
                self.copy(d, m, True).wait_recv()
        for d in (0, 1):
            for m in range(3):
                self.copy(d, m, False).wait_send()
        self.far().wait_send()

        @pl.when(jnp.logical_not(self.home))
        def _():
            self.near().wait_send()


class RowSpread:
    def __init__(self, at, src, buf, dst, ssem, rsem):
        self.at, self.src, self.buf, self.dst, self.ssem, self.rsem = at, src, buf, dst, ssem, rsem
        self.m = dst.shape[0]
        self.lanes = pl.ds(pl.multiple_of(at.piece() * 128, 128), 128)

    def keep(self, h):
        return pltpu.make_async_copy(self.src.at[pl.ds(h * self.m, self.m)], self.buf.at[self.at.y, h], self.ssem.at[6 + h])

    def start(self):
        for h in range(2):
            self.keep(h).start()
        for m in (0, 1):
            for d in (0, 1):
                self.copy(d, m, False).start()

    def copy(self, d, m, incoming):
        step = 1 - 2 * d
        h = d if m in (0, 2) else 1 - d
        back = (-step if m == 2 else 0) - (step if incoming else 0)
        ref = self.buf.at[self.at.moved("y", back), h]
        i = d * 3 + m
        src = ref if incoming or m == 2 else self.src.at[pl.ds(h * self.m, self.m)]
        return rcopy(src, ref, self.ssem.at[i], self.rsem.at[i], self.at.along("y", step))

    def middle(self):
        for d in (0, 1):
            self.copy(d, 0, True).wait_recv()
            self.copy(d, 2, False).start()

    def each(self, f, g):
        at = self.at
        for y in range(4):
            for dz in (1, 0):
                for c in range(2):
                    if dz:
                        f(y, dz, c)
                    else:
                        mine = (at.zh == y // 2) & (at.x == 2 * (y % 2) + at.k) & (at.k == c)
                        pl.when(mine)(functools.partial(g, y, c))
                        pl.when(jnp.logical_not(mine))(functools.partial(f, y, dz, c))

    def device(self, y, dz, c):
        at = self.at
        return at.device(z=2 * (y // 2) + (at.zl + dz) % 2, x=2 * (y % 2) + at.k, k=c)

    def push_copy(self, y, dz, c):
        return rcopy(
            self.buf.at[y, c], self.dst.at[:, self.lanes], self.ssem.at[8 + (y * 2 + dz) * 2 + c],
            self.rsem.at[6 + self.at.piece()], self.device(y, dz, c),
        )

    def push(self):
        for h in range(2):
            self.keep(h).wait()
        for d in (0, 1):
            for m in (1, 2):
                self.copy(d, m, True).wait_recv()

        def local(y, c):
            pltpu.make_async_copy(
                self.buf.at[y, c], self.dst.at[:, self.lanes], self.rsem.at[6 + self.at.piece()]
            ).start()

        self.each(lambda y, dz, c: self.push_copy(y, dz, c).start(), local)

    def finish(self):
        for p in range(16):
            pltpu.make_async_copy(self.buf.at[0, 0], self.dst.at[:, pl.ds(p * 128, 128)], self.rsem.at[6 + p]).wait()
        for d in (0, 1):
            for m in range(3):
                self.copy(d, m, False).wait_send()
        self.each(lambda y, dz, c: self.push_copy(y, dz, c).wait_send(), lambda y, c: None)

    def greet(self):
        at = self.at
        self.each(lambda y, dz, c: greet([self.device(y, dz, c)]), lambda y, c: None)
        for p in range(16):
            z, x = (p // 8) * 2 + p % 2, (p // 2) % 4
            mine = (at.z == z) & (at.x == x) & (at.k == at.x % 2)

            @pl.when(jnp.logical_not(mine))
            def _():
                greet([at.device(z=z, x=x, k=at.x % 2)])

        return 2 * (16 - jnp.where(at.x % 2 == at.k, 1, 0))


def backward_kernel(
    gb_hbm, hat_hbm, w_hbm, q, kvb, att, lse, cosine, sine, bounds, x, ghidden, up_part, sum_g, sum_d,
    grad_tokens, out_q, out_g, out_u, out_o, out_d,
    gb, hat, wqo, pu, pq, po, precv_u, precv_q, precv_o, part, sib, recv,
    datt, dproj, dkv, dkv_far, dkv_got, kvt, kvn, buf_o, buf_d,
    rsem_s, rsem_r, psem_s, psem_r, xsem_s, xsem_r, csem_s, csem_r, wsem_s, wsem_r, lsem,
):
    at = Place()
    k, y, zl = at.k, at.y, at.zl
    zpeer = at.device(z=at.z + 1 - 2 * zl)
    loads = [
        pltpu.make_async_copy(src, dst, lsem.at[i])
        for i, (src, dst) in enumerate(
            (
                (w_hbm.at[pl.ds(0, G0)], wqo),
                (gb_hbm, gb),
                (up_part, pu),
                (hat_hbm, hat),
            )
        )
    ]
    for c in loads:
        c.start()
    cols_q = ColSpread(at, pq.at[at.piece()], out_q, csem_s.at[0], csem_r.at[0])
    cols_g = ColSpread(at, sum_g, out_g, csem_s.at[1], csem_r.at[1])
    cols_u = ColSpread(at, pu.at[at.piece()], out_u, csem_s.at[2], csem_r.at[2])
    rows_o = RowSpread(at, po.at[at.piece()], buf_o, out_o, wsem_s.at[0], wsem_r.at[0])
    rows_d = RowSpread(at, sum_d, buf_d, out_d, wsem_s.at[1], wsem_r.at[1])
    greet([at.sibling(), at.device(z=at.z + 1 - 2 * zl, k=1 - k)])
    greet([at.along(a, r) for a in ("x", "z", "y") for r in (1, -1)])
    await_greetings(8 + rows_o.greet())

    red = RingReduce(at, part, sib, recv, rsem_s, rsem_r)
    pr_u = PlaneReduce(at, pu, precv_u, "x", "z", psem_s.at[0], psem_r.at[0])
    pr_q = PlaneReduce(at, pq, precv_q, "z", "x", psem_s.at[1], psem_r.at[1])
    pr_o = PlaneReduce(at, po, precv_o, "z", "x", psem_s.at[2], psem_r.at[2])
    cols_g.start()
    rows_d.start()
    loads[2].wait()
    pr_u.start_all()
    loads[0].wait()
    loads[1].wait()

    @pl.loop(0, 4)
    def _(i):
        g = gb[pl.ds(2 * i, 2)].reshape(256, D)
        r = dot_nt(wqo[O0 : O0 + 256, :], g)
        datt[i // 2, :, pl.ds(pl.multiple_of(256 * (i % 2), 256), 256)] = r.astype(bf16)

    cols_g.ring()

    def weight_grad(left, right, ref):
        @pl.loop(0, 4)
        def _(i):
            cols = pl.ds(pl.multiple_of(512 * i, 512), 512)
            g = dot_nn(left[0], right[0:4, :, cols].reshape(512, 512))
            g += dot_nn(left[1], right[4:8, :, cols].reshape(512, 512))
            g = g.astype(bf16)
            for s in range(4):
                ref[4 * i + s] = g[:, 128 * s : 128 * s + 128]

    weight_grad(att, gb, po)
    pr_o.start_all()

    def attend(t):
        tree_keys(kvb, kvt, kvn, t)
        for b in (3, 2, 1, 0):
            n = 256 * (b + 1)
            col = slice(128 * b, 128 * b + 128)
            qs = heads_side_by_side(q, t, b)
            dos = heads_side_by_side(datt, t, b)
            zero = jnp.zeros_like(qs)
            bias = mask_bias(bounds[t, :, col], n)
            log_total = jnp.concatenate([lse[t, h : h + 1, col] for h in range(4)], axis=1)
            s = dot_nn(kvn[:n, :], jnp.concatenate([qs, zero], axis=0)) + jnp.concatenate([bias] * 4, axis=1)
            prob = jnp.exp(s - log_total)
            dprob = dot_nn(kvn[:n, :], jnp.concatenate([zero, dos], axis=0))
            inner = jnp.sum(prob * dprob, axis=0, keepdims=True)
            ds = (prob * (dprob - inner)).astype(bf16)
            dq = dot_nn(kvt[0:64, :n], ds) * SCALE
            co, si = cosine[t, :, col], sine[t, :, col]
            for h in range(4):
                u = rotate(dq[:, 128 * h : 128 * h + 128], co, si, -1.0)
                dproj[t, 64 * h : 64 * h + 64, col] = u.astype(bf16)
            dk = dot_nt(qs, ds)
            dv = dot_nt(dos, prob.astype(bf16))
            for c in range(2 * (b + 1)):
                blk = slice(128 * c, 128 * c + 128)
                if b == 3:
                    dkv[t, c // 2, c % 2, :64, :] = dk[:, blk]
                    dkv[t, c // 2, c % 2, 64:, :] = dv[:, blk]
                else:
                    dkv[t, c // 2, c % 2, :64, :] += dk[:, blk]
                    dkv[t, c // 2, c % 2, 64:, :] += dv[:, blk]
        for b in range(4):
            dkv_far[t, b] = dkv[t, b, 1 - zl].astype(bf16)

    def far_copy(t, s):
        return rcopy(dkv_far.at[t], dkv_got.at[t], xsem_s.at[s], xsem_r.at[s], zpeer)

    def project(t, s):
        far_copy(t, s).wait_recv()
        for b in range(4):
            col = slice(128 * b, 128 * b + 128)
            total = dkv[t, b, zl] + dkv_got[t, b].astype(f32)
            dk = rotate(total[:64], cosine[t, :, col], sine[t, :, col], -1.0)
            dproj[t, 256:320, col] = dk.astype(bf16)
            dproj[t, 320:384, col] = total[64:].astype(bf16)

        @pl.loop(0, 2)
        def _(i):
            a = dproj[t, :, pl.ds(pl.multiple_of(256 * i, 256), 256)]
            r = dot_tn(a, wqo[Q0 : Q0 + 384, :]).astype(bf16)
            part[pl.ds(4 * t + 2 * i, 2)] = r.reshape(2, 128, D)

    attend(1 - k)
    far_copy(1 - k, 0).start()
    rows_d.middle()
    pr_u.middle(2)
    pr_u.middle(1)
    attend(k)
    far_copy(k, 1).start()
    rows_d.push()
    project(1 - k, 0)
    red.cross_all()
    pr_u.middle(3)
    pr_u.middle(0)
    project(k, 1)
    red.first()
    pr_o.middle_all()
    cols_g.middle()
    loads[3].wait()
    weight_grad(dproj, hat, pq)
    pr_q.start_all()
    red.second()
    pr_u.end_all()
    pr_o.end_all()
    pr_q.middle_all()
    pr_u.last()
    cols_u.start()
    pr_o.last()
    rows_o.start()
    cols_u.ring()

    def emit(rows, total):
        h = x[rows, :].astype(f32)
        inv = lax.rsqrt(jnp.mean(h * h, axis=1, keepdims=True) + epsilon)
        hat1 = h * inv
        g = ghidden[rows, :] + inv * (total - hat1 * jnp.mean(total * hat1, axis=1, keepdims=True))
        grad_tokens[rows, :] = g

    pr_q.end_all()
    rows_o.middle()
    red.collect(emit)
    pr_q.last()
    cols_q.start()
    cols_u.middle()
    rows_o.push()
    cols_q.ring()
    cols_g.finish()
    rows_d.finish()
    cols_q.middle()
    cols_u.finish()
    rows_o.finish()
    cols_q.finish()
    for s, t in ((0, 1 - k), (1, k)):
        far_copy(t, s).wait_send()
    red.finish()
    pr_u.finish()
    pr_o.finish()
    pr_q.finish()


def backward_pass(*args):
    shape = jax.ShapeDtypeStruct
    dma = pltpu.SemaphoreType.DMA
    block = pltpu.VMEM((8, 128, D), bf16)
    return pl.pallas_call(
        backward_kernel,
        name="backward_pass",
        out_shape=(
            shape((128, D), f32),
            shape((8, 384, 128), bf16),
            shape((8, FJ, 128), bf16),
            shape((8, FJ, 128), bf16),
            shape((128, D), bf16),
            shape((352, D), bf16),
        ),
        in_specs=[ANY, ANY, ANY, VM, VM, VM, VM, VM, VM, VM, VM, VM, ANY, VM, VM],
        out_specs=[VM] + [ANY] * 5,
        scratch_shapes=[
            block, block, pltpu.VMEM((G0, D), bf16),
            pltpu.VMEM((16, FJ, 128), bf16), pltpu.VMEM((16, 384, 128), bf16), pltpu.VMEM((16, 256, 128), bf16),
            pltpu.VMEM((30, FJ // 2, 128), bf16), pltpu.VMEM((30, 192, 128), bf16), pltpu.VMEM((30, 128, 128), bf16),
            block, pltpu.VMEM((4, 128, D), bf16), pltpu.VMEM((6, 64, D), bf16),
            pltpu.VMEM((2, 256, 512), bf16),
            pltpu.VMEM((2, 384, 512), bf16),
            pltpu.VMEM((2, 4, 2, 128, 128), f32),
            pltpu.VMEM((2, 4, 128, 128), bf16),
            pltpu.VMEM((2, 4, 128, 128), bf16),
            pltpu.VMEM((128, 1024), bf16),
            pltpu.VMEM((1024, 128), bf16),
            pltpu.VMEM((4, 2, 128, 128), bf16),
            pltpu.VMEM((4, 2, 352, 128), bf16),
            dma((REDUCE_SEMS,)), dma((REDUCE_SEMS,)),
            dma((3, PLANE_SEMS)), dma((3, PLANE_SEMS)), dma((2,)), dma((2,)),
            dma((3, 8)), dma((3, 8)), dma((2, 24)), dma((2, 22)), dma((5,)),
        ],
        compiler_params=pltpu.CompilerParams(
            collective_id=2, has_side_effects=True, vmem_limit_bytes=62 * 2**20
        ),
    )(*args)


def finish_kernel(og, ou, rq, rkv, oo, od, wg, wu, wq, gain1, gain2, g_gate, g_up, g_qkv, g_out, g_down, s_one, s_two):
    i = pl.program_id(0)

    @pl.when(i == 0)
    def _():
        s_one[...] = jnp.zeros_like(s_one)
        s_two[...] = jnp.zeros_like(s_two)

    total = None
    for src, w, dst in ((og, wg, g_gate), (ou, wu, g_up)):
        raw = src[...].astype(f32).T
        dst[...] = raw * gain2[...]
        dot = jnp.sum(raw * w[...].astype(f32), axis=1, keepdims=True)
        total = dot if total is None else total + dot
    s_two[...] += total

    def qkv(raw):
        g_qkv[...] = raw * gain1[...]
        s_one[...] += jnp.sum(raw * wq[...].astype(f32), axis=1, keepdims=True)

    @pl.when(i < 4)
    def _():
        qkv(rq[...].reshape(512, 128).astype(f32).T)

    @pl.when(i == 4)
    def _():
        pairs = [rkv[2 * g].astype(f32) + rkv[2 * g + 1].astype(f32) for g in range(KVH)]
        qkv(jnp.concatenate([p[:64] for p in pairs] + [p[64:] for p in pairs], axis=0).T)

    g_out[...] = oo[...].astype(f32)
    g_down[...] = od[...].astype(f32)


def finish(og, ou, oq, oo, od, wg, wu, wq, gain1, gain2):
    shape = jax.ShapeDtypeStruct
    row = lambda i: (i, 0)
    col = lambda i: (0, i)
    whole = lambda i: (0, 0)
    q_col = lambda i: (0, jnp.minimum(i, 4))
    o_row = lambda i: (jnp.minimum(i, 7), 0)
    return pl.pallas_call(
        finish_kernel,
        name="finish",
        grid=(11,),
        out_shape=(
            shape((128, FF), f32), shape((128, FF), f32), shape((128, 2560), f32), shape((128, D), f32), shape((352, D), f32),
            shape((128, 1), f32), shape((128, 1), f32),
        ),
        in_specs=[
            pl.BlockSpec((512, 128), row),
            pl.BlockSpec((512, 128), row),
            pl.BlockSpec((2, 256, 128), lambda i: (jnp.minimum(i, 3), 0, 0)),
            pl.BlockSpec((8, 128, 128), lambda i: (0, 2, 0)),
            pl.BlockSpec((16, D), o_row),
            pl.BlockSpec((32, D), row),
            pl.BlockSpec((128, 512), col),
            pl.BlockSpec((128, 512), col),
            pl.BlockSpec((128, 512), q_col),
            pl.BlockSpec((128, 1), whole),
            pl.BlockSpec((128, 1), whole),
        ],
        out_specs=(
            pl.BlockSpec((128, 512), col),
            pl.BlockSpec((128, 512), col),
            pl.BlockSpec((128, 512), q_col),
            pl.BlockSpec((16, D), o_row),
            pl.BlockSpec((32, D), row),
            pl.BlockSpec((128, 1), whole),
            pl.BlockSpec((128, 1), whole),
        ),
        compiler_params=pltpu.CompilerParams(vmem_limit_bytes=62 * 2**20),
    )(og, ou, oq, oq, oo, od, wg, wu, wq, gain1, gain2)


def segment_bounds(lengths, offsets):
    ends = jnp.cumsum(lengths)
    starts = ends - lengths
    segment = jnp.sum((offsets[:, None] >= ends[None, :]).astype(jnp.int32), axis=1)
    seg_ids = np.arange(13)
    branch_of = jnp.asarray(np.where(seg_ids > 0, 1 + 3 * ((seg_ids - 1) // 3), 0), jnp.int32)
    onehot = segment[:, None] == jnp.asarray(seg_ids, jnp.int32)[None, :]

    def pick(values):
        return jnp.sum(jnp.where(onehot, values[None, :], 0), axis=1)

    table = np.zeros((13, 13), np.int32)
    for s in range(13):
        if s:
            table[s, 1 + 3 * ((s - 1) // 3)] = 1
        else:
            table[s, 0] = 1
    table = jnp.asarray(table)
    b0 = jnp.sum(table * starts[None, :], axis=1)
    b1 = jnp.sum(table * ends[None, :], axis=1)
    is_leaf = jnp.asarray((seg_ids > 0) & ((seg_ids - 1) % 3 > 0), jnp.int32)
    depth = jnp.where(jnp.asarray(seg_ids > 0), lengths[0], 0) + is_leaf * (b1 - b0)
    position = offsets - pick(starts) + pick(depth)
    trunk = jnp.broadcast_to(lengths[0], offsets.shape)
    return jnp.stack([offsets, trunk, pick(starts), pick(b0), pick(b1)], axis=1), position


def shards(tokens, cotangent, tree_lengths, gain_attn, w_qkv, w_out, gain_mlp, w_gate, w_up, w_down):
    at = Place()
    swapped = lax.ppermute(tree_lengths, "fsdp", [(f, f ^ 1) for f in range(16)])
    lengths = jnp.where(at.k == 0, jnp.stack([tree_lengths[0], swapped[0]]), jnp.stack([swapped[0], tree_lengths[0]]))
    offsets = (
        (2 * jnp.arange(4, dtype=jnp.int32)[:, None] + at.zl) * 128 + jnp.arange(128, dtype=jnp.int32)[None, :]
    ).reshape(512)
    b_a, p_a = segment_bounds(lengths[0], offsets)
    b_b, p_b = segment_bounds(lengths[1], offsets)
    bounds = jnp.pad(jnp.stack([b_a.T, b_b.T]), ((0, 0), (0, 3), (0, 0)))
    position = jnp.stack([p_a, p_b]).astype(f32)
    frequency = 10000.0 ** (-2.0 * jnp.arange(32, dtype=f32) / 64)
    angles = position[:, None, :] * frequency[None, :, None]
    cosine, sine = jnp.cos(angles), jnp.sin(angles)

    gain1 = gain_attn.astype(f32)[:, None]
    gain2 = gain_mlp.astype(f32)[:, None]

    def columns(w, start, n, gain):
        return (lax.dynamic_slice_in_dim(w, start, n, axis=1).astype(f32) * gain).astype(bf16).T

    q_cols = columns(w_qkv, at.y * 512, 512, gain1)
    k_cols = columns(w_qkv, 2048 + at.y * 64, 64, gain1)
    v_cols = columns(w_qkv, 2304 + at.y * 64, 64, gain1)
    g_cols = columns(w_gate, at.y * 2 * FJ, 2 * FJ, gain2)
    u_cols = columns(w_up, at.y * 2 * FJ, 2 * FJ, gain2)
    wcol = jnp.stack(
        [
            jnp.concatenate(
                [q_cols[256 * i : 256 * i + 256], k_cols, v_cols, g_cols[FJ * i : FJ * i + FJ], u_cols[FJ * i : FJ * i + FJ]]
            )
            for i in range(2)
        ]
    )

    inputs = tokens.astype(f32)
    inv1 = lax.rsqrt(jnp.mean(inputs * inputs, axis=-1, keepdims=True) + epsilon)
    hat1 = (inputs * inv1).astype(bf16)
    hat_all, cot_all, w_all, q, kvb, att, lse, hidden, hat2_all = forward_pass(
        hat1, tokens, cotangent, wcol, w_out, w_down, cosine, sine, bounds
    )
    mixed, ghidden, gb_all, up_part, sum_g, sum_d = mlp_pass(hat2_all, cot_all, w_all, hidden, cotangent)
    grad_tokens, oq, og, ou, oo, od = backward_pass(
        gb_all, hat_all, w_all, q, kvb, att, lse, cosine, sine, bounds, tokens, ghidden, up_part, sum_g, sum_d
    )
    g_gate, g_up, g_qkv, g_out, g_down, grad_gain1, grad_gain2 = finish(
        og.reshape(FF, 128), ou.reshape(FF, 128), oq, oo, od, w_gate, w_up, w_qkv, gain1, gain2
    )
    return (mixed, grad_tokens, grad_gain1[:, 0], g_qkv, g_out, grad_gain2[:, 0], g_gate, g_up, g_down)


def solution(mesh):
    row = P("fsdp", None)
    tok = P(("fsdp", "ctx"), None)
    vec = P("fsdp")
    return jax.shard_map(
        shards,
        mesh=mesh,
        in_specs=(tok, tok, row, vec, row, row, vec, row, row, row),
        out_specs=(tok, tok, vec, row, row, vec, row, row, row),
        check_vma=False,
    )
```

```python
import functools

import jax
import jax.numpy as jnp
import numpy as np
from jax import lax
from jax.experimental import pallas as pl
from jax.experimental.pallas import tpu as pltpu
from jax.sharding import PartitionSpec as P

D = 2048
FF = 5632
H = 32
KVH = 4
HD = 64
FJ = FF // 8
bf16 = jnp.bfloat16
f32 = jnp.float32
MESH = pl.DeviceIdType.MESH
epsilon = 1e-05
masked_score = -1e30
ANY = pl.BlockSpec(memory_space=pl.ANY)
VM = pl.BlockSpec(memory_space=pltpu.VMEM)


class Place:
    def __init__(self):
        fs = lax.axis_index("fsdp")
        ct = lax.axis_index("ctx")
        self.zh, self.x, self.k = fs // 8, (fs // 2) % 4, fs % 2
        self.y, self.zl = ct // 2, ct % 2
        self.z = 2 * self.zh + self.zl
        self.at = {a: [getattr(self, a)] + [(getattr(self, a) + r) % 4 for r in (1, 2, 3)] for a in ("x", "y", "z")}
        self.next = {(a, r): self.device(**{a: self.at[a][r % 4]}) for a in ("x", "y", "z") for r in (1, -1)}
        self.other = self.device(k=1 - self.k)
        self.pieces = [[self.piece_of(z, x) for x in self.at["x"]] for z in self.at["z"]]

    def device(self, z=None, x=None, k=None, y=None):
        z = self.z if z is None else z
        x = self.x if x is None else x
        k = self.k if k is None else k
        y = self.y if y is None else y
        return ((z // 2) * 8 + x * 2 + k, y * 2 + z % 2)

    def sibling(self):
        return self.other

    def along(self, axis, r):
        return self.next[axis, r]

    def piece_of(self, z, x):
        return (z // 2) * 8 + x * 2 + z % 2

    def piece(self, **r):
        return self.pieces[r.get("z", 0) % 4][r.get("x", 0) % 4]

    def moved(self, axis, r):
        return self.at[axis][r % 4]


def rcopy(src, dst, ssem, rsem, dev):
    return pltpu.make_async_remote_copy(
        src_ref=src, dst_ref=dst, send_sem=ssem, recv_sem=rsem, device_id=dev, device_id_type=MESH
    )


def greet(devices):
    bar = pltpu.get_barrier_semaphore()
    for dev in devices:
        pl.semaphore_signal(bar, inc=1, device_id=dev, device_id_type=MESH)


def await_greetings(count):
    pl.semaphore_wait(pltpu.get_barrier_semaphore(), count)


class RingGather:
    messages = 12

    def __init__(self, at, own, buf, ssem, rsem, lsem):
        self.at, self.own, self.buf, self.ssem, self.rsem = at, own, buf, ssem, rsem
        self.keep = pltpu.make_async_copy(own, buf.at[at.k * 4 + at.y], lsem)

    def half(self, r, h, k=None):
        k = self.at.k if k is None else k
        return self.buf.at[k * 4 + self.at.moved("y", r), pl.ds(64 * h, 64)]

    def copy(self, d, m, incoming):
        step = 1 - 2 * d
        h = d if m in (0, 2) else 1 - d
        back = (-step if m == 2 else 0) - (step if incoming else 0)
        ref = self.half(back, h)
        i = d * 3 + m
        src = ref if incoming or m == 2 else self.own.at[pl.ds(64 * h, 64)]
        return rcopy(src, ref, self.ssem.at[i], self.rsem.at[i], self.at.along("y", step))

    def relay(self, i, incoming):
        k = 1 - self.at.k if incoming else self.at.k
        if i < 6:
            d, m = i // 3, i % 3
            step = 1 - 2 * d
            h = d if m in (0, 2) else 1 - d
            ref = self.half((-2 if m == 2 else -1) * step, h, k)
        else:
            ref = self.half(0, i - 6, k)
        src = ref if incoming or i < 6 else self.own.at[pl.ds(64 * (i - 6), 64)]
        return rcopy(src, ref, self.ssem.at[6 + i], self.rsem.at[6 + i], self.at.sibling())

    def start(self):
        for m in (0, 1):
            for d in (0, 1):
                self.copy(d, m, False).start()
        for i in (6, 7):
            self.relay(i, False).start()
        self.keep.start()

    def step(self, m):
        for d in (0, 1):
            self.copy(d, m, True).wait_recv()
            if m == 0:
                self.copy(d, 2, False).start()
            self.relay(d * 3 + m, False).start()

    def finish(self):
        self.keep.wait()
        for i in range(8):
            self.relay(i, True).wait_recv()
            self.relay(i, False).wait_send()
        for d in (0, 1):
            for m in range(3):
                self.copy(d, m, False).wait_send()


RING_SEMS = 14


class RingReduce:
    def __init__(self, at, part, sib, recv, ssem, rsem):
        self.at, self.part, self.sib, self.recv = at, part, sib, recv
        self.ssem, self.rsem = ssem, rsem

    def cross(self, r):
        y = self.at.moved("y", r)
        return rcopy(
            self.part.at[(1 - self.at.k) * 4 + y], self.sib.at[r], self.ssem.at[6 + r], self.rsem.at[6 + r], self.at.sibling()
        )

    def copy(self, d, m):
        step = 1 - 2 * d
        h = d if m in (0, 2) else 1 - d
        y = self.at.moved("y", 2 if m == 0 else step)
        i = d * 3 + m
        return rcopy(
            self.part.at[self.at.k * 4 + y, pl.ds(64 * h, 64)], self.recv.at[i], self.ssem.at[i], self.rsem.at[i], self.at.along("y", step)
        )

    def cross_all(self):
        for r in (2, 1, 3, 0):
            self.cross(r).start()

    def add(self, r, h, others):
        y = self.at.moved("y", r)

        @pl.loop(0, 4)
        def _(i):
            rows = pl.ds(pl.multiple_of(64 * h + i * 16, 16), 16)
            total = self.part[self.at.k * 4 + y, rows, :].astype(f32) + self.sib[r, rows, :].astype(f32)
            for o in others:
                total += self.recv[o, pl.ds(pl.multiple_of(i * 16, 16), 16), :].astype(f32)
            self.part[self.at.k * 4 + y, rows, :] = total.astype(bf16)

    def first(self):
        self.cross(2).wait_recv()
        for d in (0, 1):
            self.add(2, d, ())
            self.copy(d, 0).start()
        for d in (0, 1):
            r = 1 if d == 0 else 3
            self.cross(r).wait_recv()
            self.add(r, 1 - d, ())
            self.copy(d, 1).start()

    def second(self):
        for d in (0, 1):
            self.copy(d, 0).wait_recv()
            self.add(1 if d == 0 else 3, d, (d * 3,))
            self.copy(d, 2).start()

    def collect(self, emit):
        self.cross(0).wait_recv()
        for d in (0, 1):
            for m in (1, 2):
                self.copy(d, m).wait_recv()
        for h in range(2):
            left, right = (2, 4) if h == 0 else (1, 5)

            @pl.loop(0, 4)
            def _(i):
                rows = pl.ds(pl.multiple_of(64 * h + i * 16, 16), 16)
                here = pl.ds(pl.multiple_of(i * 16, 16), 16)
                total = self.part[self.at.k * 4 + self.at.y, rows, :].astype(f32) + self.sib[0, rows, :].astype(f32)
                total += self.recv[left, here, :].astype(f32) + self.recv[right, here, :].astype(f32)
                emit(rows, total)

    def finish(self):
        for r in range(4):
            self.cross(r).wait_send()
        for d in (0, 1):
            for m in range(3):
                self.copy(d, m).wait_send()


REDUCE_SEMS = 10


class PlaneReduce:
    def __init__(self, at, part, recv, first, second, ssem, rsem, base=0):
        self.at, self.part, self.recv, self.base = at, part, recv, base
        self.first, self.second, self.ssem, self.rsem = first, second, ssem, rsem
        self.rows = recv.shape[1]

    def piece(self, a, c):
        return self.at.piece(**{self.first: a, self.second: c})

    def half(self, h):
        return pl.ds(self.base + h * self.rows, self.rows)

    def copy(self, c, d, m):
        step = 1 - 2 * d
        h = d if m in (0, 2) else 1 - d
        r = 2 if m == 0 else step
        p = self.piece(r, c) if c < 4 else self.piece(0, r)
        i = c * 6 + d * 3 + m
        return rcopy(
            self.part.at[p, self.half(h)], self.recv.at[i], self.ssem.at[i], self.rsem.at[i],
            self.at.along(self.first if c < 4 else self.second, step),
        )

    def add(self, p, h, others):
        @pl.loop(0, self.rows // 32)
        def _(i):
            rows = pl.ds(pl.multiple_of(self.base + h * self.rows + i * 32, 32), 32)
            here = pl.ds(pl.multiple_of(i * 32, 32), 32)
            total = self.part[p, rows, :].astype(f32)
            for o in others:
                total += self.recv[o, here, :].astype(f32)
            self.part[p, rows, :] = total.astype(bf16)

    def start(self, c):
        for m in (0, 1):
            for d in (0, 1):
                self.copy(c, d, m).start()

    def middle(self, c):
        for d in (0, 1):
            self.copy(c, d, 0).wait_recv()
            r = 1 - 2 * d
            p = self.piece(r, c) if c < 4 else self.piece(0, r)
            self.add(p, d, (c * 6 + d * 3,))
            self.copy(c, d, 2).start()

    def end(self, c):
        for d in (0, 1):
            for m in (1, 2):
                self.copy(c, d, m).wait_recv()
        p = self.piece(0, c) if c < 4 else self.piece(0, 0)
        self.add(p, 0, (c * 6 + 2, c * 6 + 4))
        self.add(p, 1, (c * 6 + 1, c * 6 + 5))

    def start_all(self):
        for c in (2, 1, 3, 0):
            self.start(c)

    def middle_all(self):
        for c in (2, 1, 3, 0):
            self.middle(c)

    def end_all(self):
        for c in (2, 1, 3, 0):
            self.end(c)
        self.start(4)

    def last(self):
        self.middle(4)
        self.end(4)

    def finish(self):
        for c in range(5):
            for d in (0, 1):
                for m in range(3):
                    self.copy(c, d, m).wait_send()


PLANE_SEMS = 30


class PlaneGather:
    def __init__(self, at, view, first, second, ssem, rsem):
        self.at, self.view, self.first, self.second = at, view, first, second
        self.ssem, self.rsem = ssem, rsem

    def copy(self, c, d, m, incoming):
        step = 1 - 2 * d
        h = d if m in (0, 2) else 1 - d
        back = (-step if m == 2 else 0) - (step if incoming else 0)
        a, b = (back, 0) if c == 4 else (c, back)
        p = self.at.piece(**{self.first: a, self.second: b})
        ref = self.view(p, h)
        i = c * 6 + d * 3 + m
        axis = self.first if c == 4 else self.second
        return rcopy(ref, ref, self.ssem.at[i], self.rsem.at[i], self.at.along(axis, step))

    def start(self, c):
        for m in (0, 1):
            for d in (0, 1):
                self.copy(c, d, m, False).start()

    def middle(self, c):
        for d in (0, 1):
            self.copy(c, d, 0, True).wait_recv()
            self.copy(c, d, 2, False).start()

    def arrive(self, c, m):
        for d in (0, 1):
            self.copy(c, d, m, True).wait_recv()

    def step0(self):
        self.start(4)
        self.start(0)

    def step1(self):
        self.middle(4)
        self.arrive(4, 1)
        self.start(3)
        self.start(1)

    def step2(self):
        self.middle(0)
        self.arrive(4, 2)
        self.start(2)

    def step3(self):
        for c in (3, 1, 2):
            self.middle(c)

    def step4(self):
        for c in range(4):
            self.arrive(c, 1)
            self.arrive(c, 2)
        for c in range(5):
            for d in (0, 1):
                for m in range(3):
                    self.copy(c, d, m, False).wait_send()


def dot_nt(a, b):
    return lax.dot_general(a, b, (((1,), (1,)), ((), ())), preferred_element_type=f32)


def dot_nn(a, b):
    return lax.dot_general(a, b, (((1,), (0,)), ((), ())), preferred_element_type=f32)


def dot_tn(a, b):
    return lax.dot_general(a, b, (((0,), (0,)), ((), ())), preferred_element_type=f32)


Q0, O0, G0, U0, D0, ROWS = 0, 384, 640, 1344, 2048, 2752
SCALE = HD**-0.5


def rotate(u, cosine, sine, sign):
    a, b = u[:32], u[32:]
    s = sine * sign
    return jnp.concatenate([a * cosine - b * s, b * cosine + a * s], axis=0)


def mask_bias(bounds, n):
    key = lax.broadcasted_iota(jnp.int32, (n, 128), 0)
    own, trunk, start, b0, b1 = [bounds[i : i + 1, :] for i in range(5)]
    keep = (key <= own) & ((key < trunk) | (key >= start) | ((key >= b0) & (key < b1)))
    return jnp.where(keep, 0.0, masked_score)


def heads_side_by_side(ref, t, y):
    return jnp.concatenate([ref[t, 64 * h : 64 * h + 64, 128 * y : 128 * y + 128] for h in range(4)], axis=1)


def tree_keys(kvb, kvt, kvn, t):
    for y in range(4):
        for z in range(2):
            b = 2 * y + z
            blk = kvb[t, y, z]
            kvt[:, 128 * b : 128 * b + 128] = blk
            kvn[128 * b : 128 * b + 128, :] = blk.astype(f32).T.astype(bf16)


def forward_kernel(
    hat, x, cot, wcol, wo, wd, cosine, sine, bounds,
    hat_out, cot_all, w_all, q_out, kvb, att, lse, hidden, hat2_all,
    hat_all, wqo, part, sib, recv, kvt, kvn, own2,
    hsem_s, hsem_r, csem_s, csem_r, gsem_s, gsem_r, psem_s, psem_r, rsem_s, rsem_r,
    colsem_s, colsem_r, rowsem_s, rowsem_r, kvsem_s, kvsem_r, lsem,
):
    at = Place()
    k, y, zl = at.k, at.y, at.zl
    own8 = at.zh * 4 + at.x
    is_src = own8 // 2 == y
    kd = at.x % 2
    both = jnp.where(is_src & (kd == k), 1, 0)
    src_n = jnp.where(is_src, 1, 0)
    j = 2 * y + k
    jz, jx = (j // 4) * 2 + zl, j % 4
    zpeer = at.device(z=at.z + 1 - 2 * zl)

    piece = at.piece()
    lanes = pl.ds(pl.multiple_of(piece * 128, 128), 128)
    greet([at.sibling()] + [at.along(a, r) for a in ("x", "z", "y") for r in (1, -1)])
    for s in range(2):
        mine = (jz == at.z) & (jx == at.x) & (k == s)

        @pl.when(jnp.logical_not(mine))
        def _():
            greet([at.device(z=jz, x=jx, k=s)])

    def row_dest(t):
        q = (own8 + t) % 8
        z = (q // 4) * 2 + zl
        return at.device(z=z, x=q % 4, k=kd), at.piece_of(z, q % 4)

    @pl.when(is_src)
    def _():
        for t in range(8):
            dev, _ = row_dest(t)
            if t == 0:

                @pl.when(kd != k)
                def _():
                    greet([dev])
            else:
                greet([dev])

    await_greetings(7 + (2 - both) + src_n * 8 - both * src_n)

    ring_h = RingGather(at, hat, hat_all, hsem_s, hsem_r, lsem.at[0])
    ring_c = RingGather(at, cot, cot_all, csem_s, csem_r, lsem.at[1])
    ring_2 = RingGather(at, own2, hat2_all, gsem_s, gsem_r, lsem.at[3])
    red = RingReduce(at, part, sib, recv, rsem_s, rsem_r)

    cols = ((0, 384, wqo, Q0), (384, 1408, w_all, G0))
    rows = ((wo, wqo, O0, 128), (wd, w_all, D0, 352))

    def col_send(i):
        s0, n, dst, d0 = cols[i]
        return rcopy(
            wcol.at[1 - k, pl.ds(s0, n)], dst.at[pl.ds(d0, n), lanes], colsem_s.at[i], colsem_r.at[i], at.sibling()
        )

    def col_keep(i):
        s0, n, dst, d0 = cols[i]
        return pltpu.make_async_copy(wcol.at[k, pl.ds(s0, n)], dst.at[pl.ds(d0, n), lanes], colsem_r.at[i])

    def row_send(i, t):
        src, dst, d0, n = rows[i]
        dev, p = row_dest(t)
        there = pl.ds(pl.multiple_of(p * 128, 128), 128)
        return rcopy(
            src.at[:, there], dst.at[pl.ds(pl.multiple_of(d0 + k * n, 16), n), there],
            rowsem_s.at[i, t], rowsem_r.at[i, k], dev,
        )

    def row_keep(i):
        src, dst, d0, n = rows[i]
        return pltpu.make_async_copy(
            src.at[:, lanes], dst.at[pl.ds(pl.multiple_of(d0 + k * n, 16), n), lanes], rowsem_r.at[i, k]
        )

    def row_in(i, s):
        src, dst, d0, n = rows[i]
        there = dst.at[pl.ds(d0 + s * n, n), lanes]
        return rcopy(there, there, rowsem_s.at[i, s], rowsem_r.at[i, s], at.device(z=jz, x=jx, k=s))

    @pl.when(k == zl)
    def _():
        for i in range(2):
            col_send(i).start()
            col_keep(i).start()

    ring_h.start()

    @pl.when(is_src)
    def _():
        for i in range(2):
            for t in range(1, 8):
                row_send(i, t).start()

            @pl.when(kd == k)
            def _():
                row_keep(i).start()

            @pl.when(kd != k)
            def _():
                row_send(i, 0).start()

    def view(ref, r0, n):
        return lambda p, h: ref.at[pl.ds(r0 + h * (n // 2), n // 2), pl.ds(pl.multiple_of(p * 128, 128), 128)]

    planes = [
        PlaneGather(at, view(ref, r0, n), *order, psem_s.at[i], psem_r.at[i])
        for i, (ref, r0, n, order) in enumerate(
            (
                (wqo, Q0, 192, ("x", "z")),
                (wqo, Q0 + 192, 192, ("z", "x")),
                (wqo, O0, 256, ("z", "x")),
                (w_all, G0, 704, ("x", "z")),
                (w_all, U0, 704, ("z", "x")),
                (w_all, D0, 352, ("x", "z")),
                (w_all, D0 + 352, 352, ("z", "x")),
            )
        )
    ]
    pq, po, bulk = planes[:2], planes[2], planes[3:]
    col_keep(0).wait()
    for p in pq:
        p.step0()
    for s in range(2):
        row_in(0, s).wait_recv()
    po.step0()
    ring_h.step(0)
    for p in pq:
        p.step1()
    po.step1()
    ring_h.step(1)
    for p in pq:
        p.step2()
    po.step2()
    for p in pq:
        p.step3()
    po.step3()
    col_keep(1).wait()
    for p in bulk[:2]:
        p.step0()
    for s in range(2):
        row_in(1, s).wait_recv()
    for p in bulk[2:]:
        p.step0()
    ring_h.step(2)
    ring_h.finish()
    ring_c.start()
    for p in pq:
        p.step4()

    def project(t, c):
        h = hat_all[pl.ds(4 * t + 2 * c, 2)].reshape(256, D)
        proj = dot_nt(wqo[Q0 : Q0 + 384, :], h)
        col = pl.ds(pl.multiple_of(256 * c, 256), 256)
        co, si = cosine[t, :, col], sine[t, :, col]
        for head in range(4):
            u = rotate(proj[64 * head : 64 * head + 64], co, si, 1.0)
            q_out[t, 64 * head : 64 * head + 64, col] = (u * SCALE).astype(bf16)
        kv = jnp.concatenate([rotate(proj[256:320], co, si, 1.0), proj[320:]], axis=0).astype(bf16)
        for b in range(2):
            kvb[t, 2 * c + b, zl] = kv[:, 128 * b : 128 * b + 128]

    def kv_send():
        ref = kvb.at[k, :, zl]
        return rcopy(ref, ref, kvsem_s.at[0], kvsem_r.at[0], zpeer)

    def kv_in():
        ref = kvb.at[k, :, 1 - zl]
        return rcopy(ref, ref, kvsem_s.at[0], kvsem_r.at[0], zpeer)

    def kv_relay(kk):
        ref = kvb.at[kk, :, 1 - zl]
        return rcopy(ref, ref, kvsem_s.at[1], kvsem_r.at[1], at.sibling())

    pl.loop(0, 2)(functools.partial(project, k))
    kv_send().start()
    pl.loop(0, 2)(functools.partial(project, 1 - k))
    h_out = pltpu.make_async_copy(hat_all, hat_out, lsem.at[0])
    h_out.start()
    ring_c.step(0)
    kv_in().wait_recv()
    kv_relay(k).start()
    for p in bulk:
        p.step1()
    po.step4()
    w_out_copy = pltpu.make_async_copy(wqo, w_all.at[pl.ds(0, G0)], lsem.at[2])
    w_out_copy.start()
    kv_relay(1 - k).wait_recv()

    def attend(t):
        tree_keys(kvb, kvt, kvn, t)
        for b in range(4):
            n = 256 * (b + 1)
            col = slice(128 * b, 128 * b + 128)
            qs = heads_side_by_side(q_out, t, b)
            qs = jnp.concatenate([qs, jnp.zeros_like(qs)], axis=0)
            bias = mask_bias(bounds[t, :, col], n)
            s = dot_nn(kvn[:n, :], qs) + jnp.concatenate([bias] * 4, axis=1)
            peak = jnp.max(s, axis=0, keepdims=True)
            e = jnp.exp(s - peak)
            total = jnp.sum(e, axis=0, keepdims=True)
            o = dot_nn(kvt[64:128, :n], e.astype(bf16)) / total
            log_total = peak + jnp.log(total)
            for head in range(4):
                c = slice(128 * head, 128 * head + 128)
                att[t, 64 * head : 64 * head + 64, col] = o[:, c].astype(bf16)
                lse[t, head : head + 1, col] = log_total[:, c]

        @pl.loop(0, 2)
        def _(i):
            a = att[t, :, pl.ds(pl.multiple_of(256 * i, 256), 256)]
            r = dot_tn(a, wqo[O0 : O0 + 256, :]).astype(bf16)
            part[pl.ds(4 * t + 2 * i, 2)] = r.reshape(2, 128, D)

    attend(1 - k)
    red.cross_all()
    ring_c.step(1)
    attend(k)
    red.first()
    for p in bulk:
        p.step2()
    ring_c.step(2)
    red.second()
    for p in bulk:
        p.step3()

    def emit(rows, total):
        h = x[rows, :].astype(f32) + total
        hidden[rows, :] = h
        inv = lax.rsqrt(jnp.mean(h * h, axis=1, keepdims=True) + epsilon)
        own2[rows, :] = (h * inv).astype(bf16)

    red.collect(emit)
    ring_2.start()
    ring_c.finish()
    ring_2.step(0)
    ring_2.step(1)
    for p in bulk[:2]:
        p.step4()
    ring_2.step(2)
    for p in bulk[2:]:
        p.step4()
    ring_2.finish()
    red.finish()
    h_out.wait()
    w_out_copy.wait()
    kv_send().wait_send()
    kv_relay(k).wait_send()

    @pl.when(k == zl)
    def _():
        for i in range(2):
            col_send(i).wait_send()

    @pl.when(is_src)
    def _():
        for i in range(2):
            for t in range(1, 8):
                row_send(i, t).wait_send()

            @pl.when(kd != k)
            def _():
                row_send(i, 0).wait_send()


def forward_pass(hat, x, cot, wcol, wo, wd, cosine, sine, bounds):
    shape = jax.ShapeDtypeStruct
    dma = pltpu.SemaphoreType.DMA
    return pl.pallas_call(
        forward_kernel,
        name="forward_pass",
        out_shape=(
            shape((8, 128, D), bf16),
            shape((8, 128, D), bf16),
            shape((ROWS, D), bf16),
            shape((2, 256, 512), bf16),
            shape((2, 4, 2, 128, 128), bf16),
            shape((2, 256, 512), bf16),
            shape((2, 8, 512), f32),
            shape((128, D), f32),
            shape((8, 128, D), bf16),
        ),
        in_specs=[VM] * 9,
        out_specs=[ANY, ANY, ANY, VM, VM, VM, VM, VM, ANY],
        scratch_shapes=[
            pltpu.VMEM((8, 128, D), bf16),
            pltpu.VMEM((G0, D), bf16),
            pltpu.VMEM((8, 128, D), bf16),
            pltpu.VMEM((4, 128, D), bf16),
            pltpu.VMEM((6, 64, D), bf16),
            pltpu.VMEM((128, 1024), bf16),
            pltpu.VMEM((1024, 128), bf16),
            pltpu.VMEM((128, D), bf16),
        ]
        + [dma((RING_SEMS,))] * 6
        + [dma((7, PLANE_SEMS))] * 2
        + [dma((REDUCE_SEMS,))] * 2
        + [dma((2,)), dma((2,)), dma((2, 8)), dma((2, 2)), dma((2,)), dma((2,)), dma((4,))],
        compiler_params=pltpu.CompilerParams(
            collective_id=0, has_side_effects=True, vmem_limit_bytes=56 * 2**20
        ),
    )(hat, x, cot, wcol, wo, wd, cosine, sine, bounds)


def mlp_kernel(
    hat2_hbm, cot_hbm, w_hbm, hidden, cot,
    mixed, ghidden, gb_all, up_part, sum_g, sum_d,
    hat2, cotv, wgu, wdn, part, sib, recv, innert, dgu, pd, pg, pu, precv_d, precv_g, own_gb, mpart, msib, mrecv,
    rsem_s, rsem_r, msem_s, msem_r, gsem_s, gsem_r, psem_s, psem_r, lsem,
):
    at = Place()
    k, y = at.k, at.y
    loads = [
        pltpu.make_async_copy(src, dst, lsem.at[i])
        for i, (src, dst) in enumerate(
            (
                (w_hbm.at[pl.ds(G0, 1408)], wgu),
                (hat2_hbm, hat2),
                (w_hbm.at[pl.ds(D0, 704)], wdn),
                (cot_hbm, cotv),
            )
        )
    ]
    for c in loads:
        c.start()
    greet([at.sibling()] + [at.along(a, r) for a in ("x", "z", "y") for r in (1, -1)])
    await_greetings(7)
    red = RingReduce(at, part, sib, recv, rsem_s, rsem_r)
    redm = RingReduce(at, mpart, msib, mrecv, msem_s, msem_r)
    ring = RingGather(at, own_gb, gb_all, gsem_s, gsem_r, lsem.at[0])
    pr_d = PlaneReduce(at, pd, precv_d, "x", "z", psem_s.at[0], psem_r.at[0])
    pr_g = PlaneReduce(at, pg, precv_g, "z", "x", psem_s.at[1], psem_r.at[1])
    def columns(t, i):
        slot = 4 * t + 2 * i
        return slot, pl.ds(pl.multiple_of(slot * 128, 256), 256)

    loads[0].wait()
    loads[1].wait()

    @pl.loop(0, 4)
    def _(i):
        slot, cols = columns(0, i)
        both = dot_nt(wgu[...], hat2[pl.ds(slot, 2)].reshape(256, D))
        gate, up = both[:FJ], both[FJ:]
        sig = jax.nn.sigmoid(gate)
        silu = gate * sig
        innert[:, cols] = (silu * up).astype(bf16)
        dgu[:FJ, cols] = (up * sig * (1.0 + gate * (1.0 - sig))).astype(bf16)
        dgu[FJ:, cols] = silu.astype(bf16)

    loads[2].wait()

    def mix(t):
        @pl.loop(0, 2)
        def _(i):
            slot, cols = columns(t, i)
            r = dot_tn(innert[:, cols], wdn[...]).astype(bf16)
            mpart[pl.ds(slot, 2)] = r.reshape(2, 128, D)

    def mlp_back(t):
        @pl.loop(0, 2)
        def _(i):
            slot, cols = columns(t, i)
            gi = dot_nt(wdn[...], cotv[pl.ds(slot, 2)].reshape(256, D))
            dgu[:FJ, cols] = (gi * dgu[:FJ, cols].astype(f32)).astype(bf16)
            dgu[FJ:, cols] = (gi * dgu[FJ:, cols].astype(f32)).astype(bf16)

        @pl.loop(0, 2)
        def _(i):
            slot, cols = columns(t, i)
            r = dot_tn(dgu[:, cols], wgu[...]).astype(bf16)
            part[pl.ds(slot, 2)] = r.reshape(2, 128, D)

    def weight_grad(left, right, out):
        @pl.loop(0, 4)
        def _(i):
            cols = pl.ds(pl.multiple_of(512 * i, 512), 512)
            g = dot_nn(left[...], right[:, :, cols].reshape(1024, 512)).astype(bf16)
            for q in range(4):
                out[4 * i + q] = g[:, 128 * q : 128 * q + 128]

    loads[3].wait()
    mix(1 - k)
    redm.cross_all()
    mix(k)
    redm.first()
    mlp_back(1 - k)
    red.cross_all()
    redm.second()
    mlp_back(k)
    red.first()
    weight_grad(innert, cotv, pd)
    pr_d.start_all()
    red.second()

    def emit_mixed(rows, total):
        mixed[rows, :] = (hidden[rows, :] + total).astype(bf16)

    redm.collect(emit_mixed)
    weight_grad(dgu.at[:FJ], hat2, pg)
    pr_g.start_all()
    pr_d.middle_all()

    def emit(rows, total):
        h = hidden[rows, :]
        inv = lax.rsqrt(jnp.mean(h * h, axis=1, keepdims=True) + epsilon)
        hat = h * inv
        g = cot[rows, :].astype(f32) + inv * (total - hat * jnp.mean(total * hat, axis=1, keepdims=True))
        ghidden[rows, :] = g
        own_gb[rows, :] = g.astype(bf16)

    red.collect(emit)
    ring.start()
    pr_g.middle_all()

    ring.step(0)
    weight_grad(dgu.at[FJ:], hat2, pu)
    u_out = pltpu.make_async_copy(pu, up_part, lsem.at[4])
    u_out.start()
    ring.step(1)
    pr_d.end_all()
    pr_g.end_all()
    red.finish()
    ring.step(2)

    pr_d.last()
    d_out = pltpu.make_async_copy(pd.at[at.piece()], sum_d, lsem.at[2])
    d_out.start()
    pr_g.last()
    g_out = pltpu.make_async_copy(pg.at[at.piece()], sum_g, lsem.at[3])
    g_out.start()
    ring.finish()
    pr_d.finish()
    pr_g.finish()
    redm.finish()
    u_out.wait()
    d_out.wait()
    g_out.wait()


def mlp_pass(hat2_all, cot_all, w_all, hidden, cot):
    shape = jax.ShapeDtypeStruct
    dma = pltpu.SemaphoreType.DMA
    block = pltpu.VMEM((8, 128, D), bf16)
    return pl.pallas_call(
        mlp_kernel,
        name="mlp_pass",
        out_shape=(
            shape((128, D), bf16),
            shape((128, D), f32),
            shape((8, 128, D), bf16),
            shape((16, FJ, 128), bf16),
            shape((FJ, 128), bf16),
            shape((FJ, 128), bf16),
        ),
        in_specs=[ANY, ANY, ANY, VM, VM],
        out_specs=[VM, VM, ANY, ANY, ANY, ANY],
        scratch_shapes=[
            block, block,
            pltpu.VMEM((2 * FJ, D), bf16), pltpu.VMEM((FJ, D), bf16),
            block,
            pltpu.VMEM((4, 128, D), bf16),
            pltpu.VMEM((6, 64, D), bf16),
            pltpu.VMEM((FJ, 1024), bf16), pltpu.VMEM((2 * FJ, 1024), bf16),
            pltpu.VMEM((16, FJ, 128), bf16), pltpu.VMEM((16, FJ, 128), bf16), pltpu.VMEM((16, FJ, 128), bf16),
            pltpu.VMEM((30, FJ // 2, 128), bf16), pltpu.VMEM((30, FJ // 2, 128), bf16),
            pltpu.VMEM((128, D), bf16),
            block, pltpu.VMEM((4, 128, D), bf16), pltpu.VMEM((6, 64, D), bf16),
            dma((REDUCE_SEMS,)), dma((REDUCE_SEMS,)), dma((REDUCE_SEMS,)), dma((REDUCE_SEMS,)), dma((RING_SEMS,)), dma((RING_SEMS,)),
            dma((2, PLANE_SEMS)), dma((2, PLANE_SEMS)), dma((5,)),
        ],
        compiler_params=pltpu.CompilerParams(
            collective_id=1, has_side_effects=True, vmem_limit_bytes=62 * 2**20
        ),
    )(hat2_all, cot_all, w_all, hidden, cot)


class ColSpread:
    def __init__(self, at, src, dst, ssem, rsem):
        self.at, self.src, self.dst, self.ssem, self.rsem = at, src, dst, ssem, rsem
        self.home = at.k == at.zl
        self.there = dst.at[2 * at.y + at.k]

    def near(self):
        return rcopy(self.src, self.there, self.ssem.at[6], self.rsem.at[6 + self.at.k], self.at.sibling())

    def far(self):
        at = self.at
        dev = at.device(z=at.z + 1 - 2 * at.zl, k=at.zl)
        return rcopy(self.src, self.there, self.ssem.at[7], self.rsem.at[6 + at.k], dev)

    def start(self):
        self.far().start()

        @pl.when(self.home)
        def _():
            pltpu.make_async_copy(self.src, self.there, self.rsem.at[6 + self.at.k]).start()

        @pl.when(jnp.logical_not(self.home))
        def _():
            self.near().start()

    def copy(self, d, m, incoming):
        step = 1 - 2 * d
        h = d if m in (0, 2) else 1 - d
        back = (-step if m == 2 else 0) - (step if incoming else 0)
        ref = self.dst.at[2 * self.at.moved("y", back) + h]
        i = d * 3 + m
        return rcopy(ref, ref, self.ssem.at[i], self.rsem.at[i], self.at.along("y", step))

    def ring(self):
        for h in range(2):
            pltpu.make_async_copy(self.src, self.dst.at[2 * self.at.y + h], self.rsem.at[6 + h]).wait()
        for m in (0, 1):
            for d in (0, 1):
                self.copy(d, m, False).start()

    def middle(self):
        for d in (0, 1):
            self.copy(d, 0, True).wait_recv()
            self.copy(d, 2, False).start()

    def finish(self):
        for d in (0, 1):
            for m in (1, 2):
                self.copy(d, m, True).wait_recv()
        for d in (0, 1):
            for m in range(3):
                self.copy(d, m, False).wait_send()
        self.far().wait_send()

        @pl.when(jnp.logical_not(self.home))
        def _():
            self.near().wait_send()


class RowSpread:
    def __init__(self, at, src, buf, dst, ssem, rsem):
        self.at, self.src, self.buf, self.dst, self.ssem, self.rsem = at, src, buf, dst, ssem, rsem
        self.m = dst.shape[0]
        self.lanes = pl.ds(pl.multiple_of(at.piece() * 128, 128), 128)

    def keep(self, h):
        return pltpu.make_async_copy(self.src.at[pl.ds(h * self.m, self.m)], self.buf.at[self.at.y, h], self.ssem.at[6 + h])

    def start(self):
        for h in range(2):
            self.keep(h).start()
        for m in (0, 1):
            for d in (0, 1):
                self.copy(d, m, False).start()

    def copy(self, d, m, incoming):
        step = 1 - 2 * d
        h = d if m in (0, 2) else 1 - d
        back = (-step if m == 2 else 0) - (step if incoming else 0)
        ref = self.buf.at[self.at.moved("y", back), h]
        i = d * 3 + m
        src = ref if incoming or m == 2 else self.src.at[pl.ds(h * self.m, self.m)]
        return rcopy(src, ref, self.ssem.at[i], self.rsem.at[i], self.at.along("y", step))

    def middle(self):
        for d in (0, 1):
            self.copy(d, 0, True).wait_recv()
            self.copy(d, 2, False).start()

    def each(self, f, g):
        at = self.at
        for y in range(4):
            for dz in (1, 0):
                for c in range(2):
                    if dz:
                        f(y, dz, c)
                    else:
                        mine = (at.zh == y // 2) & (at.x == 2 * (y % 2) + at.k) & (at.k == c)
                        pl.when(mine)(functools.partial(g, y, c))
                        pl.when(jnp.logical_not(mine))(functools.partial(f, y, dz, c))

    def device(self, y, dz, c):
        at = self.at
        return at.device(z=2 * (y // 2) + (at.zl + dz) % 2, x=2 * (y % 2) + at.k, k=c)

    def push_copy(self, y, dz, c):
        return rcopy(
            self.buf.at[y, c], self.dst.at[:, self.lanes], self.ssem.at[8 + (y * 2 + dz) * 2 + c],
            self.rsem.at[6 + self.at.piece()], self.device(y, dz, c),
        )

    def push(self):
        for h in range(2):
            self.keep(h).wait()
        for d in (0, 1):
            for m in (1, 2):
                self.copy(d, m, True).wait_recv()

        def local(y, c):
            pltpu.make_async_copy(
                self.buf.at[y, c], self.dst.at[:, self.lanes], self.rsem.at[6 + self.at.piece()]
            ).start()

        self.each(lambda y, dz, c: self.push_copy(y, dz, c).start(), local)

    def finish(self):
        for p in range(16):
            pltpu.make_async_copy(self.buf.at[0, 0], self.dst.at[:, pl.ds(p * 128, 128)], self.rsem.at[6 + p]).wait()
        for d in (0, 1):
            for m in range(3):
                self.copy(d, m, False).wait_send()
        self.each(lambda y, dz, c: self.push_copy(y, dz, c).wait_send(), lambda y, c: None)

    def greet(self):
        at = self.at
        self.each(lambda y, dz, c: greet([self.device(y, dz, c)]), lambda y, c: None)
        for p in range(16):
            z, x = (p // 8) * 2 + p % 2, (p // 2) % 4
            mine = (at.z == z) & (at.x == x) & (at.k == at.x % 2)

            @pl.when(jnp.logical_not(mine))
            def _():
                greet([at.device(z=z, x=x, k=at.x % 2)])

        return 2 * (16 - jnp.where(at.x % 2 == at.k, 1, 0))


def backward_kernel(
    gb_hbm, hat_hbm, w_hbm, q, kvb, att, lse, cosine, sine, bounds, x, ghidden, up_part, sum_g, sum_d,
    grad_tokens, out_q, out_g, out_u, out_o, out_d,
    gb, hat, wqo, pu, pq, po, precv_u, precv_q, precv_o, part, sib, recv,
    datt, dproj, dkv, dkv_far, dkv_got, kvt, kvn, buf_o, buf_d,
    rsem_s, rsem_r, psem_s, psem_r, xsem_s, xsem_r, csem_s, csem_r, wsem_s, wsem_r, lsem,
):
    at = Place()
    k, y, zl = at.k, at.y, at.zl
    zpeer = at.device(z=at.z + 1 - 2 * zl)
    loads = [
        pltpu.make_async_copy(src, dst, lsem.at[i])
        for i, (src, dst) in enumerate(
            (
                (w_hbm.at[pl.ds(0, G0)], wqo),
                (gb_hbm, gb),
                (up_part, pu),
                (hat_hbm, hat),
            )
        )
    ]
    for c in loads:
        c.start()
    cols_q = ColSpread(at, pq.at[at.piece()], out_q, csem_s.at[0], csem_r.at[0])
    cols_g = ColSpread(at, sum_g, out_g, csem_s.at[1], csem_r.at[1])
    cols_u = ColSpread(at, pu.at[at.piece()], out_u, csem_s.at[2], csem_r.at[2])
    rows_o = RowSpread(at, po.at[at.piece()], buf_o, out_o, wsem_s.at[0], wsem_r.at[0])
    rows_d = RowSpread(at, sum_d, buf_d, out_d, wsem_s.at[1], wsem_r.at[1])
    greet([at.sibling(), at.device(z=at.z + 1 - 2 * zl, k=1 - k)])
    greet([at.along(a, r) for a in ("x", "z", "y") for r in (1, -1)])
    await_greetings(8 + rows_o.greet())

    red = RingReduce(at, part, sib, recv, rsem_s, rsem_r)
    pr_u = PlaneReduce(at, pu, precv_u, "x", "z", psem_s.at[0], psem_r.at[0])
    pr_q = PlaneReduce(at, pq, precv_q, "z", "x", psem_s.at[1], psem_r.at[1])
    pr_o = PlaneReduce(at, po, precv_o, "z", "x", psem_s.at[2], psem_r.at[2])
    cols_g.start()
    rows_d.start()
    loads[2].wait()
    pr_u.start_all()
    loads[0].wait()
    loads[1].wait()

    @pl.loop(0, 4)
    def _(i):
        g = gb[pl.ds(2 * i, 2)].reshape(256, D)
        r = dot_nt(wqo[O0 : O0 + 256, :], g)
        datt[i // 2, :, pl.ds(pl.multiple_of(256 * (i % 2), 256), 256)] = r.astype(bf16)

    cols_g.ring()

    def weight_grad(left, right, ref):
        @pl.loop(0, 4)
        def _(i):
            cols = pl.ds(pl.multiple_of(512 * i, 512), 512)
            g = dot_nn(left[0], right[0:4, :, cols].reshape(512, 512))
            g += dot_nn(left[1], right[4:8, :, cols].reshape(512, 512))
            g = g.astype(bf16)
            for s in range(4):
                ref[4 * i + s] = g[:, 128 * s : 128 * s + 128]

    weight_grad(att, gb, po)
    pr_o.start_all()

    def attend(t):
        tree_keys(kvb, kvt, kvn, t)
        for b in (3, 2, 1, 0):
            n = 256 * (b + 1)
            col = slice(128 * b, 128 * b + 128)
            qs = heads_side_by_side(q, t, b)
            dos = heads_side_by_side(datt, t, b)
            zero = jnp.zeros_like(qs)
            bias = mask_bias(bounds[t, :, col], n)
            log_total = jnp.concatenate([lse[t, h : h + 1, col] for h in range(4)], axis=1)
            s = dot_nn(kvn[:n, :], jnp.concatenate([qs, zero], axis=0)) + jnp.concatenate([bias] * 4, axis=1)
            prob = jnp.exp(s - log_total)
            dprob = dot_nn(kvn[:n, :], jnp.concatenate([zero, dos], axis=0))
            inner = jnp.sum(prob * dprob, axis=0, keepdims=True)
            ds = (prob * (dprob - inner)).astype(bf16)
            dq = dot_nn(kvt[0:64, :n], ds) * SCALE
            co, si = cosine[t, :, col], sine[t, :, col]
            for h in range(4):
                u = rotate(dq[:, 128 * h : 128 * h + 128], co, si, -1.0)
                dproj[t, 64 * h : 64 * h + 64, col] = u.astype(bf16)
            dk = dot_nt(qs, ds)
            dv = dot_nt(dos, prob.astype(bf16))
            for c in range(2 * (b + 1)):
                blk = slice(128 * c, 128 * c + 128)
                if b == 3:
                    dkv[t, c // 2, c % 2, :64, :] = dk[:, blk]
                    dkv[t, c // 2, c % 2, 64:, :] = dv[:, blk]
                else:
                    dkv[t, c // 2, c % 2, :64, :] += dk[:, blk]
                    dkv[t, c // 2, c % 2, 64:, :] += dv[:, blk]
        for b in range(4):
            dkv_far[t, b] = dkv[t, b, 1 - zl].astype(bf16)

    def far_copy(t, s):
        return rcopy(dkv_far.at[t], dkv_got.at[t], xsem_s.at[s], xsem_r.at[s], zpeer)

    def project(t, s):
        far_copy(t, s).wait_recv()
        for b in range(4):
            col = slice(128 * b, 128 * b + 128)
            total = dkv[t, b, zl] + dkv_got[t, b].astype(f32)
            dk = rotate(total[:64], cosine[t, :, col], sine[t, :, col], -1.0)
            dproj[t, 256:320, col] = dk.astype(bf16)
            dproj[t, 320:384, col] = total[64:].astype(bf16)

        @pl.loop(0, 2)
        def _(i):
            a = dproj[t, :, pl.ds(pl.multiple_of(256 * i, 256), 256)]
            r = dot_tn(a, wqo[Q0 : Q0 + 384, :]).astype(bf16)
            part[pl.ds(4 * t + 2 * i, 2)] = r.reshape(2, 128, D)

    attend(1 - k)
    far_copy(1 - k, 0).start()
    rows_d.middle()
    pr_u.middle(2)
    pr_u.middle(1)
    attend(k)
    far_copy(k, 1).start()
    rows_d.push()
    project(1 - k, 0)
    red.cross_all()
    pr_u.middle(3)
    pr_u.middle(0)
    project(k, 1)
    red.first()
    pr_o.middle_all()
    cols_g.middle()
    loads[3].wait()
    weight_grad(dproj, hat, pq)
    pr_q.start_all()
    red.second()
    pr_u.end_all()
    pr_o.end_all()
    pr_q.middle_all()
    pr_u.last()
    cols_u.start()
    pr_o.last()
    rows_o.start()
    cols_u.ring()

    def emit(rows, total):
        h = x[rows, :].astype(f32)
        inv = lax.rsqrt(jnp.mean(h * h, axis=1, keepdims=True) + epsilon)
        hat1 = h * inv
        g = ghidden[rows, :] + inv * (total - hat1 * jnp.mean(total * hat1, axis=1, keepdims=True))
        grad_tokens[rows, :] = g

    pr_q.end_all()
    rows_o.middle()
    red.collect(emit)
    pr_q.last()
    cols_q.start()
    cols_u.middle()
    rows_o.push()
    cols_q.ring()
    cols_g.finish()
    rows_d.finish()
    cols_q.middle()
    cols_u.finish()
    rows_o.finish()
    cols_q.finish()
    for s, t in ((0, 1 - k), (1, k)):
        far_copy(t, s).wait_send()
    red.finish()
    pr_u.finish()
    pr_o.finish()
    pr_q.finish()


def backward_pass(*args):
    shape = jax.ShapeDtypeStruct
    dma = pltpu.SemaphoreType.DMA
    block = pltpu.VMEM((8, 128, D), bf16)
    return pl.pallas_call(
        backward_kernel,
        name="backward_pass",
        out_shape=(
            shape((128, D), f32),
            shape((8, 384, 128), bf16),
            shape((8, FJ, 128), bf16),
            shape((8, FJ, 128), bf16),
            shape((128, D), bf16),
            shape((352, D), bf16),
        ),
        in_specs=[ANY, ANY, ANY, VM, VM, VM, VM, VM, VM, VM, VM, VM, ANY, VM, VM],
        out_specs=[VM] + [ANY] * 5,
        scratch_shapes=[
            block, block, pltpu.VMEM((G0, D), bf16),
            pltpu.VMEM((16, FJ, 128), bf16), pltpu.VMEM((16, 384, 128), bf16), pltpu.VMEM((16, 256, 128), bf16),
            pltpu.VMEM((30, FJ // 2, 128), bf16), pltpu.VMEM((30, 192, 128), bf16), pltpu.VMEM((30, 128, 128), bf16),
            block, pltpu.VMEM((4, 128, D), bf16), pltpu.VMEM((6, 64, D), bf16),
            pltpu.VMEM((2, 256, 512), bf16),
            pltpu.VMEM((2, 384, 512), bf16),
            pltpu.VMEM((2, 4, 2, 128, 128), f32),
            pltpu.VMEM((2, 4, 128, 128), bf16),
            pltpu.VMEM((2, 4, 128, 128), bf16),
            pltpu.VMEM((128, 1024), bf16),
            pltpu.VMEM((1024, 128), bf16),
            pltpu.VMEM((4, 2, 128, 128), bf16),
            pltpu.VMEM((4, 2, 352, 128), bf16),
            dma((REDUCE_SEMS,)), dma((REDUCE_SEMS,)),
            dma((3, PLANE_SEMS)), dma((3, PLANE_SEMS)), dma((2,)), dma((2,)),
            dma((3, 8)), dma((3, 8)), dma((2, 24)), dma((2, 22)), dma((5,)),
        ],
        compiler_params=pltpu.CompilerParams(
            collective_id=2, has_side_effects=True, vmem_limit_bytes=62 * 2**20
        ),
    )(*args)


def finish_kernel(og, ou, oq, oo, od, wg, wu, wq, gain1, gain2, g_gate, g_up, g_qkv, g_out, g_down, s_one, s_two):
    i = pl.program_id(0)

    @pl.when(i == 0)
    def _():
        s_one[...] = jnp.zeros_like(s_one)
        s_two[...] = jnp.zeros_like(s_two)

    total = None
    for src, w, dst in ((og, wg, g_gate), (ou, wu, g_up)):
        raw = src[...].astype(f32).T
        dst[...] = raw * gain2[...]
        dot = jnp.sum(raw * w[...].astype(f32), axis=1, keepdims=True)
        total = dot if total is None else total + dot
    s_two[...] += total

    def qkv(raw, start):
        cols = pl.ds(start, 512)
        g_qkv[:, cols] = raw * gain1[...]
        s_one[...] += jnp.sum(raw * wq[:, cols].astype(f32), axis=1, keepdims=True)

    qkv(oq[pl.ds(2 * i, 2), :256, :].reshape(512, 128).astype(f32).T, pl.multiple_of(512 * i, 512))

    @pl.when(i == 3)
    def _():
        pairs = [oq[2 * g, 256:, :].astype(f32) + oq[2 * g + 1, 256:, :].astype(f32) for g in range(KVH)]
        qkv(jnp.concatenate([p[:64] for p in pairs] + [p[64:] for p in pairs], axis=0).T, 2048)

    g_out[...] = oo[...].astype(f32)
    g_down[...] = od[...].astype(f32)


def finish(og, ou, oq, oo, od, wg, wu, wq, gain1, gain2):
    shape = jax.ShapeDtypeStruct
    row = lambda i: (i, 0)
    col = lambda i: (0, i)
    whole = lambda i: (0, 0)
    d_row = lambda i: (jnp.minimum(i, 1), 0)
    return pl.pallas_call(
        finish_kernel,
        name="finish",
        grid=(4,),
        out_shape=(
            shape((128, FF), f32), shape((128, FF), f32), shape((128, 2560), f32), shape((128, D), f32), shape((352, D), f32),
            shape((128, 1), f32), shape((128, 1), f32),
        ),
        in_specs=[
            pl.BlockSpec((1408, 128), row),
            pl.BlockSpec((1408, 128), row),
            pl.BlockSpec((8, 384, 128), lambda i: (0, 0, 0)),
            pl.BlockSpec((32, D), row),
            pl.BlockSpec((176, D), d_row),
            pl.BlockSpec((128, 1408), col),
            pl.BlockSpec((128, 1408), col),
            pl.BlockSpec((128, 2560), whole),
            pl.BlockSpec((128, 1), whole),
            pl.BlockSpec((128, 1), whole),
        ],
        out_specs=(
            pl.BlockSpec((128, 1408), col),
            pl.BlockSpec((128, 1408), col),
            pl.BlockSpec((128, 2560), whole),
            pl.BlockSpec((32, D), row),
            pl.BlockSpec((176, D), d_row),
            pl.BlockSpec((128, 1), whole),
            pl.BlockSpec((128, 1), whole),
        ),
        compiler_params=pltpu.CompilerParams(vmem_limit_bytes=62 * 2**20),
    )(og, ou, oq, oo, od, wg, wu, wq, gain1, gain2)


def segment_bounds(lengths, offsets):
    ends = jnp.cumsum(lengths)
    starts = ends - lengths
    segment = jnp.sum((offsets[:, None] >= ends[None, :]).astype(jnp.int32), axis=1)
    seg_ids = np.arange(13)
    branch_of = jnp.asarray(np.where(seg_ids > 0, 1 + 3 * ((seg_ids - 1) // 3), 0), jnp.int32)
    onehot = segment[:, None] == jnp.asarray(seg_ids, jnp.int32)[None, :]

    def pick(values):
        return jnp.sum(jnp.where(onehot, values[None, :], 0), axis=1)

    table = np.zeros((13, 13), np.int32)
    for s in range(13):
        if s:
            table[s, 1 + 3 * ((s - 1) // 3)] = 1
        else:
            table[s, 0] = 1
    table = jnp.asarray(table)
    b0 = jnp.sum(table * starts[None, :], axis=1)
    b1 = jnp.sum(table * ends[None, :], axis=1)
    is_leaf = jnp.asarray((seg_ids > 0) & ((seg_ids - 1) % 3 > 0), jnp.int32)
    depth = jnp.where(jnp.asarray(seg_ids > 0), lengths[0], 0) + is_leaf * (b1 - b0)
    position = offsets - pick(starts) + pick(depth)
    trunk = jnp.broadcast_to(lengths[0], offsets.shape)
    return jnp.stack([offsets, trunk, pick(starts), pick(b0), pick(b1)], axis=1), position


def shards(tokens, cotangent, tree_lengths, gain_attn, w_qkv, w_out, gain_mlp, w_gate, w_up, w_down):
    at = Place()
    swapped = lax.ppermute(tree_lengths, "fsdp", [(f, f ^ 1) for f in range(16)])
    lengths = jnp.where(at.k == 0, jnp.stack([tree_lengths[0], swapped[0]]), jnp.stack([swapped[0], tree_lengths[0]]))
    offsets = (
        (2 * jnp.arange(4, dtype=jnp.int32)[:, None] + at.zl) * 128 + jnp.arange(128, dtype=jnp.int32)[None, :]
    ).reshape(512)
    b_a, p_a = segment_bounds(lengths[0], offsets)
    b_b, p_b = segment_bounds(lengths[1], offsets)
    bounds = jnp.pad(jnp.stack([b_a.T, b_b.T]), ((0, 0), (0, 3), (0, 0)))
    position = jnp.stack([p_a, p_b]).astype(f32)
    frequency = 10000.0 ** (-2.0 * jnp.arange(32, dtype=f32) / 64)
    angles = position[:, None, :] * frequency[None, :, None]
    cosine, sine = jnp.cos(angles), jnp.sin(angles)

    gain1 = gain_attn.astype(f32)[:, None]
    gain2 = gain_mlp.astype(f32)[:, None]

    def columns(w, start, n, gain):
        return (lax.dynamic_slice_in_dim(w, start, n, axis=1).astype(f32) * gain).astype(bf16).T

    q_cols = columns(w_qkv, at.y * 512, 512, gain1)
    k_cols = columns(w_qkv, 2048 + at.y * 64, 64, gain1)
    v_cols = columns(w_qkv, 2304 + at.y * 64, 64, gain1)
    g_cols = columns(w_gate, at.y * 2 * FJ, 2 * FJ, gain2)
    u_cols = columns(w_up, at.y * 2 * FJ, 2 * FJ, gain2)
    wcol = jnp.stack(
        [
            jnp.concatenate(
                [q_cols[256 * i : 256 * i + 256], k_cols, v_cols, g_cols[FJ * i : FJ * i + FJ], u_cols[FJ * i : FJ * i + FJ]]
            )
            for i in range(2)
        ]
    )

    inputs = tokens.astype(f32)
    inv1 = lax.rsqrt(jnp.mean(inputs * inputs, axis=-1, keepdims=True) + epsilon)
    hat1 = (inputs * inv1).astype(bf16)
    hat_all, cot_all, w_all, q, kvb, att, lse, hidden, hat2_all = forward_pass(
        hat1, tokens, cotangent, wcol, w_out, w_down, cosine, sine, bounds
    )
    mixed, ghidden, gb_all, up_part, sum_g, sum_d = mlp_pass(hat2_all, cot_all, w_all, hidden, cotangent)
    grad_tokens, oq, og, ou, oo, od = backward_pass(
        gb_all, hat_all, w_all, q, kvb, att, lse, cosine, sine, bounds, tokens, ghidden, up_part, sum_g, sum_d
    )
    g_gate, g_up, g_qkv, g_out, g_down, grad_gain1, grad_gain2 = finish(
        og.reshape(FF, 128), ou.reshape(FF, 128), oq, oo, od, w_gate, w_up, w_qkv, gain1, gain2
    )
    return (mixed, grad_tokens, grad_gain1[:, 0], g_qkv, g_out, grad_gain2[:, 0], g_gate, g_up, g_down)


def solution(mesh):
    row = P("fsdp", None)
    tok = P(("fsdp", "ctx"), None)
    vec = P("fsdp")
    return jax.shard_map(
        shards,
        mesh=mesh,
        in_specs=(tok, tok, row, vec, row, row, vec, row, row, row),
        out_specs=(tok, tok, vec, row, row, vec, row, row, row),
        check_vma=False,
    )
```

```python
import functools

import jax
import jax.numpy as jnp
import numpy as np
from jax import lax
from jax.experimental import pallas as pl
from jax.experimental.pallas import tpu as pltpu
from jax.sharding import PartitionSpec as P

D = 2048
FF = 5632
H = 32
KVH = 4
HD = 64
FJ = FF // 8
bf16 = jnp.bfloat16
f32 = jnp.float32
MESH = pl.DeviceIdType.MESH
epsilon = 1e-05
masked_score = -1e30
ANY = pl.BlockSpec(memory_space=pl.ANY)
VM = pl.BlockSpec(memory_space=pltpu.VMEM)


class Place:
    def __init__(self):
        fs = lax.axis_index("fsdp")
        ct = lax.axis_index("ctx")
        self.zh, self.x, self.k = fs // 8, (fs // 2) % 4, fs % 2
        self.y, self.zl = ct // 2, ct % 2
        self.z = 2 * self.zh + self.zl
        self.at = {a: [getattr(self, a)] + [(getattr(self, a) + r) % 4 for r in (1, 2, 3)] for a in ("x", "y", "z")}
        self.next = {(a, r): self.device(**{a: self.at[a][r % 4]}) for a in ("x", "y", "z") for r in (1, -1)}
        self.other = self.device(k=1 - self.k)
        self.pieces = [[self.piece_of(z, x) for x in self.at["x"]] for z in self.at["z"]]

    def device(self, z=None, x=None, k=None, y=None):
        z = self.z if z is None else z
        x = self.x if x is None else x
        k = self.k if k is None else k
        y = self.y if y is None else y
        return ((z // 2) * 8 + x * 2 + k, y * 2 + z % 2)

    def sibling(self):
        return self.other

    def along(self, axis, r):
        return self.next[axis, r]

    def piece_of(self, z, x):
        return (z // 2) * 8 + x * 2 + z % 2

    def piece(self, **r):
        return self.pieces[r.get("z", 0) % 4][r.get("x", 0) % 4]

    def moved(self, axis, r):
        return self.at[axis][r % 4]


def rcopy(src, dst, ssem, rsem, dev):
    return pltpu.make_async_remote_copy(
        src_ref=src, dst_ref=dst, send_sem=ssem, recv_sem=rsem, device_id=dev, device_id_type=MESH
    )


def greet(devices):
    bar = pltpu.get_barrier_semaphore()
    for dev in devices:
        pl.semaphore_signal(bar, inc=1, device_id=dev, device_id_type=MESH)


def await_greetings(count):
    pl.semaphore_wait(pltpu.get_barrier_semaphore(), count)


class RingGather:
    messages = 12

    def __init__(self, at, own, buf, ssem, rsem, lsem):
        self.at, self.own, self.buf, self.ssem, self.rsem = at, own, buf, ssem, rsem
        self.keep = pltpu.make_async_copy(own, buf.at[at.k * 4 + at.y], lsem)

    def half(self, r, h, k=None):
        k = self.at.k if k is None else k
        return self.buf.at[k * 4 + self.at.moved("y", r), pl.ds(64 * h, 64)]

    def copy(self, d, m, incoming):
        step = 1 - 2 * d
        h = d if m in (0, 2) else 1 - d
        back = (-step if m == 2 else 0) - (step if incoming else 0)
        ref = self.half(back, h)
        i = d * 3 + m
        src = ref if incoming or m == 2 else self.own.at[pl.ds(64 * h, 64)]
        return rcopy(src, ref, self.ssem.at[i], self.rsem.at[i], self.at.along("y", step))

    def relay(self, i, incoming):
        k = 1 - self.at.k if incoming else self.at.k
        if i < 6:
            d, m = i // 3, i % 3
            step = 1 - 2 * d
            h = d if m in (0, 2) else 1 - d
            ref = self.half((-2 if m == 2 else -1) * step, h, k)
        else:
            ref = self.half(0, i - 6, k)
        src = ref if incoming or i < 6 else self.own.at[pl.ds(64 * (i - 6), 64)]
        return rcopy(src, ref, self.ssem.at[6 + i], self.rsem.at[6 + i], self.at.sibling())

    def start(self):
        for m in (0, 1):
            for d in (0, 1):
                self.copy(d, m, False).start()
        for i in (6, 7):
            self.relay(i, False).start()
        self.keep.start()

    def step(self, m):
        for d in (0, 1):
            self.copy(d, m, True).wait_recv()
            if m == 0:
                self.copy(d, 2, False).start()
            self.relay(d * 3 + m, False).start()

    def finish(self):
        self.keep.wait()
        for i in range(8):
            self.relay(i, True).wait_recv()
            self.relay(i, False).wait_send()
        for d in (0, 1):
            for m in range(3):
                self.copy(d, m, False).wait_send()


RING_SEMS = 14


class RingReduce:
    def __init__(self, at, part, sib, recv, ssem, rsem):
        self.at, self.part, self.sib, self.recv = at, part, sib, recv
        self.ssem, self.rsem = ssem, rsem

    def cross(self, r):
        y = self.at.moved("y", r)
        return rcopy(
            self.part.at[(1 - self.at.k) * 4 + y], self.sib.at[r], self.ssem.at[6 + r], self.rsem.at[6 + r], self.at.sibling()
        )

    def copy(self, d, m):
        step = 1 - 2 * d
        h = d if m in (0, 2) else 1 - d
        y = self.at.moved("y", 2 if m == 0 else step)
        i = d * 3 + m
        return rcopy(
            self.part.at[self.at.k * 4 + y, pl.ds(64 * h, 64)], self.recv.at[i], self.ssem.at[i], self.rsem.at[i], self.at.along("y", step)
        )

    def cross_all(self):
        for r in (2, 1, 3, 0):
            self.cross(r).start()

    def add(self, r, h, others):
        y = self.at.moved("y", r)

        @pl.loop(0, 4)
        def _(i):
            rows = pl.ds(pl.multiple_of(64 * h + i * 16, 16), 16)
            total = self.part[self.at.k * 4 + y, rows, :].astype(f32) + self.sib[r, rows, :].astype(f32)
            for o in others:
                total += self.recv[o, pl.ds(pl.multiple_of(i * 16, 16), 16), :].astype(f32)
            self.part[self.at.k * 4 + y, rows, :] = total.astype(bf16)

    def first(self):
        self.cross(2).wait_recv()
        for d in (0, 1):
            self.add(2, d, ())
            self.copy(d, 0).start()
        for d in (0, 1):
            r = 1 if d == 0 else 3
            self.cross(r).wait_recv()
            self.add(r, 1 - d, ())
            self.copy(d, 1).start()

    def second(self):
        for d in (0, 1):
            self.copy(d, 0).wait_recv()
            self.add(1 if d == 0 else 3, d, (d * 3,))
            self.copy(d, 2).start()

    def collect(self, emit):
        self.cross(0).wait_recv()
        for d in (0, 1):
            for m in (1, 2):
                self.copy(d, m).wait_recv()
        for h in range(2):
            left, right = (2, 4) if h == 0 else (1, 5)

            @pl.loop(0, 4)
            def _(i):
                rows = pl.ds(pl.multiple_of(64 * h + i * 16, 16), 16)
                here = pl.ds(pl.multiple_of(i * 16, 16), 16)
                total = self.part[self.at.k * 4 + self.at.y, rows, :].astype(f32) + self.sib[0, rows, :].astype(f32)
                total += self.recv[left, here, :].astype(f32) + self.recv[right, here, :].astype(f32)
                emit(rows, total)

    def finish(self):
        for r in range(4):
            self.cross(r).wait_send()
        for d in (0, 1):
            for m in range(3):
                self.copy(d, m).wait_send()


REDUCE_SEMS = 10


class PlaneReduce:
    def __init__(self, at, part, recv, first, second, ssem, rsem, base=0):
        self.at, self.part, self.recv, self.base = at, part, recv, base
        self.first, self.second, self.ssem, self.rsem = first, second, ssem, rsem
        self.rows = recv.shape[1]

    def piece(self, a, c):
        return self.at.piece(**{self.first: a, self.second: c})

    def half(self, h):
        return pl.ds(self.base + h * self.rows, self.rows)

    def copy(self, c, d, m):
        step = 1 - 2 * d
        h = d if m in (0, 2) else 1 - d
        r = 2 if m == 0 else step
        p = self.piece(r, c) if c < 4 else self.piece(0, r)
        i = c * 6 + d * 3 + m
        return rcopy(
            self.part.at[p, self.half(h)], self.recv.at[i], self.ssem.at[i], self.rsem.at[i],
            self.at.along(self.first if c < 4 else self.second, step),
        )

    def add(self, p, h, others):
        @pl.loop(0, self.rows // 32)
        def _(i):
            rows = pl.ds(pl.multiple_of(self.base + h * self.rows + i * 32, 32), 32)
            here = pl.ds(pl.multiple_of(i * 32, 32), 32)
            total = self.part[p, rows, :].astype(f32)
            for o in others:
                total += self.recv[o, here, :].astype(f32)
            self.part[p, rows, :] = total.astype(bf16)

    def start(self, c):
        for m in (0, 1):
            for d in (0, 1):
                self.copy(c, d, m).start()

    def middle(self, c):
        for d in (0, 1):
            self.copy(c, d, 0).wait_recv()
            r = 1 - 2 * d
            p = self.piece(r, c) if c < 4 else self.piece(0, r)
            self.add(p, d, (c * 6 + d * 3,))
            self.copy(c, d, 2).start()

    def end(self, c):
        for d in (0, 1):
            for m in (1, 2):
                self.copy(c, d, m).wait_recv()
        p = self.piece(0, c) if c < 4 else self.piece(0, 0)
        self.add(p, 0, (c * 6 + 2, c * 6 + 4))
        self.add(p, 1, (c * 6 + 1, c * 6 + 5))

    def start_all(self):
        for c in (2, 1, 3, 0):
            self.start(c)

    def middle_all(self):
        for c in (2, 1, 3, 0):
            self.middle(c)

    def end_all(self):
        for c in (2, 1, 3, 0):
            self.end(c)
        self.start(4)

    def last(self):
        self.middle(4)
        self.end(4)

    def finish(self):
        for c in range(5):
            for d in (0, 1):
                for m in range(3):
                    self.copy(c, d, m).wait_send()


PLANE_SEMS = 30


class PlaneGather:
    def __init__(self, at, view, first, second, ssem, rsem):
        self.at, self.view, self.first, self.second = at, view, first, second
        self.ssem, self.rsem = ssem, rsem

    def copy(self, c, d, m, incoming):
        step = 1 - 2 * d
        h = d if m in (0, 2) else 1 - d
        back = (-step if m == 2 else 0) - (step if incoming else 0)
        a, b = (back, 0) if c == 4 else (c, back)
        p = self.at.piece(**{self.first: a, self.second: b})
        ref = self.view(p, h)
        i = c * 6 + d * 3 + m
        axis = self.first if c == 4 else self.second
        return rcopy(ref, ref, self.ssem.at[i], self.rsem.at[i], self.at.along(axis, step))

    def start(self, c):
        for m in (0, 1):
            for d in (0, 1):
                self.copy(c, d, m, False).start()

    def middle(self, c):
        for d in (0, 1):
            self.copy(c, d, 0, True).wait_recv()
            self.copy(c, d, 2, False).start()

    def arrive(self, c, m):
        for d in (0, 1):
            self.copy(c, d, m, True).wait_recv()

    def step0(self):
        self.start(4)
        self.start(0)

    def step1(self):
        self.middle(4)
        self.arrive(4, 1)
        self.start(3)
        self.start(1)

    def step2(self):
        self.middle(0)
        self.arrive(4, 2)
        self.start(2)

    def step3(self):
        for c in (3, 1, 2):
            self.middle(c)

    def step4(self):
        for c in range(4):
            self.arrive(c, 1)
            self.arrive(c, 2)
        for c in range(5):
            for d in (0, 1):
                for m in range(3):
                    self.copy(c, d, m, False).wait_send()


def dot_nt(a, b):
    return lax.dot_general(a, b, (((1,), (1,)), ((), ())), preferred_element_type=f32)


def dot_nn(a, b):
    return lax.dot_general(a, b, (((1,), (0,)), ((), ())), preferred_element_type=f32)


def dot_tn(a, b):
    return lax.dot_general(a, b, (((0,), (0,)), ((), ())), preferred_element_type=f32)


Q0, O0, G0, U0, D0, ROWS = 0, 384, 640, 1344, 2048, 2752
SCALE = HD**-0.5


def rotate(u, cosine, sine, sign):
    a, b = u[:32], u[32:]
    s = sine * sign
    return jnp.concatenate([a * cosine - b * s, b * cosine + a * s], axis=0)


def mask_bias(bounds, n):
    key = lax.broadcasted_iota(jnp.int32, (n, 128), 0)
    own, trunk, start, b0, b1 = [bounds[i : i + 1, :] for i in range(5)]
    keep = (key <= own) & ((key < trunk) | (key >= start) | ((key >= b0) & (key < b1)))
    return jnp.where(keep, 0.0, masked_score)


def heads_side_by_side(ref, t, y):
    return jnp.concatenate([ref[t, 64 * h : 64 * h + 64, 128 * y : 128 * y + 128] for h in range(4)], axis=1)


def tree_keys(kvb, kvt, kvn, t):
    for y in range(4):
        for z in range(2):
            b = 2 * y + z
            blk = kvb[t, y, z]
            kvt[:, 128 * b : 128 * b + 128] = blk
            kvn[128 * b : 128 * b + 128, :] = blk.astype(f32).T.astype(bf16)


def forward_kernel(
    hat, x, cot, wcol, wo, wd, cosine, sine, bounds,
    hat_out, cot_all, w_all, q_out, kvb, att, lse, hidden, hat2_all,
    hat_all, wqo, part, sib, recv, kvt, kvn, own2,
    hsem_s, hsem_r, csem_s, csem_r, gsem_s, gsem_r, psem_s, psem_r, rsem_s, rsem_r,
    colsem_s, colsem_r, rowsem_s, rowsem_r, kvsem_s, kvsem_r, lsem,
):
    at = Place()
    k, y, zl = at.k, at.y, at.zl
    own8 = at.zh * 4 + at.x
    is_src = own8 // 2 == y
    kd = at.x % 2
    both = jnp.where(is_src & (kd == k), 1, 0)
    src_n = jnp.where(is_src, 1, 0)
    j = 2 * y + k
    jz, jx = (j // 4) * 2 + zl, j % 4
    zpeer = at.device(z=at.z + 1 - 2 * zl)

    piece = at.piece()
    lanes = pl.ds(pl.multiple_of(piece * 128, 128), 128)
    greet([at.sibling()] + [at.along(a, r) for a in ("x", "z", "y") for r in (1, -1)])
    for s in range(2):
        mine = (jz == at.z) & (jx == at.x) & (k == s)

        @pl.when(jnp.logical_not(mine))
        def _():
            greet([at.device(z=jz, x=jx, k=s)])

    def row_dest(t):
        q = (own8 + t) % 8
        z = (q // 4) * 2 + zl
        return at.device(z=z, x=q % 4, k=kd), at.piece_of(z, q % 4)

    @pl.when(is_src)
    def _():
        for t in range(8):
            dev, _ = row_dest(t)
            if t == 0:

                @pl.when(kd != k)
                def _():
                    greet([dev])
            else:
                greet([dev])

    await_greetings(7 + (2 - both) + src_n * 8 - both * src_n)

    ring_h = RingGather(at, hat, hat_all, hsem_s, hsem_r, lsem.at[0])
    ring_c = RingGather(at, cot, cot_all, csem_s, csem_r, lsem.at[1])
    ring_2 = RingGather(at, own2, hat2_all, gsem_s, gsem_r, lsem.at[3])
    red = RingReduce(at, part, sib, recv, rsem_s, rsem_r)

    cols = ((0, 384, wqo, Q0), (384, 1408, w_all, G0))
    rows = ((wo, wqo, O0, 128), (wd, w_all, D0, 352))

    def col_send(i):
        s0, n, dst, d0 = cols[i]
        return rcopy(
            wcol.at[1 - k, pl.ds(s0, n)], dst.at[pl.ds(d0, n), lanes], colsem_s.at[i], colsem_r.at[i], at.sibling()
        )

    def col_keep(i):
        s0, n, dst, d0 = cols[i]
        return pltpu.make_async_copy(wcol.at[k, pl.ds(s0, n)], dst.at[pl.ds(d0, n), lanes], colsem_r.at[i])

    def row_send(i, t):
        src, dst, d0, n = rows[i]
        dev, p = row_dest(t)
        there = pl.ds(pl.multiple_of(p * 128, 128), 128)
        return rcopy(
            src.at[:, there], dst.at[pl.ds(pl.multiple_of(d0 + k * n, 16), n), there],
            rowsem_s.at[i, t], rowsem_r.at[i, k], dev,
        )

    def row_keep(i):
        src, dst, d0, n = rows[i]
        return pltpu.make_async_copy(
            src.at[:, lanes], dst.at[pl.ds(pl.multiple_of(d0 + k * n, 16), n), lanes], rowsem_r.at[i, k]
        )

    def row_in(i, s):
        src, dst, d0, n = rows[i]
        there = dst.at[pl.ds(d0 + s * n, n), lanes]
        return rcopy(there, there, rowsem_s.at[i, s], rowsem_r.at[i, s], at.device(z=jz, x=jx, k=s))

    @pl.when(k == zl)
    def _():
        for i in range(2):
            col_send(i).start()
            col_keep(i).start()

    ring_h.start()

    @pl.when(is_src)
    def _():
        for i in range(2):
            for t in range(1, 8):
                row_send(i, t).start()

            @pl.when(kd == k)
            def _():
                row_keep(i).start()

            @pl.when(kd != k)
            def _():
                row_send(i, 0).start()

    def view(ref, r0, n):
        return lambda p, h: ref.at[pl.ds(r0 + h * (n // 2), n // 2), pl.ds(pl.multiple_of(p * 128, 128), 128)]

    planes = [
        PlaneGather(at, view(ref, r0, n), *order, psem_s.at[i], psem_r.at[i])
        for i, (ref, r0, n, order) in enumerate(
            (
                (wqo, Q0, 192, ("x", "z")),
                (wqo, Q0 + 192, 192, ("z", "x")),
                (wqo, O0, 256, ("z", "x")),
                (w_all, G0, 704, ("x", "z")),
                (w_all, U0, 704, ("z", "x")),
                (w_all, D0, 352, ("x", "z")),
                (w_all, D0 + 352, 352, ("z", "x")),
            )
        )
    ]
    pq, po, bulk = planes[:2], planes[2], planes[3:]
    col_keep(0).wait()
    for p in pq:
        p.step0()
    for s in range(2):
        row_in(0, s).wait_recv()
    po.step0()
    ring_h.step(0)
    for p in pq:
        p.step1()
    po.step1()
    ring_h.step(1)
    for p in pq:
        p.step2()
    po.step2()
    for p in pq:
        p.step3()
    po.step3()
    col_keep(1).wait()
    for p in bulk[:2]:
        p.step0()
    for s in range(2):
        row_in(1, s).wait_recv()
    for p in bulk[2:]:
        p.step0()
    ring_h.step(2)
    ring_h.finish()
    ring_c.start()
    for p in pq:
        p.step4()

    def project(t, c):
        h = hat_all[pl.ds(4 * t + 2 * c, 2)].reshape(256, D)
        proj = dot_nt(wqo[Q0 : Q0 + 384, :], h)
        col = pl.ds(pl.multiple_of(256 * c, 256), 256)
        co, si = cosine[t, :, col], sine[t, :, col]
        for head in range(4):
            u = rotate(proj[64 * head : 64 * head + 64], co, si, 1.0)
            q_out[t, 64 * head : 64 * head + 64, col] = (u * SCALE).astype(bf16)
        kv = jnp.concatenate([rotate(proj[256:320], co, si, 1.0), proj[320:]], axis=0).astype(bf16)
        for b in range(2):
            kvb[t, 2 * c + b, zl] = kv[:, 128 * b : 128 * b + 128]

    def kv_send():
        ref = kvb.at[k, :, zl]
        return rcopy(ref, ref, kvsem_s.at[0], kvsem_r.at[0], zpeer)

    def kv_in():
        ref = kvb.at[k, :, 1 - zl]
        return rcopy(ref, ref, kvsem_s.at[0], kvsem_r.at[0], zpeer)

    def kv_relay(kk):
        ref = kvb.at[kk, :, 1 - zl]
        return rcopy(ref, ref, kvsem_s.at[1], kvsem_r.at[1], at.sibling())

    pl.loop(0, 2)(functools.partial(project, k))
    kv_send().start()
    pl.loop(0, 2)(functools.partial(project, 1 - k))
    h_out = pltpu.make_async_copy(hat_all, hat_out, lsem.at[0])
    h_out.start()
    ring_c.step(0)
    kv_in().wait_recv()
    kv_relay(k).start()
    for p in bulk:
        p.step1()
    po.step4()
    w_out_copy = pltpu.make_async_copy(wqo, w_all.at[pl.ds(0, G0)], lsem.at[2])
    w_out_copy.start()
    kv_relay(1 - k).wait_recv()

    def attend(t):
        tree_keys(kvb, kvt, kvn, t)
        for b in range(4):
            n = 256 * (b + 1)
            col = slice(128 * b, 128 * b + 128)
            qs = heads_side_by_side(q_out, t, b)
            qs = jnp.concatenate([qs, jnp.zeros_like(qs)], axis=0)
            bias = mask_bias(bounds[t, :, col], n)
            s = dot_nn(kvn[:n, :], qs) + jnp.concatenate([bias] * 4, axis=1)
            peak = jnp.max(s, axis=0, keepdims=True)
            e = jnp.exp(s - peak)
            total = jnp.sum(e, axis=0, keepdims=True)
            o = dot_nn(kvt[64:128, :n], e.astype(bf16)) / total
            log_total = peak + jnp.log(total)
            for head in range(4):
                c = slice(128 * head, 128 * head + 128)
                att[t, 64 * head : 64 * head + 64, col] = o[:, c].astype(bf16)
                lse[t, head : head + 1, col] = log_total[:, c]

        @pl.loop(0, 2)
        def _(i):
            a = att[t, :, pl.ds(pl.multiple_of(256 * i, 256), 256)]
            r = dot_tn(a, wqo[O0 : O0 + 256, :]).astype(bf16)
            part[pl.ds(4 * t + 2 * i, 2)] = r.reshape(2, 128, D)

    attend(1 - k)
    red.cross_all()
    ring_c.step(1)
    attend(k)
    red.first()
    for p in bulk:
        p.step2()
    ring_c.step(2)
    red.second()
    for p in bulk:
        p.step3()

    def emit(rows, total):
        h = x[rows, :].astype(f32) + total
        hidden[rows, :] = h
        inv = lax.rsqrt(jnp.mean(h * h, axis=1, keepdims=True) + epsilon)
        own2[rows, :] = (h * inv).astype(bf16)

    red.collect(emit)
    ring_2.start()
    ring_c.finish()
    ring_2.step(0)
    ring_2.step(1)
    for p in bulk[:2]:
        p.step4()
    ring_2.step(2)
    for p in bulk[2:]:
        p.step4()
    ring_2.finish()
    red.finish()
    h_out.wait()
    w_out_copy.wait()
    kv_send().wait_send()
    kv_relay(k).wait_send()

    @pl.when(k == zl)
    def _():
        for i in range(2):
            col_send(i).wait_send()

    @pl.when(is_src)
    def _():
        for i in range(2):
            for t in range(1, 8):
                row_send(i, t).wait_send()

            @pl.when(kd != k)
            def _():
                row_send(i, 0).wait_send()


def forward_pass(hat, x, cot, wcol, wo, wd, cosine, sine, bounds):
    shape = jax.ShapeDtypeStruct
    dma = pltpu.SemaphoreType.DMA
    return pl.pallas_call(
        forward_kernel,
        name="forward_pass",
        out_shape=(
            shape((8, 128, D), bf16),
            shape((8, 128, D), bf16),
            shape((ROWS, D), bf16),
            shape((2, 256, 512), bf16),
            shape((2, 4, 2, 128, 128), bf16),
            shape((2, 256, 512), bf16),
            shape((2, 8, 512), f32),
            shape((128, D), f32),
            shape((8, 128, D), bf16),
        ),
        in_specs=[VM] * 9,
        out_specs=[ANY, ANY, ANY, VM, VM, VM, VM, VM, ANY],
        scratch_shapes=[
            pltpu.VMEM((8, 128, D), bf16),
            pltpu.VMEM((G0, D), bf16),
            pltpu.VMEM((8, 128, D), bf16),
            pltpu.VMEM((4, 128, D), bf16),
            pltpu.VMEM((6, 64, D), bf16),
            pltpu.VMEM((128, 1024), bf16),
            pltpu.VMEM((1024, 128), bf16),
            pltpu.VMEM((128, D), bf16),
        ]
        + [dma((RING_SEMS,))] * 6
        + [dma((7, PLANE_SEMS))] * 2
        + [dma((REDUCE_SEMS,))] * 2
        + [dma((2,)), dma((2,)), dma((2, 8)), dma((2, 2)), dma((2,)), dma((2,)), dma((4,))],
        compiler_params=pltpu.CompilerParams(
            collective_id=0, has_side_effects=True, vmem_limit_bytes=56 * 2**20
        ),
    )(hat, x, cot, wcol, wo, wd, cosine, sine, bounds)


def mlp_kernel(
    hat2_hbm, cot_hbm, w_hbm, hidden, cot,
    mixed, ghidden, gb_all, up_part, sum_g, sum_d,
    hat2, cotv, wgu, wdn, part, sib, recv, innert, dgu, pd, pg, pu, precv_d, precv_g, own_gb, mpart, msib, mrecv,
    rsem_s, rsem_r, msem_s, msem_r, gsem_s, gsem_r, psem_s, psem_r, lsem,
):
    at = Place()
    k, y = at.k, at.y
    loads = [
        pltpu.make_async_copy(src, dst, lsem.at[i])
        for i, (src, dst) in enumerate(
            (
                (w_hbm.at[pl.ds(G0, 1408)], wgu),
                (hat2_hbm, hat2),
                (w_hbm.at[pl.ds(D0, 704)], wdn),
                (cot_hbm, cotv),
            )
        )
    ]
    for c in loads:
        c.start()
    greet([at.sibling()] + [at.along(a, r) for a in ("x", "z", "y") for r in (1, -1)])
    await_greetings(7)
    red = RingReduce(at, part, sib, recv, rsem_s, rsem_r)
    redm = RingReduce(at, mpart, msib, mrecv, msem_s, msem_r)
    ring = RingGather(at, own_gb, gb_all, gsem_s, gsem_r, lsem.at[0])
    pr_d = PlaneReduce(at, pd, precv_d, "x", "z", psem_s.at[0], psem_r.at[0])
    pr_g = PlaneReduce(at, pg, precv_g, "z", "x", psem_s.at[1], psem_r.at[1])
    def columns(t, i):
        slot = 4 * t + 2 * i
        return slot, pl.ds(pl.multiple_of(slot * 128, 256), 256)

    loads[0].wait()
    loads[1].wait()

    @pl.loop(0, 4)
    def _(i):
        slot, cols = columns(0, i)
        both = dot_nt(wgu[...], hat2[pl.ds(slot, 2)].reshape(256, D))
        gate, up = both[:FJ], both[FJ:]
        sig = jax.nn.sigmoid(gate)
        silu = gate * sig
        innert[:, cols] = (silu * up).astype(bf16)
        dgu[:FJ, cols] = (up * sig * (1.0 + gate * (1.0 - sig))).astype(bf16)
        dgu[FJ:, cols] = silu.astype(bf16)

    loads[2].wait()

    def mix(t):
        @pl.loop(0, 2)
        def _(i):
            slot, cols = columns(t, i)
            r = dot_tn(innert[:, cols], wdn[...]).astype(bf16)
            mpart[pl.ds(slot, 2)] = r.reshape(2, 128, D)

    def mlp_back(t):
        @pl.loop(0, 2)
        def _(i):
            slot, cols = columns(t, i)
            gi = dot_nt(wdn[...], cotv[pl.ds(slot, 2)].reshape(256, D))
            dgu[:FJ, cols] = (gi * dgu[:FJ, cols].astype(f32)).astype(bf16)
            dgu[FJ:, cols] = (gi * dgu[FJ:, cols].astype(f32)).astype(bf16)

        @pl.loop(0, 2)
        def _(i):
            slot, cols = columns(t, i)
            r = dot_tn(dgu[:, cols], wgu[...]).astype(bf16)
            part[pl.ds(slot, 2)] = r.reshape(2, 128, D)

    def weight_grad(left, right, out):
        @pl.loop(0, 4)
        def _(i):
            cols = pl.ds(pl.multiple_of(512 * i, 512), 512)
            g = dot_nn(left[...], right[:, :, cols].reshape(1024, 512)).astype(bf16)
            for q in range(4):
                out[4 * i + q] = g[:, 128 * q : 128 * q + 128]

    loads[3].wait()
    mix(1 - k)
    redm.cross_all()
    mix(k)
    redm.first()
    mlp_back(1 - k)
    red.cross_all()
    redm.second()
    mlp_back(k)
    red.first()
    weight_grad(innert, cotv, pd)
    pr_d.start_all()
    red.second()

    def emit_mixed(rows, total):
        mixed[rows, :] = (hidden[rows, :] + total).astype(bf16)

    redm.collect(emit_mixed)
    weight_grad(dgu.at[:FJ], hat2, pg)
    pr_g.start_all()
    pr_d.middle_all()

    def emit(rows, total):
        h = hidden[rows, :]
        inv = lax.rsqrt(jnp.mean(h * h, axis=1, keepdims=True) + epsilon)
        hat = h * inv
        g = cot[rows, :].astype(f32) + inv * (total - hat * jnp.mean(total * hat, axis=1, keepdims=True))
        ghidden[rows, :] = g
        own_gb[rows, :] = g.astype(bf16)

    red.collect(emit)
    ring.start()
    pr_g.middle_all()

    ring.step(0)
    weight_grad(dgu.at[FJ:], hat2, pu)
    u_out = pltpu.make_async_copy(pu, up_part, lsem.at[4])
    u_out.start()
    ring.step(1)
    pr_d.end_all()
    pr_g.end_all()
    red.finish()
    ring.step(2)

    pr_d.last()
    d_out = pltpu.make_async_copy(pd.at[at.piece()], sum_d, lsem.at[2])
    d_out.start()
    pr_g.last()
    g_out = pltpu.make_async_copy(pg.at[at.piece()], sum_g, lsem.at[3])
    g_out.start()
    ring.finish()
    pr_d.finish()
    pr_g.finish()
    redm.finish()
    u_out.wait()
    d_out.wait()
    g_out.wait()


def mlp_pass(hat2_all, cot_all, w_all, hidden, cot):
    shape = jax.ShapeDtypeStruct
    dma = pltpu.SemaphoreType.DMA
    block = pltpu.VMEM((8, 128, D), bf16)
    return pl.pallas_call(
        mlp_kernel,
        name="mlp_pass",
        out_shape=(
            shape((128, D), bf16),
            shape((128, D), f32),
            shape((8, 128, D), bf16),
            shape((16, FJ, 128), bf16),
            shape((FJ, 128), bf16),
            shape((FJ, 128), bf16),
        ),
        in_specs=[ANY, ANY, ANY, VM, VM],
        out_specs=[VM, VM, ANY, ANY, ANY, ANY],
        scratch_shapes=[
            block, block,
            pltpu.VMEM((2 * FJ, D), bf16), pltpu.VMEM((FJ, D), bf16),
            block,
            pltpu.VMEM((4, 128, D), bf16),
            pltpu.VMEM((6, 64, D), bf16),
            pltpu.VMEM((FJ, 1024), bf16), pltpu.VMEM((2 * FJ, 1024), bf16),
            pltpu.VMEM((16, FJ, 128), bf16), pltpu.VMEM((16, FJ, 128), bf16), pltpu.VMEM((16, FJ, 128), bf16),
            pltpu.VMEM((30, FJ // 2, 128), bf16), pltpu.VMEM((30, FJ // 2, 128), bf16),
            pltpu.VMEM((128, D), bf16),
            block, pltpu.VMEM((4, 128, D), bf16), pltpu.VMEM((6, 64, D), bf16),
            dma((REDUCE_SEMS,)), dma((REDUCE_SEMS,)), dma((REDUCE_SEMS,)), dma((REDUCE_SEMS,)), dma((RING_SEMS,)), dma((RING_SEMS,)),
            dma((2, PLANE_SEMS)), dma((2, PLANE_SEMS)), dma((5,)),
        ],
        compiler_params=pltpu.CompilerParams(
            collective_id=1, has_side_effects=True, vmem_limit_bytes=62 * 2**20
        ),
    )(hat2_all, cot_all, w_all, hidden, cot)


class ColSpread:
    def __init__(self, at, src, dst, ssem, rsem):
        self.at, self.src, self.dst, self.ssem, self.rsem = at, src, dst, ssem, rsem
        self.home = at.k == at.zl
        self.there = dst.at[2 * at.y + at.k]

    def near(self):
        return rcopy(self.src, self.there, self.ssem.at[6], self.rsem.at[6 + self.at.k], self.at.sibling())

    def far(self):
        at = self.at
        dev = at.device(z=at.z + 1 - 2 * at.zl, k=at.zl)
        return rcopy(self.src, self.there, self.ssem.at[7], self.rsem.at[6 + at.k], dev)

    def start(self):
        self.far().start()

        @pl.when(self.home)
        def _():
            pltpu.make_async_copy(self.src, self.there, self.rsem.at[6 + self.at.k]).start()

        @pl.when(jnp.logical_not(self.home))
        def _():
            self.near().start()

    def copy(self, d, m, incoming):
        step = 1 - 2 * d
        h = d if m in (0, 2) else 1 - d
        back = (-step if m == 2 else 0) - (step if incoming else 0)
        ref = self.dst.at[2 * self.at.moved("y", back) + h]
        i = d * 3 + m
        return rcopy(ref, ref, self.ssem.at[i], self.rsem.at[i], self.at.along("y", step))

    def ring(self):
        for h in range(2):
            pltpu.make_async_copy(self.src, self.dst.at[2 * self.at.y + h], self.rsem.at[6 + h]).wait()
        for m in (0, 1):
            for d in (0, 1):
                self.copy(d, m, False).start()

    def middle(self):
        for d in (0, 1):
            self.copy(d, 0, True).wait_recv()
            self.copy(d, 2, False).start()

    def finish(self):
        for d in (0, 1):
            for m in (1, 2):
                self.copy(d, m, True).wait_recv()
        for d in (0, 1):
            for m in range(3):
                self.copy(d, m, False).wait_send()
        self.far().wait_send()

        @pl.when(jnp.logical_not(self.home))
        def _():
            self.near().wait_send()


class RowSpread:
    def __init__(self, at, src, buf, dst, ssem, rsem):
        self.at, self.src, self.buf, self.dst, self.ssem, self.rsem = at, src, buf, dst, ssem, rsem
        self.m = dst.shape[0]
        self.lanes = pl.ds(pl.multiple_of(at.piece() * 128, 128), 128)

    def keep(self, h):
        return pltpu.make_async_copy(self.src.at[pl.ds(h * self.m, self.m)], self.buf.at[self.at.y, h], self.ssem.at[6 + h])

    def start(self):
        for h in range(2):
            self.keep(h).start()
        for m in (0, 1):
            for d in (0, 1):
                self.copy(d, m, False).start()

    def copy(self, d, m, incoming):
        step = 1 - 2 * d
        h = d if m in (0, 2) else 1 - d
        back = (-step if m == 2 else 0) - (step if incoming else 0)
        ref = self.buf.at[self.at.moved("y", back), h]
        i = d * 3 + m
        src = ref if incoming or m == 2 else self.src.at[pl.ds(h * self.m, self.m)]
        return rcopy(src, ref, self.ssem.at[i], self.rsem.at[i], self.at.along("y", step))

    def middle(self):
        for d in (0, 1):
            self.copy(d, 0, True).wait_recv()
            self.copy(d, 2, False).start()

    def each(self, f, g):
        at = self.at
        for y in range(4):
            for dz in (1, 0):
                for c in range(2):
                    if dz:
                        f(y, dz, c)
                    else:
                        mine = (at.zh == y // 2) & (at.x == 2 * (y % 2) + at.k) & (at.k == c)
                        pl.when(mine)(functools.partial(g, y, c))
                        pl.when(jnp.logical_not(mine))(functools.partial(f, y, dz, c))

    def device(self, y, dz, c):
        at = self.at
        return at.device(z=2 * (y // 2) + (at.zl + dz) % 2, x=2 * (y % 2) + at.k, k=c)

    def push_copy(self, y, dz, c):
        return rcopy(
            self.buf.at[y, c], self.dst.at[:, self.lanes], self.ssem.at[8 + (y * 2 + dz) * 2 + c],
            self.rsem.at[6 + self.at.piece()], self.device(y, dz, c),
        )

    def push(self):
        for h in range(2):
            self.keep(h).wait()
        for d in (0, 1):
            for m in (1, 2):
                self.copy(d, m, True).wait_recv()

        def local(y, c):
            pltpu.make_async_copy(
                self.buf.at[y, c], self.dst.at[:, self.lanes], self.rsem.at[6 + self.at.piece()]
            ).start()

        self.each(lambda y, dz, c: self.push_copy(y, dz, c).start(), local)

    def finish(self):
        for p in range(16):
            pltpu.make_async_copy(self.buf.at[0, 0], self.dst.at[:, pl.ds(p * 128, 128)], self.rsem.at[6 + p]).wait()
        for d in (0, 1):
            for m in range(3):
                self.copy(d, m, False).wait_send()
        self.each(lambda y, dz, c: self.push_copy(y, dz, c).wait_send(), lambda y, c: None)

    def greet(self):
        at = self.at
        self.each(lambda y, dz, c: greet([self.device(y, dz, c)]), lambda y, c: None)
        for p in range(16):
            z, x = (p // 8) * 2 + p % 2, (p // 2) % 4
            mine = (at.z == z) & (at.x == x) & (at.k == at.x % 2)

            @pl.when(jnp.logical_not(mine))
            def _():
                greet([at.device(z=z, x=x, k=at.x % 2)])

        return 2 * (16 - jnp.where(at.x % 2 == at.k, 1, 0))


def backward_kernel(
    gb_hbm, hat_hbm, w_hbm, q, kvb, att, lse, cosine, sine, bounds, x, ghidden, up_part, sum_g, sum_d,
    grad_tokens, out_q, out_g, out_u, out_o, out_d,
    gb, hat, wqo, pu, pq, po, precv_u, precv_q, precv_o, part, sib, recv,
    datt, dproj, dkv, dkv_far, dkv_got, kvt, kvn, buf_o, buf_d,
    rsem_s, rsem_r, psem_s, psem_r, xsem_s, xsem_r, csem_s, csem_r, wsem_s, wsem_r, lsem,
):
    at = Place()
    k, y, zl = at.k, at.y, at.zl
    zpeer = at.device(z=at.z + 1 - 2 * zl)
    loads = [
        pltpu.make_async_copy(src, dst, lsem.at[i])
        for i, (src, dst) in enumerate(
            (
                (w_hbm.at[pl.ds(0, G0)], wqo),
                (gb_hbm, gb),
                (up_part, pu),
                (hat_hbm, hat),
            )
        )
    ]
    for c in loads:
        c.start()
    cols_q = ColSpread(at, pq.at[at.piece()], out_q, csem_s.at[0], csem_r.at[0])
    cols_g = ColSpread(at, sum_g, out_g, csem_s.at[1], csem_r.at[1])
    cols_u = ColSpread(at, pu.at[at.piece()], out_u, csem_s.at[2], csem_r.at[2])
    rows_o = RowSpread(at, po.at[at.piece()], buf_o, out_o, wsem_s.at[0], wsem_r.at[0])
    rows_d = RowSpread(at, sum_d, buf_d, out_d, wsem_s.at[1], wsem_r.at[1])
    greet([at.sibling(), at.device(z=at.z + 1 - 2 * zl, k=1 - k)])
    greet([at.along(a, r) for a in ("x", "z", "y") for r in (1, -1)])
    await_greetings(8 + rows_o.greet())

    red = RingReduce(at, part, sib, recv, rsem_s, rsem_r)
    pr_u = PlaneReduce(at, pu, precv_u, "x", "z", psem_s.at[0], psem_r.at[0])
    pr_q = PlaneReduce(at, pq, precv_q, "z", "x", psem_s.at[1], psem_r.at[1])
    pr_o = PlaneReduce(at, po, precv_o, "z", "x", psem_s.at[2], psem_r.at[2])
    cols_g.start()
    rows_d.start()
    loads[2].wait()
    pr_u.start_all()
    loads[0].wait()
    loads[1].wait()

    @pl.loop(0, 4)
    def _(i):
        g = gb[pl.ds(2 * i, 2)].reshape(256, D)
        r = dot_nt(wqo[O0 : O0 + 256, :], g)
        datt[i // 2, :, pl.ds(pl.multiple_of(256 * (i % 2), 256), 256)] = r.astype(bf16)

    cols_g.ring()

    def weight_grad(left, right, ref):
        @pl.loop(0, 4)
        def _(i):
            cols = pl.ds(pl.multiple_of(512 * i, 512), 512)
            g = dot_nn(left[0], right[0:4, :, cols].reshape(512, 512))
            g += dot_nn(left[1], right[4:8, :, cols].reshape(512, 512))
            g = g.astype(bf16)
            for s in range(4):
                ref[4 * i + s] = g[:, 128 * s : 128 * s + 128]

    weight_grad(att, gb, po)
    pr_o.start_all()

    def attend(t):
        tree_keys(kvb, kvt, kvn, t)
        for b in (3, 2, 1, 0):
            n = 256 * (b + 1)
            col = slice(128 * b, 128 * b + 128)
            qs = heads_side_by_side(q, t, b)
            dos = heads_side_by_side(datt, t, b)
            zero = jnp.zeros_like(qs)
            bias = mask_bias(bounds[t, :, col], n)
            log_total = jnp.concatenate([lse[t, h : h + 1, col] for h in range(4)], axis=1)
            s = dot_nn(kvn[:n, :], jnp.concatenate([qs, zero], axis=0)) + jnp.concatenate([bias] * 4, axis=1)
            prob = jnp.exp(s - log_total)
            dprob = dot_nn(kvn[:n, :], jnp.concatenate([zero, dos], axis=0))
            inner = jnp.sum(prob * dprob, axis=0, keepdims=True)
            ds = (prob * (dprob - inner)).astype(bf16)
            dq = dot_nn(kvt[0:64, :n], ds) * SCALE
            co, si = cosine[t, :, col], sine[t, :, col]
            for h in range(4):
                u = rotate(dq[:, 128 * h : 128 * h + 128], co, si, -1.0)
                dproj[t, 64 * h : 64 * h + 64, col] = u.astype(bf16)
            dk = dot_nt(qs, ds)
            dv = dot_nt(dos, prob.astype(bf16))
            for c in range(2 * (b + 1)):
                blk = slice(128 * c, 128 * c + 128)
                if b == 3:
                    dkv[t, c // 2, c % 2, :64, :] = dk[:, blk]
                    dkv[t, c // 2, c % 2, 64:, :] = dv[:, blk]
                else:
                    dkv[t, c // 2, c % 2, :64, :] += dk[:, blk]
                    dkv[t, c // 2, c % 2, 64:, :] += dv[:, blk]
        for b in range(4):
            dkv_far[t, b] = dkv[t, b, 1 - zl].astype(bf16)

    def far_copy(t, s):
        return rcopy(dkv_far.at[t], dkv_got.at[t], xsem_s.at[s], xsem_r.at[s], zpeer)

    def project(t, s):
        far_copy(t, s).wait_recv()
        for b in range(4):
            col = slice(128 * b, 128 * b + 128)
            total = dkv[t, b, zl] + dkv_got[t, b].astype(f32)
            dk = rotate(total[:64], cosine[t, :, col], sine[t, :, col], -1.0)
            dproj[t, 256:320, col] = dk.astype(bf16)
            dproj[t, 320:384, col] = total[64:].astype(bf16)

        @pl.loop(0, 2)
        def _(i):
            a = dproj[t, :, pl.ds(pl.multiple_of(256 * i, 256), 256)]
            r = dot_tn(a, wqo[Q0 : Q0 + 384, :]).astype(bf16)
            part[pl.ds(4 * t + 2 * i, 2)] = r.reshape(2, 128, D)

    attend(1 - k)
    far_copy(1 - k, 0).start()
    rows_d.middle()
    pr_u.middle(2)
    pr_u.middle(1)
    attend(k)
    far_copy(k, 1).start()
    rows_d.push()
    project(1 - k, 0)
    red.cross_all()
    pr_u.middle(3)
    pr_u.middle(0)
    project(k, 1)
    red.first()
    pr_o.middle_all()
    cols_g.middle()
    loads[3].wait()
    weight_grad(dproj, hat, pq)
    pr_q.start_all()
    red.second()
    pr_u.end_all()
    pr_o.end_all()
    pr_q.middle_all()
    pr_u.last()
    cols_u.start()
    pr_o.last()
    rows_o.start()
    cols_u.ring()

    def emit(rows, total):
        h = x[rows, :].astype(f32)
        inv = lax.rsqrt(jnp.mean(h * h, axis=1, keepdims=True) + epsilon)
        hat1 = h * inv
        g = ghidden[rows, :] + inv * (total - hat1 * jnp.mean(total * hat1, axis=1, keepdims=True))
        grad_tokens[rows, :] = g

    pr_q.end_all()
    rows_o.middle()
    red.collect(emit)
    pr_q.last()
    cols_q.start()
    cols_u.middle()
    rows_o.push()
    cols_q.ring()
    cols_g.finish()
    rows_d.finish()
    cols_q.middle()
    cols_u.finish()
    rows_o.finish()
    cols_q.finish()
    for s, t in ((0, 1 - k), (1, k)):
        far_copy(t, s).wait_send()
    red.finish()
    pr_u.finish()
    pr_o.finish()
    pr_q.finish()


def backward_pass(*args):
    shape = jax.ShapeDtypeStruct
    dma = pltpu.SemaphoreType.DMA
    block = pltpu.VMEM((8, 128, D), bf16)
    return pl.pallas_call(
        backward_kernel,
        name="backward_pass",
        out_shape=(
            shape((128, D), f32),
            shape((8, 384, 128), bf16),
            shape((8, FJ, 128), bf16),
            shape((8, FJ, 128), bf16),
            shape((128, D), bf16),
            shape((352, D), bf16),
        ),
        in_specs=[ANY, ANY, ANY, VM, VM, VM, VM, VM, VM, VM, VM, VM, ANY, VM, VM],
        out_specs=[VM] + [ANY] * 5,
        scratch_shapes=[
            block, block, pltpu.VMEM((G0, D), bf16),
            pltpu.VMEM((16, FJ, 128), bf16), pltpu.VMEM((16, 384, 128), bf16), pltpu.VMEM((16, 256, 128), bf16),
            pltpu.VMEM((30, FJ // 2, 128), bf16), pltpu.VMEM((30, 192, 128), bf16), pltpu.VMEM((30, 128, 128), bf16),
            block, pltpu.VMEM((4, 128, D), bf16), pltpu.VMEM((6, 64, D), bf16),
            pltpu.VMEM((2, 256, 512), bf16),
            pltpu.VMEM((2, 384, 512), bf16),
            pltpu.VMEM((2, 4, 2, 128, 128), f32),
            pltpu.VMEM((2, 4, 128, 128), bf16),
            pltpu.VMEM((2, 4, 128, 128), bf16),
            pltpu.VMEM((128, 1024), bf16),
            pltpu.VMEM((1024, 128), bf16),
            pltpu.VMEM((4, 2, 128, 128), bf16),
            pltpu.VMEM((4, 2, 352, 128), bf16),
            dma((REDUCE_SEMS,)), dma((REDUCE_SEMS,)),
            dma((3, PLANE_SEMS)), dma((3, PLANE_SEMS)), dma((2,)), dma((2,)),
            dma((3, 8)), dma((3, 8)), dma((2, 24)), dma((2, 22)), dma((5,)),
        ],
        compiler_params=pltpu.CompilerParams(
            collective_id=2, has_side_effects=True, vmem_limit_bytes=62 * 2**20
        ),
    )(*args)


def finish_kernel(og, ou, oq, oo, od, wg, wu, wq, gain1, gain2, g_gate, g_up, g_qkv, g_out, g_down, o_one, o_two, s_one, s_two):
    i = pl.program_id(0)

    @pl.when(i == 0)
    def _():
        s_one[...] = jnp.zeros_like(s_one)
        s_two[...] = jnp.zeros_like(s_two)

    total = None
    for src, w, dst in ((og, wg, g_gate), (ou, wu, g_up)):
        raw = src[...].astype(f32).T
        dst[...] = raw * gain2[...]
        dot = jnp.sum(raw * w[...].astype(f32), axis=1, keepdims=True)
        total = dot if total is None else total + dot
    s_two[...] += total

    def qkv(raw, start):
        cols = pl.ds(start, 512)
        g_qkv[:, cols] = raw * gain1[...]
        s_one[...] += jnp.sum(raw * wq[:, cols].astype(f32), axis=1, keepdims=True)

    qkv(oq[pl.ds(2 * i, 2), :256, :].reshape(512, 128).astype(f32).T, pl.multiple_of(512 * i, 512))

    @pl.when(i == 3)
    def _():
        pairs = [oq[2 * g, 256:, :].astype(f32) + oq[2 * g + 1, 256:, :].astype(f32) for g in range(KVH)]
        qkv(jnp.concatenate([p[:64] for p in pairs] + [p[64:] for p in pairs], axis=0).T, 2048)

    @pl.when(i == 3)
    def _():
        for src, dst in ((s_one, o_one), (s_two, o_two)):
            dst[...] = jnp.broadcast_to(src[...], (128, 128)).T[:1]

    g_out[...] = oo[...].astype(f32)
    g_down[...] = od[...].astype(f32)


def finish(og, ou, oq, oo, od, wg, wu, wq, gain1, gain2):
    shape = jax.ShapeDtypeStruct
    row = lambda i: (i, 0)
    col = lambda i: (0, i)
    whole = lambda i: (0, 0)
    d_row = lambda i: (jnp.minimum(i, 1), 0)
    return pl.pallas_call(
        finish_kernel,
        name="finish",
        grid=(4,),
        out_shape=(
            shape((128, FF), f32), shape((128, FF), f32), shape((128, 2560), f32), shape((128, D), f32), shape((352, D), f32),
            shape((1, 128), f32), shape((1, 128), f32),
        ),
        in_specs=[
            pl.BlockSpec((1408, 128), row),
            pl.BlockSpec((1408, 128), row),
            pl.BlockSpec((8, 384, 128), lambda i: (0, 0, 0)),
            pl.BlockSpec((32, D), row),
            pl.BlockSpec((176, D), d_row),
            pl.BlockSpec((128, 1408), col),
            pl.BlockSpec((128, 1408), col),
            pl.BlockSpec((128, 2560), whole),
            pl.BlockSpec((128, 1), whole),
            pl.BlockSpec((128, 1), whole),
        ],
        out_specs=(
            pl.BlockSpec((128, 1408), col),
            pl.BlockSpec((128, 1408), col),
            pl.BlockSpec((128, 2560), whole),
            pl.BlockSpec((32, D), row),
            pl.BlockSpec((176, D), d_row),
            pl.BlockSpec((1, 128), whole),
            pl.BlockSpec((1, 128), whole),
        ),
        scratch_shapes=[pltpu.VMEM((128, 1), f32), pltpu.VMEM((128, 1), f32)],
        compiler_params=pltpu.CompilerParams(vmem_limit_bytes=62 * 2**20),
    )(og, ou, oq, oo, od, wg, wu, wq, gain1, gain2)


def segment_bounds(lengths, offsets):
    ends = jnp.cumsum(lengths)
    starts = ends - lengths
    segment = jnp.sum((offsets[:, None] >= ends[None, :]).astype(jnp.int32), axis=1)
    seg_ids = np.arange(13)
    branch_of = jnp.asarray(np.where(seg_ids > 0, 1 + 3 * ((seg_ids - 1) // 3), 0), jnp.int32)
    onehot = segment[:, None] == jnp.asarray(seg_ids, jnp.int32)[None, :]

    def pick(values):
        return jnp.sum(jnp.where(onehot, values[None, :], 0), axis=1)

    table = np.zeros((13, 13), np.int32)
    for s in range(13):
        if s:
            table[s, 1 + 3 * ((s - 1) // 3)] = 1
        else:
            table[s, 0] = 1
    table = jnp.asarray(table)
    b0 = jnp.sum(table * starts[None, :], axis=1)
    b1 = jnp.sum(table * ends[None, :], axis=1)
    is_leaf = jnp.asarray((seg_ids > 0) & ((seg_ids - 1) % 3 > 0), jnp.int32)
    depth = jnp.where(jnp.asarray(seg_ids > 0), lengths[0], 0) + is_leaf * (b1 - b0)
    position = offsets - pick(starts) + pick(depth)
    trunk = jnp.broadcast_to(lengths[0], offsets.shape)
    return jnp.stack([offsets, trunk, pick(starts), pick(b0), pick(b1)], axis=1), position


def shards(tokens, cotangent, tree_lengths, gain_attn, w_qkv, w_out, gain_mlp, w_gate, w_up, w_down):
    at = Place()
    swapped = lax.ppermute(tree_lengths, "fsdp", [(f, f ^ 1) for f in range(16)])
    lengths = jnp.where(at.k == 0, jnp.stack([tree_lengths[0], swapped[0]]), jnp.stack([swapped[0], tree_lengths[0]]))
    offsets = (
        (2 * jnp.arange(4, dtype=jnp.int32)[:, None] + at.zl) * 128 + jnp.arange(128, dtype=jnp.int32)[None, :]
    ).reshape(512)
    b_a, p_a = segment_bounds(lengths[0], offsets)
    b_b, p_b = segment_bounds(lengths[1], offsets)
    bounds = jnp.pad(jnp.stack([b_a.T, b_b.T]), ((0, 0), (0, 3), (0, 0)))
    position = jnp.stack([p_a, p_b]).astype(f32)
    frequency = 10000.0 ** (-2.0 * jnp.arange(32, dtype=f32) / 64)
    angles = position[:, None, :] * frequency[None, :, None]
    cosine, sine = jnp.cos(angles), jnp.sin(angles)

    gain1 = gain_attn.astype(f32)[:, None]
    gain2 = gain_mlp.astype(f32)[:, None]

    def columns(w, start, n, gain):
        return (lax.dynamic_slice_in_dim(w, start, n, axis=1).astype(f32) * gain).astype(bf16).T

    q_cols = columns(w_qkv, at.y * 512, 512, gain1)
    k_cols = columns(w_qkv, 2048 + at.y * 64, 64, gain1)
    v_cols = columns(w_qkv, 2304 + at.y * 64, 64, gain1)
    g_cols = columns(w_gate, at.y * 2 * FJ, 2 * FJ, gain2)
    u_cols = columns(w_up, at.y * 2 * FJ, 2 * FJ, gain2)
    wcol = jnp.stack(
        [
            jnp.concatenate(
                [q_cols[256 * i : 256 * i + 256], k_cols, v_cols, g_cols[FJ * i : FJ * i + FJ], u_cols[FJ * i : FJ * i + FJ]]
            )
            for i in range(2)
        ]
    )

    inputs = tokens.astype(f32)
    inv1 = lax.rsqrt(jnp.mean(inputs * inputs, axis=-1, keepdims=True) + epsilon)
    hat1 = (inputs * inv1).astype(bf16)
    hat_all, cot_all, w_all, q, kvb, att, lse, hidden, hat2_all = forward_pass(
        hat1, tokens, cotangent, wcol, w_out, w_down, cosine, sine, bounds
    )
    mixed, ghidden, gb_all, up_part, sum_g, sum_d = mlp_pass(hat2_all, cot_all, w_all, hidden, cotangent)
    grad_tokens, oq, og, ou, oo, od = backward_pass(
        gb_all, hat_all, w_all, q, kvb, att, lse, cosine, sine, bounds, tokens, ghidden, up_part, sum_g, sum_d
    )
    g_gate, g_up, g_qkv, g_out, g_down, grad_gain1, grad_gain2 = finish(
        og.reshape(FF, 128), ou.reshape(FF, 128), oq, oo, od, w_gate, w_up, w_qkv, gain1, gain2
    )
    return (mixed, grad_tokens, grad_gain1[0], g_qkv, g_out, grad_gain2[0], g_gate, g_up, g_down)


def solution(mesh):
    row = P("fsdp", None)
    tok = P(("fsdp", "ctx"), None)
    vec = P("fsdp")
    return jax.shard_map(
        shards,
        mesh=mesh,
        in_specs=(tok, tok, row, vec, row, row, vec, row, row, row),
        out_specs=(tok, tok, vec, row, row, vec, row, row, row),
        check_vma=False,
    )
```
